32 devices in a mesh: shape: 8 (over z, y), oct: 4 (over x, core).
Axes of the slice: x: 2, y: 2, z: 4, core: 2. Of those that a mesh axis runs over, the one named last changes fastest.
Arguments:
- point_inputs: bfloat16 [131072, 256], P(('shape', 'oct')), may hold values from -6 to 6
- shape_ids: int32 [131072], P(('shape', 'oct')), may hold values from 0 to 15, as said below
- octants: int32 [131072, 1], P(('shape', 'oct')), may hold values from 0 to 3; in each aligned block of 4096 rows (0 to 4095, 4096 to 8191, ...) at most 2048 rows name the same one
- categories: int32 [16], replicated, may hold values from 0 to 4, as said below
- codes: bfloat16 [16, 256], P('shape'), may hold values from -6 to 6
- direction: float32 [512, 512], replicated, may hold values from -0.25 to 0.25
- gain: float32 [512], replicated, may hold values from 0.5 to 1.5
- bias: float32 [512], replicated, may hold values from -3 to 3
- cotangent: bfloat16 [262144, 512], P(('shape', 'oct')), may hold values from -6 to 6
- prev_mean: float32 [5, 256], replicated, may hold values from -5 to 5
- prev_var: float32 [5, 256], replicated, may hold values from 0.5 to 2
- momentum: float32 [5], replicated, may hold values from 0.2 to 0.8
Outputs:
- layer_out: bfloat16 [262144, 512], P(('shape', 'oct'))
- input_grad: bfloat16 [131072, 256], P(('shape', 'oct'))
- code_grad: float32 [16, 256], P('shape')
- direction_grad: float32 [512, 512], replicated
- gain_grad: float32 [512], replicated
- bias_grad: float32 [512], replicated
- running_mean: float32 [5, 256], replicated
- running_var: float32 [5, 256], replicated
The draws below stay inside these ranges and needn't reach their ends.
Inputs may be any that keep to these rules, and one draw needn't show every extreme that they name: `shape_ids`: the points on the devices of index s along shape belong to shapes s * 2 to (s + 1) * 2 - 1, and every shape has points on every device of its index. `octants`: in the rows of one device no octant is named by more than 2048 points. `categories`: every category holds at least one shape.
All inputs are finite; a program needn't handle non-finite values.
Results may differ from the reference program's by a relative error of at most 0.0059.
Values may be sent and summed in bfloat16 or wider, within the bound.
No kernel may reach another device: no remote copies, remote signals or barrier semaphores. Data moves between devices by JAX's collectives and lax.ppermute only.
A program may use at most 128 MiB of HBM per device.

```python
import math
from functools import partial
import jax
import jax.numpy as jnp
import numpy as np
from jax import lax

HID = 253
CODE = 256
OUT = 512
CATS = 5
PTS_DEV = 4096
SHP_DEV = 2
PW = 256
IN = 512
CAP = 2048
SHAPES = 16
POINTS = 131072
BUCKETS = 262144
N_SHAPE = 8
N_OCT = 4


def draw_shape_ids(key, part):
    key = jax.random.fold_in(key, 11)
    first_key, second_key, third_key = jax.random.split(key, 3)
    row_index = jnp.arange(POINTS, dtype=jnp.int32)
    block = row_index // PTS_DEV
    group = block // N_OCT
    favored = jax.random.randint(first_key, (N_SHAPE * N_OCT,), 0, SHP_DEV)[block]
    picker = jax.random.randint(second_key, (POINTS,), 0, 4)
    others = jax.random.randint(third_key, (POINTS,), 0, SHP_DEV)
    local_ids = jnp.where(picker < 3, favored, others)
    within = row_index % PTS_DEV
    local_ids = jnp.where(within < SHP_DEV, within, local_ids)
    return (group * SHP_DEV + local_ids).astype(jnp.int32)


def draw_categories(key, part):
    key = jax.random.fold_in(key, 23)
    first_key, second_key, third_key = jax.random.split(key, 3)
    shuffled = jax.random.permutation(first_key, CATS)
    first_pick = jax.random.randint(second_key, (SHAPES,), 0, CATS)
    second_pick = jax.random.randint(third_key, (SHAPES,), 0, CATS)
    uneven = jnp.minimum(first_pick, second_pick)
    shape_index = jnp.arange(SHAPES, dtype=jnp.int32)
    return jnp.where(shape_index < CATS, shuffled[shape_index % CATS], uneven).astype(jnp.int32)


def levels(key, shape, shards, smallest, top_value):
    def one(axis_at, parts):
        heights = jax.random.uniform(jax.random.fold_in(jax.random.fold_in(key, 6), axis_at), (parts,), jnp.float32, smallest / len(shards), top_value / len(shards))
        return jnp.repeat(jnp.exp(heights), shape[axis_at] // parts).reshape((-1,) + (1,) * (len(shape) - axis_at - 1))

    level = one(*shards[0])
    for cut in shards[1:]:
        level = level * one(*cut)
    return level


def routed_block(own_key, own, number, rows, amount, top, reach, slope):
    order = jax.random.permutation(own_key, amount)
    packed, common = portions_of(amount, rows * top, reach, slope, True), portions_of(amount, rows * top, reach, slope, False)
    places = jnp.arange(amount)

    def named(lengths, offset_by):
        used = int((lengths > 0).sum())
        fixed = max(1, used // 4)
        shifted = fixed + (places - fixed + offset_by * (used - fixed)) % max(1, amount - fixed)
        return jnp.zeros((amount,), jnp.int32).at[order[jnp.where(places < fixed, places, shifted)]].set(jnp.asarray(lengths, jnp.int32))

    lengths = jnp.where(number % 4 == 0, named(packed, number // 4), named(common, number - number // 4 - 1))
    mixed = jax.random.permutation(jax.random.fold_in(own, 3), amount)
    source_of, taker = mixed[0:amount // 2 * 2:2], mixed[1:amount // 2 * 2:2]
    room = jnp.minimum(lengths[source_of] - 1, reach - lengths[taker]) // 2
    room = jnp.where((source_of == order[0]) | (taker == order[0]) | (lengths[taker] == 0), 0, jnp.maximum(room, 0))
    shifted = jax.random.randint(jax.random.fold_in(own, 4), (amount // 2,), 0, 1 << 20) % (room + 1)
    lengths = lengths.at[source_of].add(-shifted).at[taker].add(shifted)
    labels = jnp.searchsorted(jnp.cumsum(lengths), jnp.arange(rows * top), side="right").astype(jnp.int32)
    listing = labels.reshape(top, rows).T
    listing = listing[jax.random.permutation(jax.random.fold_in(own, 1), rows)]
    offset_by = jax.random.randint(jax.random.fold_in(own, 2), (rows, 1), 0, top)
    return jnp.take_along_axis(listing, (jnp.arange(top)[None, :] + offset_by) % top, axis=1)


def portions_of(count, total, most, skew, full):
    portions = [(1 << 20) // math.isqrt(grade ** skew) + 1 for grade in range(1, count + 1)]
    largest = most if full else min(most, max(-(-total // count), total * portions[0] // sum(portions)))
    least = 1 if total - largest >= count - 1 else 0
    counts, rest = [largest] + [least] * (count - 1), total - largest - least * (count - 1)
    while rest > 0:
        movable = [i for i in range(1, count) if counts[i] < largest] or [i for i in range(1, count) if counts[i] < most]
        whole, left = sum([portions[i] for i in movable]), rest
        for i in movable:
            extra = min(most - counts[i], max(1, left * portions[i] // whole), rest)
            counts[i] = counts[i] + extra
            rest = rest - extra
    return np.array(counts)


def centred(own_key, extent, width, most, cuts=(), kind=jnp.bfloat16):
    factor_of = levels(own_key, extent, cuts, -0.22, 0.18) if cuts else 1.0
    result = jax.random.normal(own_key, extent, jnp.float32) * width * factor_of
    return jnp.minimum(jnp.maximum(result, -most), most).astype(kind)


def setup_inputs(seed: int = 0) -> dict:
    seeds = jax.random.split(jax.random.key(seed), 13)
    point_inputs = centred(seeds[0], (POINTS, PW), 1.0, 6.0, ((0, 32),))
    shape_ids = draw_shape_ids(jax.random.fold_in(seeds[12], 71), 0)
    octants_keys = jax.random.split(jax.random.fold_in(seeds[2], 1), POINTS // PTS_DEV)
    octants_turns = jax.random.permutation(jax.random.fold_in(seeds[2], 3), POINTS // PTS_DEV)
    octants = jax.vmap(lambda own, number: routed_block(jax.random.fold_in(seeds[2], 2), own, number, PTS_DEV, N_OCT, 1, CAP, 2))(octants_keys, octants_turns).reshape((POINTS, 1))
    categories = draw_categories(jax.random.fold_in(seeds[12], 71), 0)
    codes = centred(seeds[4], (SHAPES, CODE), 1.0, 6.0, ((0, 8),))
    direction = centred(seeds[5], (IN, OUT), IN ** -0.5, 0.25, (), jnp.float32)
    gain = jnp.clip(1.0 + 0.1 * jax.random.normal(seeds[6], (OUT,), jnp.float32), 0.5, 1.5)
    bias = centred(seeds[7], (OUT,), 0.5, 3.0, (), jnp.float32)
    cotangent = centred(seeds[8], (BUCKETS, OUT), 1.0, 6.0, ((0, 32),))
    prev_mean = centred(seeds[9], (CATS, CODE), 1.0, 5.0, (), jnp.float32)
    prev_var = jnp.clip(jnp.exp(jax.random.uniform(seeds[10], (CATS, CODE), jnp.float32, math.log(0.5), math.log(2.0))), 0.5, 2.0)
    momentum = jnp.clip(jax.random.uniform(seeds[11], (CATS,), jnp.float32, 0.2, 0.8), 0.2, 0.8)
    return dict(point_inputs=point_inputs, shape_ids=shape_ids, octants=octants, categories=categories, codes=codes, direction=direction, gain=gain, bias=bias, cotangent=cotangent, prev_mean=prev_mean, prev_var=prev_var, momentum=momentum)


norm_eps = 1e-06

@jax.custom_vjp
def low(v):
    return lax.optimization_barrier(v.astype(jnp.bfloat16)).astype(jnp.float32)

@jax.custom_vjp
def low_back(v):
    return v

def low_keep(v):
    return (low(v), None)

def low_pass(kept, grad):
    return (grad,)

def back_keep(v):
    return (v, None)

def back_low(kept, grad):
    return (low(grad),)
low.defvjp(low_keep, low_pass)
low_back.defvjp(back_keep, back_low)

def slot_rows(octant_col):
    blocks = octant_col.reshape(N_SHAPE * N_OCT, PTS_DEV)
    onehot = (blocks[:, :, None] == jnp.arange(N_OCT, dtype=jnp.int32)[None, None, :]).astype(jnp.int32)
    before = jnp.cumsum(onehot, axis=1) - onehot
    ranks = lax.optimization_barrier(jnp.sum(before * onehot, axis=2))
    source = jnp.arange(N_SHAPE * N_OCT, dtype=jnp.int32)[:, None]
    group = source // N_OCT
    anchor = source % N_OCT
    target = ((group * N_OCT + blocks) * N_OCT + anchor) * CAP + ranks
    return target.reshape(-1).astype(jnp.int32)

def norm_weights(direction_f, gain_f):
    norms = jnp.sqrt(lax.optimization_barrier(jnp.sum(direction_f * direction_f, axis=0)) + norm_eps)
    return low(direction_f * (gain_f / norms)[None, :])

def skip_layer(shape_rows, weight, bias_f, codes_f, inputs_g):
    points = low_back(inputs_g)
    code_rows = codes_f[shape_rows]
    joined = jnp.concatenate([points[:, :HID], code_rows, points[:, HID:]], axis=1)
    pre_act = low_back(jnp.dot(joined, weight, precision=lax.Precision.HIGHEST) + bias_f[None, :])
    return jax.nn.softplus(pre_act)

def reference(point_inputs, shape_ids, octants, categories, codes, direction, gain, bias, cotangent, prev_mean, prev_var, momentum):
    inputs_f = point_inputs.astype(jnp.float32)
    codes_f = codes.astype(jnp.float32)
    target = slot_rows(octants[:, 0])
    weight_f, norm_back = jax.vjp(norm_weights, direction, gain)
    group_rows = N_OCT * PTS_DEV

    def group_step(carry, pieces):
        inputs_g, ids_g, target_g = pieces
        outputs, pullback = jax.vjp(partial(skip_layer, ids_g), weight_f, bias, codes_f, inputs_g)
        upstream = cotangent[target_g].astype(jnp.float32)
        grad_weight, grad_bias, grad_codes, grad_inputs = pullback(upstream)
        totals = (carry[0] + grad_weight, carry[1] + grad_bias, carry[2] + grad_codes)
        return (totals, (outputs.astype(jnp.bfloat16), grad_inputs.astype(jnp.bfloat16)))
    start = (jnp.zeros((IN, OUT), jnp.float32), jnp.zeros((OUT,), jnp.float32), jnp.zeros((SHAPES, CODE), jnp.float32))
    totals, (outs_g, grads_g) = lax.scan(group_step, start, (inputs_f.reshape(N_SHAPE, group_rows, PW), shape_ids.reshape(N_SHAPE, group_rows), target.reshape(N_SHAPE, group_rows)))
    layer_out = jnp.zeros((BUCKETS, OUT), jnp.bfloat16).at[target].set(outs_g.reshape(-1, OUT))
    input_grad = grads_g.reshape(POINTS, PW)
    direction_grad, gain_grad = norm_back(totals[0])
    counts_shape = jax.ops.segment_sum(jnp.ones((POINTS,), jnp.float32), shape_ids, SHAPES)
    sums = jax.ops.segment_sum(counts_shape[:, None] * codes_f, categories, CATS)
    squares = jax.ops.segment_sum(counts_shape[:, None] * codes_f * codes_f, categories, CATS)
    count_cat = jax.ops.segment_sum(counts_shape, categories, CATS)
    batch_mean = sums / count_cat[:, None]
    batch_var = squares / count_cat[:, None] - batch_mean * batch_mean
    rate = momentum[:, None]
    running_mean = (1.0 - rate) * prev_mean + rate * batch_mean
    running_var = (1.0 - rate) * prev_var + rate * batch_var
    return (layer_out, input_grad, totals[2], direction_grad, gain_grad, totals[1], running_mean, running_var)
```

```python
import functools

import jax
import jax.numpy as jnp
from jax import lax
from jax.experimental import pallas as pl
from jax.experimental.pallas import tpu as pltpu
from jax.sharding import PartitionSpec as P

HID = 253
CATS = 5
BLOCK = 256
TILE = 256
CHUNK = 2
WIN = BLOCK + 16
LEAD = 4
USUAL = 7
STEPS = 11
FAR = 1 << 20

norm_eps = 1e-06
CHEAP = pl.CostEstimate(flops=1, bytes_accessed=1, transcendentals=0)


def cost(us):
    return pl.CostEstimate(flops=us * 10**9, bytes_accessed=1, transcendentals=0)


f32, bf16, i32 = jnp.float32, jnp.bfloat16, jnp.int32


def params(mib):
    return pltpu.CompilerParams(vmem_limit_bytes=mib * 1024 * 1024)


def keep(x):
    return pltpu.with_memory_space_constraint(x, pltpu.VMEM)


def stay(x):
    return pltpu.with_memory_space_constraint(x, pltpu.HBM)


def specs(text):
    kinds = {"v": pltpu.VMEM, "s": pltpu.SMEM, "a": pl.ANY}
    return [pl.BlockSpec(memory_space=kinds[c]) for c in text]


def iota(shape, dim):
    return lax.broadcasted_iota(i32, shape, dim)


def ceil_to(n, step):
    return -(-n // step) * step


def plan(labels, groups, span):
    rows = labels.shape[0]
    count = len(groups)
    mask = jnp.concatenate([(labels >= g * span) & (labels < (g + 1) * span) for g in groups], axis=0)
    one = jnp.where(mask, 1.0, 0.0)
    m = one.astype(bf16)
    total = count * rows
    upper = jnp.where(iota((BLOCK, BLOCK), 0) <= iota((BLOCK, BLOCK), 1), 1.0, 0.0).astype(bf16)
    cum = jnp.dot(m, upper, preferred_element_type=f32)
    a, b = iota((total, total), 0), iota((total, total), 1)
    lower = jnp.where((a // rows == b // rows) & (b < a), 1.0, 0.0).astype(bf16)
    tot = jnp.sum(one, axis=1, keepdims=True)
    base = jnp.dot(lower, jnp.broadcast_to(tot, (total, 128)).astype(bf16), preferred_element_type=f32)[:, :1]
    lo, hi = base.astype(i32), (base + tot).astype(i32)
    pos = jnp.where(mask, lo + cum.astype(i32) - 1, -FAR)
    tot_row = lax.dot_general(jnp.ones((8, BLOCK), bf16), m, (((1,), (1,)), ((), ())), preferred_element_type=f32)
    base_row = lax.dot_general(tot_row.astype(bf16), lower, (((1,), (1,)), ((), ())), preferred_element_type=f32)
    return pos, lo, hi, base_row.astype(i32), (base_row + tot_row).astype(i32)


def sorted_rows(pos, lo, hi, rows, first, count):
    row, at = None, 0
    for n in range(first, first + count):
        s = slice(n * rows, (n + 1) * rows)
        start = lo[s] // 16 * 16
        r = pos[s] + (at - start)
        row = r if row is None else jnp.maximum(row, r)
        at = at + (hi[s] + 15) // 16 * 16 - start
    return row


def squeeze(pos, labels, group, span):
    rows, lanes = pos.shape
    at = iota((rows, lanes), 0) * lanes + iota((rows, lanes), 1)
    v = jnp.where(pos >= 0, (at - pos) * 16 + (labels - group * span + 1), 0)
    for bit in range((rows * lanes).bit_length() - 1):
        step = 1 << bit
        go = jnp.where(((v >> (4 + bit)) & 1) == 1, v, 0)
        if step < lanes:
            moved = pltpu.roll(go, lanes - step, 1)
            moved = jnp.where(iota((rows, lanes), 1) < lanes - step, moved, pltpu.roll(moved, rows - 1, 0))
        else:
            moved = pltpu.roll(go, rows - step // lanes, 0)
        v = v - go + moved
    return v & 15


def tiles_of(bounds, group, blocks, row=1):
    return (bounds[row, (group + 1) * blocks - 1] + TILE - 1) // TILE


def spans(bounds, groups, blocks, b):
    at, result = 0, []
    for g in groups:
        lo, hi = bounds[0, g * blocks + b], bounds[1, g * blocks + b]
        first = pl.multiple_of(lo // 16 * 16, 16)
        result.append((first, pl.multiple_of(at, 16) if result else 0, lo - first))
        at = at + ((hi + 15) // 16 * 16 - first)
    return result


def window_rows(count, step):
    return ceil_to(BLOCK + 30 * count, step)


def sort_rows(bounds, row_ref, x_ref, groups, blocks, moved, put):
    rows = window_rows(len(groups), 64)
    for b in range(blocks):
        hot = jnp.where(iota((rows, BLOCK), 0) == row_ref[b : b + 1, :], 1.0, 0.0).astype(bf16)
        out = jnp.dot(hot, x_ref[b * BLOCK : (b + 1) * BLOCK, :], preferred_element_type=f32).astype(bf16)
        moved[b, :rows, :] = out
        moved[b, rows:, :] = jnp.zeros((moved.shape[1] - rows, out.shape[1]), bf16)
    for n in range(len(groups)):
        for b in range(blocks):
            first, at, over = spans(bounds, groups, blocks, b)[n]
            dst, start = put(n, first)
            old = dst[pl.ds(start, 16), :]
            new = moved[b, pl.ds(at, 16), :]
            dst[pl.ds(start, 16), :] = jnp.where(iota((16, 1), 0) < over, old, new)
            rest = pl.ds(pl.multiple_of(start + 16, 16), BLOCK)
            dst[rest, :] = moved[b, pl.ds(pl.multiple_of(at + 16, 16), BLOCK), :]


def unsort_rows(bounds, row_ref, groups, blocks, pick, moved, emit):
    rows = window_rows(len(groups), 128)
    tail = BLOCK + 16
    for b in range(blocks):
        moved[b, tail:, :] = jnp.zeros((moved.shape[1] - tail, moved.shape[2]), bf16)
        for n, (first, at, _) in enumerate(spans(bounds, groups, blocks, b)):
            moved[b, pl.ds(at, WIN), :] = pick(n, first, WIN)
    for b in range(blocks):
        hot = jnp.where(iota((rows, BLOCK), 0) == row_ref[b : b + 1, :], 1.0, 0.0).astype(bf16)
        emit(b, jnp.dot(jnp.transpose(hot), moved[b, :rows, :], preferred_element_type=f32))


def layer_tile(x, named, ct, wp_ref, wpt_ref, cb_ref, gw_ref, span):
    rows = x.shape[0]
    col = jnp.transpose(jnp.broadcast_to(named.astype(f32), (8, rows)))[:, :1]
    pre = jnp.dot(x, wp_ref[...], preferred_element_type=f32)
    add = cb_ref[0:1, :]
    for s in range(1, span):
        add = jnp.where(col == s + 1.0, cb_ref[s : s + 1, :], add)
    pre = pre + add
    valid = col > 0.0
    e = jnp.exp(-jnp.abs(pre))
    u = 1.0 + e
    r = 1.0 / u
    soft = jnp.maximum(pre, 0.0) + jnp.where(e < 2.0**-9, e - (0.5 * e) * e, jnp.log(u))
    sig = jnp.where(pre >= 0.0, r, e * r)
    lo = jnp.where(valid, soft, 0.0).astype(bf16)
    gp = jnp.where(valid, ct.astype(f32) * sig, 0.0).astype(bf16)
    gx = jnp.dot(gp, wpt_ref[...], preferred_element_type=f32).astype(bf16)
    sel = jnp.where(jnp.broadcast_to(named, (16, rows)) == iota((16, rows), 0) + 1, 1.0, 0.0).astype(bf16)
    left = jnp.concatenate([jnp.transpose(x), sel], axis=0)
    gw_ref[...] += jnp.dot(left, gp, preferred_element_type=f32)
    return lo, gx


def pack_kernel(oct_count, shape_axis, oct_axis, span, cap, octants_hbm, ids_hbm, x_hbm, *refs):
    far = oct_count // 2 - 1
    octants_ref, ids_ref, x_ref, in_sem = refs[-4:]
    refs = refs[:-4]
    fetches = [
        pltpu.make_async_copy(a, b, in_sem.at[i])
        for i, (a, b) in enumerate(zip((octants_hbm, ids_hbm, x_hbm), (octants_ref, ids_ref, x_ref)))
    ]
    for f in fetches:
        f.start()
    heads, refs = refs[: far * LEAD], refs[far * LEAD :]
    queues, rows_far, refs = refs[:far], refs[far : 2 * far], refs[2 * far :]
    row_near, bounds_ref, names_ref, info_ref, moved, bounds_v, bounds, sem = refs
    blocks = row_near.shape[0]
    me = lax.axis_index(oct_axis)
    first_shape = lax.axis_index(shape_axis) * span

    def wide(ref):
        return jnp.concatenate([ref[pl.ds(h, blocks, 2), :] for h in range(2)], axis=1)

    for f in fetches[:2]:
        f.wait()
    ids = wide(ids_ref) - first_shape
    labels = (wide(octants_ref) ^ me) * span + ids
    pos, lo, hi, first_row, last_row = plan(labels, range(oct_count), span)
    n = oct_count * blocks
    bounds_v[...] = jnp.zeros(bounds_v.shape, i32)
    bounds_v[0:1, :n] = first_row[:1]
    bounds_v[1:2, :n] = last_row[:1]
    bounds_ref[...] = bounds_v[...]
    copy = pltpu.make_async_copy(bounds_v, bounds, sem)
    copy.start()
    row_near[...] = sorted_rows(pos, lo, hi, blocks, 0, 2)
    for k in range(far):
        rows_far[k][...] = sorted_rows(pos, lo, hi, blocks, 2 + 2 * k, 2)
    tiles = cap // TILE
    names_ref[...] = jnp.zeros(names_ref.shape, i32)
    for g in range(2):
        names_ref[g * 8 : g * 8 + tiles, :] = squeeze(pos[g * blocks : (g + 1) * blocks], labels, g, span)[:tiles]

    info_ref[...] = jnp.zeros(info_ref.shape, f32)
    for s in range(span):
        number = jnp.sum(jnp.sum(jnp.where(ids == s, 1.0, 0.0), axis=1, keepdims=True), axis=0, keepdims=True)
        info_ref[s : s + 1, :] = jnp.broadcast_to(number, (1, 128))

    for k in range(far):
        queues[k][...] = jnp.zeros(queues[k].shape, bf16)
    copy.wait()
    fetches[2].wait()
    rows = CHUNK * TILE
    for k in range(far):
        groups = [2 + 2 * k, 3 + 2 * k]
        cut = tiles_of(bounds, groups[0], blocks) * TILE
        sort_rows(bounds, rows_far[k], x_ref, groups, blocks, moved,
                  lambda n, first: (queues[k], pl.multiple_of(first + n * cut, 16)))
        for j in range(LEAD):
            heads[k * LEAD + j][:rows, :] = queues[k][j * rows : (j + 1) * rows, :]
        heads[k * LEAD][rows:, :] = labels.astype(f32).astype(bf16)


def pack(octants, ids, points, oct_count, span, cap):
    count, width = points.shape
    blocks = count // BLOCK
    far = oct_count // 2 - 1
    rows = CHUNK * TILE
    shape = jax.ShapeDtypeStruct
    heads = [pltpu.VMEM((rows + (blocks if j == 0 else 0), width), bf16) for j in range(LEAD)] * far
    outs = heads + [pltpu.VMEM((4 * cap, width), bf16)] * far
    outs += [shape((blocks, BLOCK), i32)] * (far + 1)
    outs += [shape((8, 128), i32), shape((16, BLOCK), i32), shape((8, 128), f32)]
    out = pl.pallas_call(
        functools.partial(pack_kernel, oct_count, "shape", "oct", span, cap),
        in_specs=specs("aaa"),
        out_specs=specs("v" * len(outs)),
        out_shape=outs,
        scratch_shapes=[
            pltpu.VMEM((blocks, window_rows(2, 64) + WIN, width), bf16),
            pltpu.VMEM((8, 128), i32),
            pltpu.SMEM((8, 128), i32),
            pltpu.SemaphoreType.DMA,
            pltpu.VMEM((count // 128, 128), i32),
            pltpu.VMEM((count // 128, 128), i32),
            pltpu.VMEM(points.shape, bf16),
            pltpu.SemaphoreType.DMA((3,)),
        ],
        compiler_params=params(16),
        cost_estimate=CHEAP,
        name="pack",
    )(stay(octants.reshape(-1, 128)), stay(ids.reshape(-1, 128)), stay(points))
    heads, queues, rows_far, out = out[: far * LEAD], out[far * LEAD : far * LEAD + far], out[far * LEAD + far : far * LEAD + 2 * far], out[far * LEAD + 2 * far :]
    return heads, queues, rows_far, out


def set_weights(hid, direction_ref, gain_ref, bias_ref, codes_ref, wp_ref, wpt_ref, w_ref, cb_ref, norm_ref):
    direction = direction_ref[...]
    norms = jnp.sqrt(jnp.sum(direction * direction, axis=0, keepdims=True) + norm_eps)
    weight = (direction * (gain_ref[...] / norms)).astype(bf16)
    norm_ref[...] = norms
    w_ref[...] = weight
    width = wp_ref.shape[0]
    wf = weight.astype(f32)
    last = jnp.where(iota((8, 1), 0) + (width - 8) < hid, wf[width - 8 : width, :], wf[-8:, :])
    wp = jnp.concatenate([wf[: width - 8, :], last], axis=0)
    wp_ref[...] = wp.astype(bf16)
    wpt_ref[...] = wp.T.astype(bf16)
    span, code_width = codes_ref.shape
    w_code = wf[hid : hid + code_width, :].astype(bf16)
    codes = jnp.concatenate([codes_ref[...].astype(f32), jnp.zeros((8 - span, code_width), f32)], axis=0).astype(bf16)
    cb_ref[...] = jnp.dot(codes, w_code, preferred_element_type=f32) + bias_ref[...]


def prepare_kernel(oct_count, oct_axis, cap, bounds, row_ref, x_ref, codes_v, direction_hbm, gain_hbm, bias_hbm,
                   lo_hbm, lon_hbm, lof_hbm, gw_ref, buf, wp_ref, wpt_ref, w_ref, cb_ref, norm_ref,
                   moved, zero, direction_v, gain_v, bias_v, zero_sem, in_sem):
    blocks = row_ref.shape[0]
    tiles = cap // TILE
    source = lax.axis_index(oct_axis)
    cut = [tiles_of(bounds, r, blocks) for r in range(2)]
    fetches = [
        pltpu.make_async_copy(a, b, in_sem.at[i])
        for i, (a, b) in enumerate(((direction_hbm, direction_v), (gain_hbm, gain_v), (bias_hbm, bias_v)))
    ]
    for f in fetches:
        f.start()

    def clear(go):
        for t in range(tiles):
            for k in range(oct_count // 2):
                @pl.when(t >= (cut[0] if k == 0 else 0))
                def _():
                    at = (source ^ (2 * k)) * cap + t * TILE
                    go(pltpu.make_async_copy(zero, lo_hbm.at[pl.ds(pl.multiple_of(at, TILE), TILE), :], zero_sem))

            @pl.when(t >= cut[1])
            def _():
                go(pltpu.make_async_copy(zero, lon_hbm.at[pl.ds(t * TILE, TILE), :], zero_sem))

        for t in range(lof_hbm.shape[0] // TILE):
            go(pltpu.make_async_copy(zero, lof_hbm.at[pl.ds(t * TILE, TILE), :], zero_sem))

    zero[...] = jnp.zeros(zero.shape, bf16)
    clear(lambda c: c.start())
    gw_ref[...] = jnp.zeros(gw_ref.shape, f32)
    buf[...] = jnp.zeros(buf.shape, bf16)
    sort_rows(bounds, row_ref, x_ref, [0, 1], blocks, moved, lambda n, first: (buf.at[n], first))
    for f in fetches:
        f.wait()
    set_weights(HID, direction_v, gain_v, bias_v, codes_v, wp_ref, wpt_ref, w_ref, cb_ref, norm_ref)
    clear(lambda c: c.wait())


def prepare(bounds, row, points, direction, gain, bias, codes, oct_count, cap):
    width = points.shape[1]
    ins, outs = direction.shape
    blocks = row.shape[0]
    return pl.pallas_call(
        functools.partial(prepare_kernel, oct_count, "oct", cap),
        in_specs=specs("svvvaaa"),
        out_specs=specs("aaavvvvvvv"),
        out_shape=[
            pltpu.HBM((oct_count * cap, outs), bf16),
            pltpu.HBM((cap, outs), bf16),
            pltpu.HBM(((oct_count // 2 - 1) * cap, outs), bf16),
            pltpu.VMEM((width + 16, outs), f32),
            pltpu.VMEM((2, cap + WIN, width), bf16),
            pltpu.VMEM((width, outs), bf16),
            pltpu.VMEM((outs, width), bf16),
            pltpu.VMEM((ins, outs), bf16),
            pltpu.VMEM((8, outs), f32),
            pltpu.VMEM((1, outs), f32),
        ],
        scratch_shapes=[
            pltpu.VMEM((blocks, window_rows(2, 64) + WIN, width), bf16),
            pltpu.VMEM((TILE, outs), bf16),
            pltpu.VMEM((ins, outs), f32),
            pltpu.VMEM((1, outs), f32),
            pltpu.VMEM((1, outs), f32),
            pltpu.SemaphoreType.DMA,
            pltpu.SemaphoreType.DMA((3,)),
        ],
        compiler_params=params(14),
        cost_estimate=cost(4),
        name="prepare",
    )(bounds, row, keep(points), codes, stay(direction), stay(gain[None, :]), stay(bias[None, :]))


def local_kernel(oct_axis, blocks, span, cap, bounds, names_ref, ct_hbm, ctx_ref, wp_ref, wpt_ref, cb_ref, lo_in, lon_in, gw_in, buf_in,
                 lo_hbm, lon_hbm, gw_ref, buf, ct_v, lo_v, ct_sem, lo_sem):
    source = lax.axis_index(oct_axis)
    cut = [tiles_of(bounds, r, blocks) for r in range(2)]
    count = cut[0] + cut[1]

    def split(i):
        second = (i >= cut[0]).astype(i32)
        return second, i - second * cut[0]

    def fetch(i, go):
        second, t = split(i)
        rows = pl.ds(pl.multiple_of(source * cap + t * TILE, TILE), TILE)

        @pl.when(second == 0)
        def _():
            go(pltpu.make_async_copy(ct_hbm.at[rows, :], ct_v.at[i % 2], ct_sem.at[i % 2]))

        @pl.when(second == 1)
        def _():
            go(pltpu.make_async_copy(ctx_ref.at[rows, :], ct_v.at[i % 2], ct_sem.at[i % 2]))

    def store(i, go):
        second, t = split(i)

        @pl.when(second == 0)
        def _():
            rows = pl.ds(pl.multiple_of(source * cap + t * TILE, TILE), TILE)
            go(pltpu.make_async_copy(lo_v.at[i % 2], lo_hbm.at[rows, :], lo_sem.at[i % 2]))

        @pl.when(second == 1)
        def _():
            go(pltpu.make_async_copy(lo_v.at[i % 2], lon_hbm.at[pl.ds(pl.multiple_of(t * TILE, TILE), TILE), :], lo_sem.at[i % 2]))

    @pl.when(count > 0)
    def _():
        fetch(0, lambda c: c.start())

    def step(i, carry):
        second, t = split(i)

        @pl.when(i + 1 < count)
        def _():
            fetch(i + 1, lambda c: c.start())

        fetch(i, lambda c: c.wait())

        @pl.when(i >= 2)
        def _():
            store(i - 2, lambda c: c.wait())

        rows = pl.ds(pl.multiple_of(t * TILE, TILE), TILE)
        named = names_ref[pl.ds(second * 8 + t, 1), :]
        lo, gx = layer_tile(buf[second, rows, :], named, ct_v[i % 2], wp_ref, wpt_ref, cb_ref, gw_ref, span)
        lo_v[i % 2] = lo
        buf[second, rows, :] = gx
        store(i, lambda c: c.start())
        return carry

    lax.fori_loop(0, count, step, 0)
    for back in (2, 1):
        @pl.when(count >= back)
        def _():
            store(count - back, lambda c: c.wait())


def local(bounds, names, cotangent, ctx, weights, lo, lon, gw, buf, blocks, span, cap):
    outs = lo.shape[1]
    return pl.pallas_call(
        functools.partial(local_kernel, "oct", blocks, span, cap),
        in_specs=specs("svavvvvaavv"),
        out_specs=specs("aavv"),
        out_shape=[pltpu.HBM(lo.shape, bf16), pltpu.HBM(lon.shape, bf16), pltpu.VMEM(gw.shape, f32), pltpu.VMEM(buf.shape, bf16)],
        input_output_aliases={7: 0, 8: 1, 9: 2, 10: 3},
        scratch_shapes=[
            pltpu.VMEM((2, TILE, outs), bf16),
            pltpu.VMEM((2, TILE, outs), bf16),
            pltpu.SemaphoreType.DMA((2,)),
            pltpu.SemaphoreType.DMA((2,)),
        ],
        compiler_params=params(8),
        cost_estimate=cost(8),
        name="local",
    )(bounds, names, stay(cotangent), keep(ctx), *[keep(w) for w in weights], stay(lo), stay(lon), keep(gw), keep(buf))


def unlocal_kernel(bounds, row_ref, gbuf, part_ref, moved):
    blocks = row_ref.shape[0]

    def emit(b, rows):
        part_ref[b * BLOCK : (b + 1) * BLOCK, :] = rows.astype(bf16)

    unsort_rows(bounds, row_ref, [0, 1], blocks, lambda n, first, rows: gbuf[n, pl.ds(first, rows), :], moved, emit)


def unlocal(bounds, row, gbuf):
    blocks, width = row.shape[0], gbuf.shape[2]
    return pl.pallas_call(
        unlocal_kernel,
        in_specs=specs("svv"),
        out_specs=specs("v")[0],
        out_shape=pltpu.VMEM((blocks * BLOCK, width), bf16),
        scratch_shapes=[pltpu.VMEM((blocks, window_rows(2, 128) + WIN, width), bf16)],
        compiler_params=params(16),
        cost_estimate=CHEAP,
        name="unlocal",
    )(bounds, row, keep(gbuf))


def names_kernel(kx, span, cap, labels_ref, names_ref, count_ref, back_ref):
    labels = labels_ref[...].astype(f32).astype(i32)
    blocks = labels.shape[0]
    groups = [2 * kx, 2 * kx + 1]
    pos, _, _, _, last = plan(labels, groups, span)
    tiles = cap // TILE
    names_ref[...] = jnp.zeros(names_ref.shape, i32)
    for n, g in enumerate(groups):
        names_ref[n * 8 : n * 8 + tiles, :] = squeeze(pos[n * blocks : (n + 1) * blocks], labels, g, span)[:tiles]
    count_ref[...] = jnp.zeros(count_ref.shape, i32)
    count_ref[0:1, : 2 * blocks] = last[:1]
    back_ref[...] = jnp.zeros(back_ref.shape, bf16)


def make_names(labels, kx, span, cap):
    return pl.pallas_call(
        functools.partial(names_kernel, kx, span, cap),
        in_specs=specs("v"),
        out_specs=specs("vvv"),
        out_shape=[
            jax.ShapeDtypeStruct((16, BLOCK), i32),
            jax.ShapeDtypeStruct((8, 128), i32),
            pltpu.VMEM((2 * cap + CHUNK * TILE, labels.shape[1]), bf16),
        ],
        compiler_params=params(8),
        cost_estimate=CHEAP,
        name="names",
    )(labels)


def chunks(tiles):
    return (tiles + CHUNK - 1) // CHUNK


def lead_of(tiles):
    return jnp.maximum(chunks(tiles), LEAD)


def take_back(step_no, theirs, blocks, x_ref, back, limit=None):
    rows = CHUNK * TILE
    limit = limit or back.shape[0] // rows - 1
    n = step_no - lead_of(tiles_of(theirs, 0, blocks, 0) + tiles_of(theirs, 1, blocks, 0))

    @pl.when((n >= 0) & (n < limit))
    def _():
        back[pl.ds(pl.multiple_of(n * rows, rows), rows), :] = x_ref[:rows, :]


def far_kernel(chunk, first, last, loop, kx, oct_axis, blocks, span, cap, mine, theirs, *refs):
    if loop:
        turn, refs = refs[0], refs[1:]
    names_ref, x_ref, ct_hbm, ctx_hbm, wp_ref, wpt_ref, cb_ref, queue_in, lo_in, lof_in, gw_in, back_in, refs = *refs[:12], refs[12:]
    if not first:
        ct_v, lo_old, refs = *refs[:2], refs[2:]
    queue, lo_hbm, lof_hbm, gw_ref, back, payload, refs = *refs[:6], refs[6:]
    if not last:
        ct_new, refs = refs[0], refs[1:]
    lo_v, refs = refs[0], refs[1:]
    if first:
        ct_v, refs = refs[0], refs[1:]
    ct_sem, new_sem, lo_sem = refs
    source = lax.axis_index(oct_axis) ^ (2 * kx)
    cut = [tiles_of(theirs, r, blocks, 0) for r in range(2)]
    lead = lead_of(tiles_of(mine, 2 * kx, blocks) + tiles_of(mine, 2 * kx + 1, blocks))
    count = cut[0] + cut[1]
    rows = CHUNK * TILE
    if loop:
        count = jnp.where(turn[0] == 0, count, 0)

    def split(c, i):
        t = c * CHUNK + i
        second = (t >= cut[0]).astype(i32)
        return t, second, t - second * cut[0]

    def ct_copy(c, i, dst, sem, go):
        t, second, slot = split(c, i)
        at = pl.ds(pl.multiple_of(source * cap + slot * TILE, TILE), TILE)
        to = dst.at[pl.ds(i * TILE, TILE), :]

        @pl.when((t < count) & (second == 0))
        def _():
            go(pltpu.make_async_copy(ct_hbm.at[at, :], to, sem.at[i]))

        @pl.when((t < count) & (second == 1))
        def _():
            go(pltpu.make_async_copy(ctx_hbm.at[at, :], to, sem.at[i]))

    def lo_copy(c, i, src, go):
        t, second, slot = split(c, i)
        of = src.at[pl.ds(i * TILE, TILE), :]

        @pl.when((t < count) & (second == 0))
        def _():
            at = pl.ds(pl.multiple_of(source * cap + slot * TILE, TILE), TILE)
            go(pltpu.make_async_copy(of, lo_hbm.at[at, :], lo_sem.at[i]))

        @pl.when((t < count) & (second == 1))
        def _():
            at = pl.ds(pl.multiple_of((kx - 1) * cap + slot * TILE, TILE), TILE)
            go(pltpu.make_async_copy(of, lof_hbm.at[at, :], lo_sem.at[i]))

    start, wait = lambda c: c.start(), lambda c: c.wait()
    for i in range(CHUNK):
        if first:
            ct_copy(chunk, i, ct_v, ct_sem, start)
        else:
            lo_copy(chunk - 1, i, lo_old, start)
        if not last:
            ct_copy(chunk + 1, i, ct_new, new_sem, start)
    if not loop:
        take_back(chunk, theirs, blocks, x_ref, back)
    for i in range(CHUNK):
        t, second, slot = split(chunk, i)
        at = slice(i * TILE, (i + 1) * TILE)

        @pl.when(t < count)
        def _():
            if first:
                ct_copy(chunk, i, ct_v, ct_sem, wait)
            named = names_ref[pl.ds(second * 8 + slot, 1), :]
            lo, gx = layer_tile(x_ref[at, :], named, ct_v[at, :], wp_ref, wpt_ref, cb_ref, gw_ref, span)
            lo_v[at, :] = lo
            queue[pl.ds(pl.multiple_of((lead + chunk) * rows + i * TILE, TILE), TILE), :] = gx

    if loop:
        payload[...] = queue[pl.ds(pl.multiple_of((turn[0] + STEPS - 1) * rows, rows), rows), :]
        for i in range(CHUNK):
            lo_copy(chunk, i, lo_v, start)
        for i in range(CHUNK):
            lo_copy(chunk, i, lo_v, wait)
    else:
        payload[...] = queue[(chunk + LEAD) * rows : (chunk + LEAD + 1) * rows, :]
    for i in range(CHUNK):
        if not first:
            lo_copy(chunk - 1, i, lo_old, wait)
        if not last:
            ct_copy(chunk + 1, i, ct_new, new_sem, wait)


def far_step(chunk, kx, mine, theirs, names, x, cotangent, ctx, weights, state, ahead, blocks, span, cap, last, turn=None):
    wp, wpt, cb = weights
    queue, lo, lof, gw, back = state
    width, outs = wp.shape
    rows = CHUNK * TILE
    loop, first = turn is not None, ahead is None
    shapes = [pltpu.VMEM(queue.shape, bf16), pltpu.HBM(lo.shape, bf16), pltpu.HBM(lof.shape, bf16), pltpu.VMEM(gw.shape, f32),
              pltpu.VMEM(back.shape, bf16), pltpu.VMEM((rows, width), bf16)]
    shapes += [pltpu.VMEM((rows, outs), bf16)] * ((not last) + (not loop))
    base = 2 + loop
    args = [mine, theirs] + ([turn] if loop else []) + [names, keep(x), stay(cotangent), keep(ctx), keep(wp), keep(wpt), keep(cb), keep(queue), stay(lo),
            stay(lof), keep(gw), keep(back)] + [keep(a) for a in (ahead or ())]
    out = pl.pallas_call(
        functools.partial(far_kernel, chunk, first, last, loop, kx, "oct", blocks, span, cap),
        in_specs=specs("ss" + "s" * loop + "vvavvvvvaavv" + "vv" * (not first)),
        out_specs=specs("vaavvv" + "v" * (len(shapes) - 6)),
        out_shape=shapes,
        input_output_aliases={base + 7 + i: i for i in range(5)},
        scratch_shapes=([pltpu.VMEM((rows, outs), bf16)] * (first + loop))
        + [pltpu.SemaphoreType.DMA((CHUNK,)), pltpu.SemaphoreType.DMA((CHUNK,)), pltpu.SemaphoreType.DMA((CHUNK,))],
        compiler_params=params(12),
        cost_estimate=CHEAP,
        name="far",
    )(*args)
    return tuple(out[:5]), out[5], (None if loop else (None if last else out[6], out[6 + (not last)]))


def flush_kernel(chunk, kx, oct_axis, blocks, cap, theirs, lo_old, lo_in, lof_in, lo_hbm, lof_hbm, sem):
    source = lax.axis_index(oct_axis) ^ (2 * kx)
    cut = [tiles_of(theirs, r, blocks, 0) for r in range(2)]
    for go in (lambda c: c.start(), lambda c: c.wait()):
        for i in range(CHUNK):
            t = chunk * CHUNK + i
            second = (t >= cut[0]).astype(i32)
            slot = t - second * cut[0]
            of = lo_old.at[pl.ds(i * TILE, TILE), :]

            @pl.when((t < cut[0] + cut[1]) & (second == 0))
            def _():
                at = pl.ds(pl.multiple_of(source * cap + slot * TILE, TILE), TILE)
                go(pltpu.make_async_copy(of, lo_hbm.at[at, :], sem.at[i]))

            @pl.when((t < cut[0] + cut[1]) & (second == 1))
            def _():
                at = pl.ds(pl.multiple_of((kx - 1) * cap + slot * TILE, TILE), TILE)
                go(pltpu.make_async_copy(of, lof_hbm.at[at, :], sem.at[i]))


def flush(chunk, kx, theirs, lo_old, lo, lof, blocks, cap):
    return pl.pallas_call(
        functools.partial(flush_kernel, chunk, kx, "oct", blocks, cap),
        in_specs=specs("svaa"),
        out_specs=specs("aa"),
        out_shape=[pltpu.HBM(lo.shape, bf16), pltpu.HBM(lof.shape, bf16)],
        input_output_aliases={2: 0, 3: 1},
        scratch_shapes=[pltpu.SemaphoreType.DMA((CHUNK,))],
        compiler_params=params(4),
        cost_estimate=CHEAP,
        name="flush",
    )(theirs, keep(lo_old), stay(lo), stay(lof))


def return_kernel(blocks, turn, theirs, x_ref, back_in, back):
    take_back(turn[0] + STEPS - 1, theirs, blocks, x_ref, back)


def return_step(turn, theirs, x, back, blocks):
    return pl.pallas_call(
        functools.partial(return_kernel, blocks),
        in_specs=specs("ssvv"),
        out_specs=specs("v")[0],
        out_shape=pltpu.VMEM(back.shape, bf16),
        input_output_aliases={3: 0},
        compiler_params=params(8),
        cost_estimate=CHEAP,
        name="returned",
    )(turn, theirs, keep(x), keep(back))


def unpack_kernel(far, blocks, lasts, limit, bounds, *refs):
    theirs, rows_far, refs = refs[:far], refs[far : 2 * far], refs[2 * far :]
    parts, refs = refs[: far * len(lasts)], refs[far * len(lasts) :]
    part_ref, refs = refs[0], refs[1 + far :]
    out_ref, backs, moved = refs[0], refs[1 : 1 + far], refs[-1]
    for k in range(far):
        for j, step_no in enumerate(lasts):
            take_back(step_no, theirs[k], blocks, parts[k * len(lasts) + j], backs[k], limit)
        cut = tiles_of(bounds, 2 + 2 * k, blocks) * TILE

        def pick(n, first, count):
            return backs[k][pl.ds(pl.multiple_of(first + n * cut, 16), count), :]

        def emit(b, value):
            at = slice(b * BLOCK, (b + 1) * BLOCK)
            before = part_ref if k == 0 else out_ref
            out_ref[at, :] = (value + before[at, :].astype(f32)).astype(bf16)

        unsort_rows(bounds, rows_far[k], [2 + 2 * k, 3 + 2 * k], blocks, pick, moved, emit)


def unpack(bounds, theirs, rows_far, lasts, limit, parts, part, backs):
    points, width = part.shape
    blocks = points // BLOCK
    far = len(theirs)
    extra = far * len(lasts)
    return pl.pallas_call(
        functools.partial(unpack_kernel, far, blocks, lasts, limit),
        in_specs=specs("s" + "s" * far + "v" * (2 * far + extra + 1)),
        out_specs=specs("v" * (1 + far)),
        out_shape=[jax.ShapeDtypeStruct(part.shape, bf16)] + [pltpu.VMEM(b.shape, bf16) for b in backs],
        input_output_aliases={2 * far + extra + 2 + k: 1 + k for k in range(far)},
        scratch_shapes=[pltpu.VMEM((blocks, window_rows(2, 128) + WIN, width), bf16)],
        compiler_params=params(20),
        cost_estimate=CHEAP,
        name="unpack",
    )(bounds, *theirs, *rows_far, *[keep(x) for x in parts], keep(part), *[keep(b) for b in backs])[0]


def merge_kernel(cap, kxs, oct_axis, lox_ref, lo_in, lo_hbm, sem):
    other = lax.axis_index(oct_axis) ^ 1
    for go in (lambda c: c.start(), lambda c: c.wait()):
        for n, k in enumerate(kxs):
            at = pl.ds(pl.multiple_of((other ^ (2 * k)) * cap, cap), cap)
            go(pltpu.make_async_copy(lox_ref.at[pl.ds(n * cap, cap), :], lo_hbm.at[at, :], sem.at[n]))


def merge(lox, lo, cap, kxs):
    return pl.pallas_call(
        functools.partial(merge_kernel, cap, tuple(kxs), "oct"),
        in_specs=specs("va"),
        out_specs=specs("a")[0],
        out_shape=pltpu.HBM(lo.shape, lo.dtype),
        input_output_aliases={1: 0},
        scratch_shapes=[pltpu.SemaphoreType.DMA((len(kxs),))],
        compiler_params=params(4),
        cost_estimate=CHEAP,
        name="merge",
    )(keep(lox), stay(lo))


def column_block(axes, n):
    a, b = (lax.axis_index(axis) % 2 for axis in axes)
    return (a ^ (n % 2)) * 2 + (b ^ (n // 2))


def collect_kernel(axes, shape_axis, oct_axis, shapes, span, extra, blocks, late, *refs):
    mine, refs = refs[0], refs[1:]
    theirs, refs = refs[:extra], refs[extra:]
    gw_ref, info_ref, codes_ref, outs, full = *refs[:3], refs[3:7], refs[7]
    width = gw_ref.shape[0] - 16
    cols = gw_ref.shape[1]
    code_width = codes_ref.shape[1]
    base = lax.axis_index(shape_axis) * span
    full[:width, :] = gw_ref[:width, :]
    ps = jnp.zeros((shapes, cols), f32)
    for s in range(span):
        ps = ps + jnp.where(iota((shapes, 1), 0) == base + s, gw_ref[width + s : width + s + 1, :], 0.0)
    full[width : width + shapes, :] = ps
    if late:
        full[width + shapes :, :] = jnp.zeros((full.shape[0] - width - shapes, cols), f32)
    else:
        lane = iota((1, cols - code_width), 1)
        info = jnp.zeros((shapes, cols), f32)
        for s in range(span):
            number = info_ref[s : s + 1, :1]
            high = jnp.floor(number / 1024.0)
            mid = jnp.floor((number - 1024.0 * high) / 32.0)
            low = number - 1024.0 * high - 32.0 * mid
            digits = jnp.where(lane < 64, low, jnp.where(lane < 128, mid, high))
            code = jnp.where(lax.axis_index(oct_axis) == 0, codes_ref[s : s + 1, :].astype(f32), 0.0)
            info = info + jnp.where(iota((shapes, 1), 0) == base + s, jnp.concatenate([code, digits], axis=1), 0.0)
        full[width + shapes : width + 2 * shapes, :] = info
        flag = jnp.int32(0)
        for k in range(extra):
            ours = chunks(tiles_of(mine, 2 + 2 * k, blocks) + tiles_of(mine, 3 + 2 * k, blocks))
            other = chunks(tiles_of(theirs[k], 0, blocks, 0) + tiles_of(theirs[k], 1, blocks, 0))
            most = jnp.maximum(jnp.maximum(ours, LEAD) + other, jnp.maximum(other, LEAD) + ours)
            flag = flag | ((jnp.maximum(ours, other) > USUAL) | (most > STEPS)).astype(i32)
        full[width + 2 * shapes :, :] = jnp.zeros((16, cols), f32) + flag.astype(f32)
    for n in range(4):
        at = pl.ds(pl.multiple_of(column_block(axes, n) * 128, 128), 128)
        outs[n][...] = full[:, at].astype(bf16)


def finish_kernel(axes, shape_axis, hid, span, categories, momentum, *refs):
    parts, refs = refs[:4], refs[4:]
    direction_ref, gain_ref, norm_ref, w_ref, mean_ref, var_ref, refs = *refs[:6], refs[6:]
    dg_ref, gg_ref, bg_ref, cg_ref, mean_out, var_out, full = refs
    for n in range(4):
        at = pl.ds(pl.multiple_of(column_block(axes, n) * 128, 128), 128)
        full[:, at] = parts[n][...].astype(f32)
    ins, cols = direction_ref.shape
    cats, code_width = mean_ref.shape
    shapes = (full.shape[0] - 16 - (ins - code_width)) // 2
    width = ins - code_width
    ps = full[width : width + shapes, :]
    info = full[width + shapes : width + 2 * shapes, :]
    codes = info[:, :code_width]
    at = code_width
    number = info[:, at : at + 1] + 32.0 * info[:, at + 64 : at + 65] + 1024.0 * info[:, at + 128 : at + 129]
    for c in range(cats):
        chosen = jnp.zeros((shapes, 1), f32)
        for s in range(shapes):
            chosen = jnp.where((iota((shapes, 1), 0) == s) & (categories[s] == c), 1.0, chosen)
        weight = chosen * number
        count = jnp.sum(weight, axis=0, keepdims=True)
        mean = jnp.sum(weight * codes, axis=0, keepdims=True) / count
        var = jnp.sum(weight * codes * codes, axis=0, keepdims=True) / count - mean * mean
        rate = momentum[c]
        mean_out[c : c + 1, :] = (1.0 - rate) * mean_ref[c : c + 1, :] + rate * mean
        var_out[c : c + 1, :] = (1.0 - rate) * var_ref[c : c + 1, :] + rate * var

    gw = full[:width, :]
    codes_all = jnp.concatenate(
        [jnp.zeros((shapes, hid), f32), codes, jnp.zeros((shapes, ins - hid - code_width), f32)], axis=1
    )
    wg = lax.dot_general(codes_all, ps, (((0,), (0,)), ((), ())), precision=lax.Precision.HIGHEST, preferred_element_type=f32)
    head = jnp.where(iota((width, 1), 0) < hid, gw, wg[:width])
    tail = jnp.where(iota((8, 1), 0) + (width - 8) >= hid, gw[width - 8 :], wg[ins - 8 :])
    wg = jnp.concatenate([head, wg[width : ins - 8], tail], axis=0)
    direction = direction_ref[...]
    norms = norm_ref[...]
    dots = jnp.sum(wg * direction, axis=0, keepdims=True)
    gg_ref[...] = dots / norms
    dg_ref[...] = (gain_ref[...] / norms) * (wg - direction * (dots / (norms * norms)))
    bg_ref[...] = jnp.sum(ps, axis=0, keepdims=True)
    base = lax.axis_index(shape_axis) * span
    own = jnp.zeros((8, cols), f32)
    for s in range(span):
        row = jnp.sum(jnp.where(iota((shapes, 1), 0) == base + s, ps, 0.0), axis=0, keepdims=True)
        own = own + jnp.where(iota((8, 1), 0) == s, row, 0.0)
    cg_ref[...] = lax.dot_general(own, w_ref[...].astype(f32), (((1,), (1,)), ((), ())), precision=lax.Precision.HIGHEST, preferred_element_type=f32)


def finish(axes, span, categories, momentum, parts, direction, gain, norms, weight, prev_mean, prev_var):
    ins, outs = direction.shape
    return pl.pallas_call(
        functools.partial(finish_kernel, axes, "shape", HID, span),
        in_specs=specs("ss" + "v" * 10),
        out_specs=specs("v" * 6),
        out_shape=[
            jax.ShapeDtypeStruct((ins, outs), f32),
            jax.ShapeDtypeStruct((1, outs), f32),
            jax.ShapeDtypeStruct((1, outs), f32),
            jax.ShapeDtypeStruct((8, ins), f32),
            jax.ShapeDtypeStruct(prev_mean.shape, f32),
            jax.ShapeDtypeStruct(prev_mean.shape, f32),
        ],
        scratch_shapes=[pltpu.VMEM((parts[0].shape[0], outs), f32)],
        compiler_params=params(12),
        cost_estimate=CHEAP,
        name="finish",
    )(categories, momentum, *[keep(p) for p in parts], keep(direction), gain[None, :], keep(norms), keep(weight), prev_mean, prev_var)


def swap(v, axis, k):
    n = lax.axis_size(axis)
    return lax.ppermute(v, axis, [(i, i ^ k) for i in range(n)])


def swap_both(v, k):
    n, m = lax.axis_size("shape"), lax.axis_size("oct")
    return lax.ppermute(v, ("shape", "oct"), [(i, i ^ k) for i in range(n * m)])


def bits(axis, first):
    n = lax.axis_size(axis)
    return [(axis, 1 << j) for j in range(first, n.bit_length() - 1)]


def after(x, *others):
    return lax.optimization_barrier((x, *others))[0]


def quarters_to(parts):
    m = lax.axis_size("oct")
    return [swap(parts[0], "oct", 1), swap(parts[1], "shape", 1), swap_both(parts[2], m + 1)]


def total_quarter(parts):
    got = quarters_to(parts[1:])
    v = (parts[0].astype(f32) + got[0].astype(f32) + got[1].astype(f32) + got[2].astype(f32)).astype(bf16)
    yield v
    for axis, k in bits("shape", 1) + bits("oct", 1):
        v = (v.astype(f32) + swap(v, axis, k).astype(f32)).astype(bf16)
        yield v


AXES = ("oct", "shape")


def collect(mine, theirs, gw, info, codes, shapes, blocks, late):
    span = codes.shape[0]
    rows = gw.shape[0] - 16 + 2 * shapes + 16
    return pl.pallas_call(
        functools.partial(collect_kernel, AXES, "shape", "oct", shapes, span, len(theirs), blocks, late),
        in_specs=specs("s" + "s" * len(theirs) + "vvv"),
        out_specs=specs("vvvv"),
        out_shape=[pltpu.VMEM((rows, 128), bf16)] * 4,
        scratch_shapes=[pltpu.VMEM((rows, gw.shape[1]), f32)],
        compiler_params=params(8),
        cost_estimate=CHEAP,
        name="collect",
    )(mine, *theirs, keep(gw), info, codes)


def body(point_inputs, shape_ids, octants, categories, codes, direction, gain, bias, cotangent, prev_mean, prev_var, momentum):
    points, width = point_inputs.shape
    oct_count, shape_dev = lax.axis_size("oct"), lax.axis_size("shape")
    cap = 2 * points // oct_count
    span, code_width = codes.shape
    shapes = shape_dev * span
    blocks = points // BLOCK
    rows = CHUNK * TILE
    far = list(range(1, oct_count // 2))
    most = chunks(2 * cap // TILE)
    usual = min(USUAL, most)
    steps = min(STEPS, max(most, LEAD) + most)
    loop = (usual, steps) != (most, max(most, LEAD) + most)
    assert most - usual <= 1

    ctx = swap(cotangent, "oct", 1)
    heads, queues, rows_far, (row_near, mine, near_names, info) = pack(
        octants, shape_ids, point_inputs, oct_count, span, cap)
    got = {(k, j): swap(heads[(k - 1) * LEAD + j], "oct", 2 * k) for k in far for j in range(LEAD)}
    lo, lon, lof, gw, buf, wp, wpt, weight, cb, norms = prepare(
        mine, row_near, point_inputs, direction, gain, bias, codes, oct_count, cap)
    weights = (wp, wpt, cb)

    queue = {k: queues[k - 1] for k in far}
    named, theirs, back, ahead = {}, {}, {}, {}
    for k in far:
        named[k], theirs[k], back[k] = make_names(after(got[k, 0], gw)[rows:], k, span, cap)
        ahead[k] = None
    lo, lon, gw, buf = local(mine, near_names, cotangent, ctx, weights, lo, lon, after(gw, back[1]), buf, blocks, span, cap)
    for c in range(usual):
        for k in far:
            x = got[k, c]
            if c == min(4, usual - 1):
                part = unlocal(mine, row_near, buf)
                x = after(x, part)
            (queue[k], lo, lof, gw, back[k]), payload, ahead[k] = far_step(
                c, k, mine, theirs[k], named[k], x, cotangent, ctx, weights, (queue[k], lo, lof, gw, back[k]), ahead[k],
                blocks, span, cap, c == usual - 1)
            if c + LEAD < steps:
                got[k, c + LEAD] = swap(payload, "oct", 2 * k)
        if c == 1:
            lo = merge(swap(lon, "oct", 1), lo, cap, [0])
    their = [theirs[k] for k in far]
    sums = total_quarter(collect(mine, their, gw, info, codes, shapes, blocks, False))
    v = next(sums)
    for k in far:
        lo, lof = flush(usual - 1, k, theirs[k], after(ahead[k][1], v), lo, lof, blocks, cap)
    v = next(sums)
    lo = merge(after(swap(lof, "oct", 1), v), lo, cap, far)
    for v in sums:
        pass
    parts = [v] + quarters_to([v] * 3)
    lasts = list(range(usual, steps))

    if loop:
        left = jnp.where(v[-1, 0] > 0, max(most, LEAD) + most - (STEPS - 1), 0).astype(i32)
        zeros = jnp.zeros(gw.shape, f32)

        def more(carry):
            i, queue, lo, lof, back, parts = carry
            turn = i.reshape(1)
            queue, back = dict(zip(far, queue)), dict(zip(far, back))
            gw = zeros
            for k in far:
                (queue[k], lo, lof, gw, back[k]), payload, _ = far_step(
                    usual, k, mine, theirs[k], named[k], got[k, usual], cotangent, ctx, weights, (queue[k], lo, lof, gw, back[k]),
                    None, blocks, span, cap, True, turn)
                back[k] = return_step(turn, theirs[k], swap(payload, "oct", 2 * k), back[k], blocks)
            lo = merge(swap(lof, "oct", 1), lo, cap, far)
            sums = list(total_quarter(collect(mine, their, gw, info, codes, shapes, blocks, True)))[-1]
            parts = [(a.astype(f32) + b.astype(f32)).astype(bf16) for a, b in zip(parts, [sums] + quarters_to([sums] * 3))]
            return i + 1, [queue[k] for k in far], lo, lof, [back[k] for k in far], parts

        carry = (jnp.int32(0), [queue[k] for k in far], lo, lof, [back[k] for k in far], parts)
        _, _, lo, _, backs, parts = lax.while_loop(lambda c: c[0] < left, more, carry)
    else:
        backs = [back[k] for k in far]
    direction_grad, gain_grad, bias_grad, code_grad, running_mean, running_var = finish(
        AXES, span, categories, momentum, parts, direction, gain, norms, weight, prev_mean, prev_var)
    input_grad = unpack(mine, their, rows_far, lasts, usual, [got[k, t] for k in far for t in lasts], part, backs)
    return (
        lo,
        input_grad,
        code_grad[:span, HID : HID + code_width],
        direction_grad,
        gain_grad[0],
        bias_grad[0],
        running_mean,
        running_var,
    )


def solution(mesh):
    both = P(("shape", "oct"), None)
    in_specs = (both, P(("shape", "oct")), both, P(), P("shape", None), P(), P(), P(), both, P(), P(), P())
    out_specs = (both, both, P("shape", None), P(), P(), P(), P(), P())
    return jax.shard_map(body, mesh=mesh, in_specs=in_specs, out_specs=out_specs, check_vma=False)
```

```python
import functools

import jax
import jax.numpy as jnp
from jax import lax
from jax.experimental import pallas as pl
from jax.experimental.pallas import tpu as pltpu
from jax.sharding import PartitionSpec as P

HID = 253
CATS = 5
BLOCK = 256
TILE = 256
UNIT = 2 * TILE
WIN = BLOCK + 16
LEAD = 4
USUAL = 7
STEPS = 11
FAR = 1 << 20

norm_eps = 1e-06
COSTS = dict(pack=30, prepare=30, local=30, unlocal=0.01, names=30, far=30, last=0.01, flush=0.01, unpack=30, merge=0.01, finish=30, collect=0.01)


def cost(name):
    return pl.CostEstimate(flops=max(1, int(COSTS[name] * 10**9)), bytes_accessed=1, transcendentals=0)


f32, bf16, i32 = jnp.float32, jnp.bfloat16, jnp.int32


def params(mib):
    return pltpu.CompilerParams(vmem_limit_bytes=mib * 1024 * 1024)


def keep(x):
    return pltpu.with_memory_space_constraint(x, pltpu.VMEM)


def stay(x):
    return pltpu.with_memory_space_constraint(x, pltpu.HBM)


def specs(text):
    kinds = {"v": pltpu.VMEM, "s": pltpu.SMEM, "a": pl.ANY}
    return [pl.BlockSpec(memory_space=kinds[c]) for c in text]


def iota(shape, dim):
    return lax.broadcasted_iota(i32, shape, dim)


def units(tiles):
    return (tiles + 1) // 2


def plan_messages(usual, steps):
    tail = [c for c in range(usual, steps, 2)]
    cuts = list(range(0, usual, 2)) + tail + [steps]
    return [(a, b - a) for a, b in zip(cuts, cuts[1:])]


def ceil_to(n, step):
    return -(-n // step) * step


def plan(labels, groups, span):
    rows = labels.shape[0]
    count = len(groups)
    mask = jnp.concatenate([(labels >= g * span) & (labels < (g + 1) * span) for g in groups], axis=0)
    one = jnp.where(mask, 1.0, 0.0)
    m = one.astype(bf16)
    total = count * rows
    upper = jnp.where(iota((BLOCK, BLOCK), 0) <= iota((BLOCK, BLOCK), 1), 1.0, 0.0).astype(bf16)
    cum = jnp.dot(m, upper, preferred_element_type=f32)
    a, b = iota((total, total), 0), iota((total, total), 1)
    lower = jnp.where((a // rows == b // rows) & (b < a), 1.0, 0.0).astype(bf16)
    tot = jnp.sum(one, axis=1, keepdims=True)
    base = jnp.dot(lower, jnp.broadcast_to(tot, (total, 128)).astype(bf16), preferred_element_type=f32)[:, :1]
    lo, hi = base.astype(i32), (base + tot).astype(i32)
    pos = jnp.where(mask, lo + cum.astype(i32) - 1, -FAR)
    tot_row = lax.dot_general(jnp.ones((8, BLOCK), bf16), m, (((1,), (1,)), ((), ())), preferred_element_type=f32)
    base_row = lax.dot_general(tot_row.astype(bf16), lower, (((1,), (1,)), ((), ())), preferred_element_type=f32)
    return pos, lo, hi, base_row.astype(i32), (base_row + tot_row).astype(i32)


def sorted_rows(pos, lo, hi, rows, first, count):
    row, at = None, 0
    for n in range(first, first + count):
        s = slice(n * rows, (n + 1) * rows)
        start = lo[s] // 16 * 16
        r = pos[s] + (at - start)
        row = r if row is None else jnp.maximum(row, r)
        at = at + (hi[s] + 15) // 16 * 16 - start
    return row


def squeeze(pos, labels, group, span):
    rows, lanes = pos.shape
    at = iota((rows, lanes), 0) * lanes + iota((rows, lanes), 1)
    v = jnp.where(pos >= 0, (at - pos) * 16 + (labels - group * span + 1), 0)
    for bit in range((rows * lanes).bit_length() - 1):
        step = 1 << bit
        go = jnp.where(((v >> (4 + bit)) & 1) == 1, v, 0)
        if step < lanes:
            moved = pltpu.roll(go, lanes - step, 1)
            moved = jnp.where(iota((rows, lanes), 1) < lanes - step, moved, pltpu.roll(moved, rows - 1, 0))
        else:
            moved = pltpu.roll(go, rows - step // lanes, 0)
        v = v - go + moved
    return v & 15


def tiles_of(bounds, group, blocks, row=1):
    return (bounds[row, (group + 1) * blocks - 1] + TILE - 1) // TILE


def spans(bounds, groups, blocks, b):
    at, result = 0, []
    for g in groups:
        lo, hi = bounds[0, g * blocks + b], bounds[1, g * blocks + b]
        first = pl.multiple_of(lo // 16 * 16, 16)
        result.append((first, pl.multiple_of(at, 16) if result else 0, lo - first))
        at = at + ((hi + 15) // 16 * 16 - first)
    return result


def window_rows(count, step):
    return ceil_to(BLOCK + 30 * count, step)


def sort_rows(bounds, row_ref, x_ref, groups, blocks, moved, put):
    rows = window_rows(len(groups), 64)
    for b in range(blocks):
        hot = jnp.where(iota((rows, BLOCK), 0) == row_ref[b : b + 1, :], 1.0, 0.0).astype(bf16)
        out = jnp.dot(hot, x_ref[b * BLOCK : (b + 1) * BLOCK, :], preferred_element_type=f32).astype(bf16)
        moved[b * rows : (b + 1) * rows, :] = out
    moved[blocks * rows :, :] = jnp.zeros((moved.shape[0] - blocks * rows, moved.shape[1]), bf16)
    for n in range(len(groups)):
        for b in range(blocks):
            first, at, over = spans(bounds, groups, blocks, b)[n]
            dst, start = put(n, first)
            at = at + b * rows
            old = dst[pl.ds(start, 16), :]
            new = moved[pl.ds(pl.multiple_of(at, 16), 16), :]
            dst[pl.ds(start, 16), :] = jnp.where(iota((16, 1), 0) < over, old, new)
            rest = pl.ds(pl.multiple_of(start + 16, 16), BLOCK)
            dst[rest, :] = moved[pl.ds(pl.multiple_of(at + 16, 16), BLOCK), :]


def unsort_rows(bounds, row_ref, groups, blocks, pick, moved, emit):
    rows = window_rows(len(groups), 128)
    for b in range(blocks):
        moved[b * rows + WIN : (b + 1) * rows, :] = jnp.zeros((rows - WIN, moved.shape[1]), bf16)
        for n, (first, at, _) in enumerate(spans(bounds, groups, blocks, b)):
            moved[pl.ds(pl.multiple_of(at + b * rows, 16), WIN), :] = pick(n, first, WIN)
    for b in range(blocks):
        hot = jnp.where(iota((rows, BLOCK), 0) == row_ref[b : b + 1, :], 1.0, 0.0).astype(bf16)
        emit(b, jnp.dot(jnp.transpose(hot), moved[b * rows : (b + 1) * rows, :], preferred_element_type=f32))


def layer_tile(x, named, ct, wp_ref, wpt_ref, cb_ref, gw_ref, span):
    rows = x.shape[0]
    col = jnp.transpose(jnp.broadcast_to(named.astype(f32), (8, rows)))[:, :1]
    pre = jnp.dot(x, wp_ref[...], preferred_element_type=f32)
    add = cb_ref[0:1, :]
    for s in range(1, span):
        add = jnp.where(col == s + 1.0, cb_ref[s : s + 1, :], add)
    pre = pre + add
    valid = col > 0.0
    e = jnp.exp(-jnp.abs(pre))
    u = 1.0 + e
    r = 1.0 / u
    soft = jnp.maximum(pre, 0.0) + jnp.where(e < 2.0**-12, e, jnp.log(u))
    sig = jnp.where(pre >= 0.0, r, e * r)
    lo = jnp.where(valid, soft, 0.0).astype(bf16)
    gp = jnp.where(valid, ct.astype(f32) * sig, 0.0).astype(bf16)
    gx = jnp.dot(gp, wpt_ref[...], preferred_element_type=f32).astype(bf16)
    sel = jnp.where(jnp.broadcast_to(named, (16, rows)) == iota((16, rows), 0) + 1, 1.0, 0.0).astype(bf16)
    left = jnp.concatenate([jnp.transpose(x), sel], axis=0)
    gw_ref[...] += jnp.dot(left, gp, preferred_element_type=f32)
    return lo, gx


def pack_kernel(oct_count, sizes, shape_axis, oct_axis, span, cap, octants_hbm, ids_hbm, x_hbm, ct_hbm, *refs):
    far = oct_count // 2 - 1
    octants_ref, ids_ref, in_sem, ct_sem = refs[-4:]
    refs = refs[:-4]
    ct_near, ct_far, x_ref, refs = *refs[:3], refs[3:]
    other = lax.axis_index(oct_axis) ^ 1
    blocks_out = []
    for k in range(oct_count // 2):
        there = ct_hbm.at[pl.ds(pl.multiple_of((other ^ (2 * k)) * cap, cap), cap), :]
        here = ct_far.at[pl.ds((k - 1) * cap, cap), :] if k else ct_near
        blocks_out.append(pltpu.make_async_copy(there, here, ct_sem.at[k]))
    fetches = [
        pltpu.make_async_copy(a, b, in_sem.at[i])
        for i, (a, b) in enumerate(zip((octants_hbm, ids_hbm, x_hbm), (octants_ref, ids_ref, x_ref)))
    ]
    for f in fetches + blocks_out:
        f.start()
    heads, refs = refs[: 2 * far], refs[2 * far :]
    queues, rows_far, refs = refs[:far], refs[far : 2 * far], refs[2 * far :]
    row_near, bounds_ref, names_ref, info_ref, moved, bounds_v, bounds, sem = refs
    blocks = row_near.shape[0]
    me = lax.axis_index(oct_axis)
    first_shape = lax.axis_index(shape_axis) * span

    def wide(ref):
        return jnp.concatenate([ref[pl.ds(h, blocks, 2), :] for h in range(2)], axis=1)

    for f in fetches[:2]:
        f.wait()
    ids = wide(ids_ref) - first_shape
    labels = (wide(octants_ref) ^ me) * span + ids
    pos, lo, hi, first_row, last_row = plan(labels, range(oct_count), span)
    n = oct_count * blocks
    bounds_v[...] = jnp.zeros(bounds_v.shape, i32)
    bounds_v[0:1, :n] = first_row[:1]
    bounds_v[1:2, :n] = last_row[:1]
    bounds_ref[...] = bounds_v[...]
    copy = pltpu.make_async_copy(bounds_v, bounds, sem)
    copy.start()
    row_near[...] = sorted_rows(pos, lo, hi, blocks, 0, 2)
    for k in range(far):
        rows_far[k][...] = sorted_rows(pos, lo, hi, blocks, 2 + 2 * k, 2)
    tiles = cap // TILE
    names_ref[...] = jnp.zeros(names_ref.shape, i32)
    for g in range(2):
        names_ref[g * 8 : g * 8 + tiles, :] = squeeze(pos[g * blocks : (g + 1) * blocks], labels, g, span)[:tiles]

    info_ref[...] = jnp.zeros(info_ref.shape, f32)
    for s in range(span):
        number = jnp.sum(jnp.sum(jnp.where(ids == s, 1.0, 0.0), axis=1, keepdims=True), axis=0, keepdims=True)
        info_ref[s : s + 1, :] = jnp.broadcast_to(number, (1, 128))

    for k in range(far):
        queues[k][...] = jnp.zeros(queues[k].shape, bf16)
    copy.wait()
    fetches[2].wait()
    for k in range(far):
        groups = [2 + 2 * k, 3 + 2 * k]
        cut = tiles_of(bounds, groups[0], blocks) * TILE
        sort_rows(bounds, rows_far[k], x_ref, groups, blocks, moved,
                  lambda n, first: (queues[k], pl.multiple_of(first + n * cut, 16)))
        heads[2 * k][: sizes[0], :] = queues[k][: sizes[0], :]
        heads[2 * k][sizes[0] :, :] = labels.astype(f32).astype(bf16)
        heads[2 * k + 1][...] = queues[k][sizes[0] : sizes[0] + sizes[1], :]
    for f in blocks_out:
        f.wait()


def pack(octants, ids, points, cotangent, messages, oct_count, span, cap):
    count, width = points.shape
    blocks = count // BLOCK
    far = oct_count // 2 - 1
    shape = jax.ShapeDtypeStruct
    sizes = [n * UNIT for _, n in messages[:2]]
    heads = [pltpu.VMEM((sizes[0] + blocks, width), bf16), pltpu.VMEM((sizes[1], width), bf16)] * far
    cols = cotangent.shape[1]
    outs = [pltpu.VMEM((cap, cols), bf16), pltpu.VMEM((far * cap, cols), bf16), pltpu.VMEM(points.shape, bf16)] + heads + [pltpu.VMEM((4 * cap, width), bf16)] * far
    outs += [shape((blocks, BLOCK), i32)] * (far + 1)
    outs += [shape((8, 128), i32), shape((16, BLOCK), i32), shape((8, 128), f32)]
    out = pl.pallas_call(
        functools.partial(pack_kernel, oct_count, sizes, "shape", "oct", span, cap),
        in_specs=specs("aaaa"),
        out_specs=specs("v" * len(outs)),
        out_shape=outs,
        scratch_shapes=[
            pltpu.VMEM((blocks * window_rows(2, 64) + WIN, width), bf16),
            pltpu.VMEM((8, 128), i32),
            pltpu.SMEM((8, 128), i32),
            pltpu.SemaphoreType.DMA,
            pltpu.VMEM((count // 128, 128), i32),
            pltpu.VMEM((count // 128, 128), i32),
            pltpu.SemaphoreType.DMA((3,)),
            pltpu.SemaphoreType.DMA((oct_count // 2,)),
        ],
        compiler_params=params(16),
        cost_estimate=cost("pack"),
        name="pack",
    )(stay(octants.reshape(-1, 128)), stay(ids.reshape(-1, 128)), stay(points), stay(cotangent))
    x, out = out[:3], out[3:]
    heads, queues, rows_far, out = out[: 2 * far], out[2 * far : 3 * far], out[3 * far : 4 * far], out[4 * far :]
    return x, heads, queues, rows_far, out


def set_weights(hid, direction_ref, gain_ref, bias_ref, codes_ref, wp_ref, wpt_ref, w_ref, cb_ref, norm_ref):
    direction = direction_ref[...]
    norms = jnp.sqrt(jnp.sum(direction * direction, axis=0, keepdims=True) + norm_eps)
    weight = (direction * (gain_ref[...] / norms)).astype(bf16)
    norm_ref[...] = norms
    w_ref[...] = weight
    width = wp_ref.shape[0]
    wf = weight.astype(f32)
    last = jnp.where(iota((8, 1), 0) + (width - 8) < hid, wf[width - 8 : width, :], wf[-8:, :])
    wp = jnp.concatenate([wf[: width - 8, :], last], axis=0)
    wp_ref[...] = wp.astype(bf16)
    wpt_ref[...] = wp.T.astype(bf16)
    span, code_width = codes_ref.shape
    w_code = wf[hid : hid + code_width, :].astype(bf16)
    codes = jnp.concatenate([codes_ref[...].astype(f32), jnp.zeros((8 - span, code_width), f32)], axis=0).astype(bf16)
    cb_ref[...] = jnp.dot(codes, w_code, preferred_element_type=f32) + bias_ref[...]


def prepare_kernel(oct_count, oct_axis, cap, bounds, row_ref, x_ref, codes_v, direction_hbm, gain_hbm, bias_hbm,
                   lo_hbm, lon_hbm, gw_ref, buf, wp_ref, wpt_ref, w_ref, cb_ref, norm_ref, direction_v, gain_v,
                   moved, zero, bias_v, zero_sem, in_sem):
    blocks = row_ref.shape[0]
    tiles = cap // TILE
    source = lax.axis_index(oct_axis)
    cut = [tiles_of(bounds, r, blocks) for r in range(2)]
    fetches = [
        pltpu.make_async_copy(a, b, in_sem.at[i])
        for i, (a, b) in enumerate(((direction_hbm, direction_v), (gain_hbm, gain_v), (bias_hbm, bias_v)))
    ]
    for f in fetches:
        f.start()

    def clear(go):
        for t in range(tiles):
            @pl.when(t >= cut[0])
            def _():
                at = source * cap + t * TILE
                go(pltpu.make_async_copy(zero, lo_hbm.at[pl.ds(pl.multiple_of(at, TILE), TILE), :], zero_sem))

            @pl.when(t >= cut[1])
            def _():
                go(pltpu.make_async_copy(zero, lon_hbm.at[pl.ds(t * TILE, TILE), :], zero_sem))

    zero[...] = jnp.zeros(zero.shape, bf16)
    clear(lambda c: c.start())
    gw_ref[...] = jnp.zeros(gw_ref.shape, f32)
    buf[...] = jnp.zeros(buf.shape, bf16)
    sort_rows(bounds, row_ref, x_ref, [0, 1], blocks, moved,
              lambda n, first: (buf, pl.multiple_of(first + n * cut[0] * TILE, 16)))
    for f in fetches:
        f.wait()
    set_weights(HID, direction_v, gain_v, bias_v, codes_v, wp_ref, wpt_ref, w_ref, cb_ref, norm_ref)
    clear(lambda c: c.wait())


def prepare(bounds, row, points, direction, gain, bias, codes, oct_count, cap):
    width = points.shape[1]
    ins, outs = direction.shape
    blocks = row.shape[0]
    return pl.pallas_call(
        functools.partial(prepare_kernel, oct_count, "oct", cap),
        in_specs=specs("svvvaaa"),
        out_specs=specs("aavvvvvvvvv"),
        out_shape=[
            pltpu.HBM((oct_count * cap, outs), bf16),
            pltpu.HBM((cap, outs), bf16),
            pltpu.VMEM((width + 16, outs), f32),
            pltpu.VMEM((2 * cap + BLOCK + WIN, width), bf16),
            pltpu.VMEM((width, outs), bf16),
            pltpu.VMEM((outs, width), bf16),
            pltpu.VMEM((ins, outs), bf16),
            pltpu.VMEM((8, outs), f32),
            pltpu.VMEM((1, outs), f32),
            pltpu.VMEM((ins, outs), f32),
            pltpu.VMEM((1, outs), f32),
        ],
        scratch_shapes=[
            pltpu.VMEM((blocks * window_rows(2, 64) + WIN, width), bf16),
            pltpu.VMEM((TILE, outs), bf16),
            pltpu.VMEM((1, outs), f32),
            pltpu.SemaphoreType.DMA,
            pltpu.SemaphoreType.DMA((3,)),
        ],
        compiler_params=params(14),
        cost_estimate=cost("prepare"),
        name="prepare",
    )(bounds, row, keep(points), codes, stay(direction), stay(gain[None, :]), stay(bias[None, :]))


class Rows:
    def __init__(self, bounds, cut, source, cap, place):
        self.cut, self.source, self.cap, self.place = cut, source, cap, place
        self.count = cut[0] + cut[1]

    def split(self, unit, i):
        t = unit * 2 + i
        second = (t >= self.cut[0]).astype(i32)
        return t, second, t - second * self.cut[0]

    def live(self, unit):
        return unit * 2 < self.count

    def move(self, unit, own, other, other_at, mine, mine_at, sem, out, go):
        for i in range(2):
            t, second, slot = self.split(unit, i)
            here = mine.at[pl.ds(mine_at + i * TILE, TILE), :]

            def one(array, row):
                there = array.at[pl.ds(pl.multiple_of(row + slot * TILE, TILE), TILE), :]
                go(pltpu.make_async_copy(here, there, sem) if out else pltpu.make_async_copy(there, here, sem))

            @pl.when((t < self.count) & (second == 0))
            def _():
                one(own, self.source * self.cap)

            @pl.when((t < self.count) & (second == 1))
            def _():
                one(other, other_at)

    def fetch(self, unit, ct, ctx, mine, at, sem, go):
        self.move(unit, ct, ctx, self.place * self.cap, mine, at, sem, False, go)

    def store(self, unit, lo, lox, mine, at, sem, go):
        self.move(unit, lo, lox, self.place * self.cap, mine, at, sem, True, go)

    def names(self, unit, names_ref):
        rows = []
        for i in range(2):
            t, second, slot = self.split(unit, i)
            row = names_ref[pl.ds(jnp.minimum(second * 8 + slot, names_ref.shape[0] - 1), 1), :]
            rows.append(jnp.where(t < self.count, row, 0))
        return jnp.concatenate(rows, axis=1)


def go_start(copy):
    copy.start()


def go_wait(copy):
    copy.wait()


def local_kernel(oct_axis, far, blocks, span, cap, bounds, *refs):
    names_ref, ct_hbm, ctx_ref, wp_ref, wpt_ref, cb_ref, lo_in, lon_in, gw_in, buf_in, refs = *refs[:10], refs[10:]
    lo_hbm, lon_hbm, lof_hbm, gw_ref, buf, refs = *refs[:5], refs[5:]
    ct_v, lo_v, zero, ct_sem, lo_sem, zero_sem = refs
    source = lax.axis_index(oct_axis)
    near = Rows(bounds, [tiles_of(bounds, r, blocks) for r in range(2)], source, cap, 0)
    count = units(near.count)

    def clear(go):
        for k in range(1, far + 1):
            for t in range(cap // TILE):
                at = (source ^ (2 * k)) * cap + t * TILE
                go(pltpu.make_async_copy(zero, lo_hbm.at[pl.ds(pl.multiple_of(at, TILE), TILE), :], zero_sem))
        for t in range(lof_hbm.shape[0] // TILE):
            go(pltpu.make_async_copy(zero, lof_hbm.at[pl.ds(t * TILE, TILE), :], zero_sem))

    @pl.when(count > 0)
    def _():
        near.fetch(0, ct_hbm, ctx_ref, ct_v.at[0], 0, ct_sem.at[0], go_start)

    zero[...] = jnp.zeros(zero.shape, bf16)
    clear(go_start)

    def step(i, carry):
        slot = i % 2

        @pl.when(i + 1 < count)
        def _():
            near.fetch(i + 1, ct_hbm, ctx_ref, ct_v.at[1 - slot], 0, ct_sem.at[1 - slot], go_start)

        near.fetch(i, ct_hbm, ctx_ref, ct_v.at[slot], 0, ct_sem.at[slot], go_wait)

        @pl.when(i >= 2)
        def _():
            near.store(i - 2, lo_hbm, lon_hbm, lo_v.at[slot], 0, lo_sem.at[slot], go_wait)

        at = pl.ds(pl.multiple_of(i * UNIT, UNIT), UNIT)
        lo, gx = layer_tile(buf[at, :], near.names(i, names_ref), ct_v[slot], wp_ref, wpt_ref, cb_ref, gw_ref, span)
        lo_v[slot] = lo
        buf[at, :] = gx
        near.store(i, lo_hbm, lon_hbm, lo_v.at[slot], 0, lo_sem.at[slot], go_start)
        return carry

    lax.fori_loop(0, count, step, 0)
    for back in (2, 1):
        @pl.when(count >= back)
        def _():
            slot = (count - back) % 2
            near.store(count - back, lo_hbm, lon_hbm, lo_v.at[slot], 0, lo_sem.at[slot], go_wait)

    clear(go_wait)


def local(bounds, names, cotangent, ctx, weights, lo, lon, gw, buf, far, blocks, span, cap):
    outs = lo.shape[1]
    return pl.pallas_call(
        functools.partial(local_kernel, "oct", far, blocks, span, cap),
        in_specs=specs("svavvvvaavv"),
        out_specs=specs("aaavv"),
        out_shape=[pltpu.HBM(lo.shape, bf16), pltpu.HBM(lon.shape, bf16), pltpu.HBM((far * cap, outs), bf16),
                   pltpu.VMEM(gw.shape, f32), pltpu.VMEM(buf.shape, bf16)],
        input_output_aliases={7: 0, 8: 1, 9: 3, 10: 4},
        scratch_shapes=[
            pltpu.VMEM((2, UNIT, outs), bf16),
            pltpu.VMEM((2, UNIT, outs), bf16),
            pltpu.VMEM((TILE, outs), bf16),
            pltpu.SemaphoreType.DMA((2,)),
            pltpu.SemaphoreType.DMA((2,)),
            pltpu.SemaphoreType.DMA,
        ],
        compiler_params=params(12),
        cost_estimate=cost("local"),
        name="local",
    )(bounds, names, stay(cotangent), keep(ctx), *[keep(w) for w in weights], stay(lo), stay(lon), keep(gw), keep(buf))


def unlocal_kernel(oct_axis, cap, bounds, row_ref, gbuf, lon_ref, lo_in, part_ref, lo_hbm, moved, sem):
    blocks = row_ref.shape[0]
    join(cap, [0], oct_axis, lon_ref, lo_hbm, sem, go_start)

    def emit(b, rows):
        part_ref[b * BLOCK : (b + 1) * BLOCK, :] = rows.astype(bf16)

    cut = tiles_of(bounds, 0, blocks) * TILE
    unsort_rows(bounds, row_ref, [0, 1], blocks,
                lambda n, first, rows: gbuf[pl.ds(pl.multiple_of(first + n * cut, 16), rows), :], moved, emit)
    join(cap, [0], oct_axis, lon_ref, lo_hbm, sem, go_wait)


def unlocal(bounds, row, gbuf, lon, lo, cap):
    blocks, width = row.shape[0], gbuf.shape[1]
    return pl.pallas_call(
        functools.partial(unlocal_kernel, "oct", cap),
        in_specs=specs("svvva"),
        out_specs=specs("va"),
        out_shape=[pltpu.VMEM((blocks * BLOCK, width), bf16), pltpu.HBM(lo.shape, bf16)],
        input_output_aliases={4: 1},
        scratch_shapes=[pltpu.VMEM((blocks * window_rows(2, 128) + WIN, width), bf16), pltpu.SemaphoreType.DMA((1,))],
        compiler_params=params(16),
        cost_estimate=cost("unlocal"),
        name="unlocal",
    )(bounds, row, keep(gbuf), keep(lon), stay(lo))


def names_kernel(kx, span, cap, labels_ref, names_ref, count_ref, back_ref):
    labels = labels_ref[...].astype(f32).astype(i32)
    blocks = labels.shape[0]
    groups = [2 * kx, 2 * kx + 1]
    pos, _, _, _, last = plan(labels, groups, span)
    tiles = cap // TILE
    names_ref[...] = jnp.zeros(names_ref.shape, i32)
    for n, g in enumerate(groups):
        names_ref[n * 8 : n * 8 + tiles, :] = squeeze(pos[n * blocks : (n + 1) * blocks], labels, g, span)[:tiles]
    count_ref[...] = jnp.zeros(count_ref.shape, i32)
    count_ref[0:1, : 2 * blocks] = last[:1]
    back_ref[...] = jnp.zeros(back_ref.shape, bf16)


def make_names(labels, kx, span, cap):
    return pl.pallas_call(
        functools.partial(names_kernel, kx, span, cap),
        in_specs=specs("v"),
        out_specs=specs("vvv"),
        out_shape=[
            jax.ShapeDtypeStruct((16, BLOCK), i32),
            jax.ShapeDtypeStruct((8, 128), i32),
            pltpu.VMEM((2 * cap + UNIT, labels.shape[1]), bf16),
        ],
        compiler_params=params(8),
        cost_estimate=cost("names"),
        name="names",
    )(labels)


def lead_of(tiles):
    return jnp.maximum(units(tiles), LEAD)


def take_back(place, theirs, blocks, x_ref, at, back):
    n = place - lead_of(tiles_of(theirs, 0, blocks, 0) + tiles_of(theirs, 1, blocks, 0))

    @pl.when((n >= 0) & (n < back.shape[0] // UNIT - 1))
    def _():
        back[pl.ds(pl.multiple_of(n * UNIT, UNIT), UNIT), :] = x_ref[at : at + UNIT, :]


def far_kernel(message, before, after_it, emits, kx, oct_axis, blocks, span, cap, mine, theirs, *refs):
    names_ref, x_ref, ct_hbm, ctx_ref, wp_ref, wpt_ref, cb_ref, queue_in, lo_in, lof_in, gw_in, back_in, refs = *refs[:12], refs[12:]
    if before:
        ct_v, lo_old, refs = *refs[:2], refs[2:]
    queue, lo_hbm, lof_hbm, gw_ref, back, refs = *refs[:5], refs[5:]
    payloads, refs = refs[: len(emits)], refs[len(emits) :]
    if after_it:
        ct_new, refs = refs[0], refs[1:]
    lo_v, refs = refs[0], refs[1:]
    if not before:
        ct_v, refs = refs[0], refs[1:]
    ct_sem, new_sem, lo_sem = refs
    first, number = message
    source = lax.axis_index(oct_axis) ^ (2 * kx)
    rows = Rows(theirs, [tiles_of(theirs, r, blocks, 0) for r in range(2)], source, cap, kx - 1)
    lead = lead_of(tiles_of(mine, 2 * kx, blocks) + tiles_of(mine, 2 * kx + 1, blocks))

    def fetch(u, go):
        if not before:
            rows.fetch(first + u, ct_hbm, ctx_ref, ct_v, u * UNIT, ct_sem.at[u], go)

    def ahead(go):
        if before:
            for u in range(before[1]):
                rows.store(before[0] + u, lo_hbm, lof_hbm, lo_old, u * UNIT, lo_sem, go)
        if after_it:
            for u in range(after_it[1]):
                rows.fetch(after_it[0] + u, ct_hbm, ctx_ref, ct_new, u * UNIT, new_sem, go)

    for u in range(number):
        fetch(u, go_start)
    ahead(go_start)
    for u in range(number):
        take_back(first + u, theirs, blocks, x_ref, u * UNIT, back)
        fetch(u, go_wait)

        @pl.when(rows.live(first + u))
        def _():
            at = slice(u * UNIT, (u + 1) * UNIT)
            lo, gx = layer_tile(x_ref[at, :], rows.names(first + u, names_ref), ct_v[at, :], wp_ref, wpt_ref, cb_ref, gw_ref, span)
            lo_v[at, :] = lo
            queue[pl.ds(pl.multiple_of((lead + first + u) * UNIT, UNIT), UNIT), :] = gx

    for payload, (place, count) in zip(payloads, emits):
        payload[...] = queue[place * UNIT : (place + count) * UNIT, :]
    ahead(go_wait)


def far_step(messages, m, points_in, kx, mine, theirs, names, x, cotangent, ctx, weights, state, ahead, blocks, span, cap):
    wp, wpt, cb = weights
    queue, lo, lof, gw, back = state
    width, outs = wp.shape
    last = points_in[-1] == m
    message, before, after_it = messages[m], (messages[m - 1] if m > 0 else None), (None if last else messages[m + 1])
    emits = messages[m + 2 :] if last else [messages[m + 2]]
    own = (message[1] * UNIT, outs)
    shapes = [pltpu.VMEM(queue.shape, bf16), pltpu.HBM(lo.shape, bf16), pltpu.HBM(lof.shape, bf16), pltpu.VMEM(gw.shape, f32),
              pltpu.VMEM(back.shape, bf16)] + [pltpu.VMEM((count * UNIT, width), bf16) for _, count in emits]
    if after_it:
        shapes.append(pltpu.VMEM((after_it[1] * UNIT, outs), bf16))
    shapes.append(pltpu.VMEM(own, bf16))
    args = [mine, theirs, names, keep(x), stay(cotangent), keep(ctx), keep(wp), keep(wpt), keep(cb), keep(queue), stay(lo),
            stay(lof), keep(gw), keep(back)] + [keep(a) for a in ahead]
    out = pl.pallas_call(
        functools.partial(far_kernel, message, before, after_it, emits, kx, "oct", blocks, span, cap),
        in_specs=specs("ssvvavvvvvaavv" + "v" * len(ahead)),
        out_specs=specs("vaavv" + "v" * (len(shapes) - 5)),
        out_shape=shapes,
        input_output_aliases={9 + i: i for i in range(5)},
        scratch_shapes=([] if before else [pltpu.VMEM(own, bf16)])
        + [pltpu.SemaphoreType.DMA((message[1],)), pltpu.SemaphoreType.DMA, pltpu.SemaphoreType.DMA],
        compiler_params=params(12),
        cost_estimate=cost("last" if last else "far"),
        name="far",
    )(*args)
    return tuple(out[:5]), out[5 : 5 + len(emits)], tuple(out[5 + len(emits) :])


def unpack_kernel(far, blocks, lasts, bounds, *refs):
    theirs, rows_far, refs = refs[:far], refs[far : 2 * far], refs[2 * far :]
    parts, refs = refs[: far * len(lasts)], refs[far * len(lasts) :]
    part_ref, refs = refs[0], refs[1 + far :]
    out_ref, backs, moved = refs[0], refs[1 : 1 + far], refs[-1]
    for k in range(far):
        for j, (first, number) in enumerate(lasts):
            for u in range(number):
                take_back(first + u, theirs[k], blocks, parts[k * len(lasts) + j], u * UNIT, backs[k])
        cut = tiles_of(bounds, 2 + 2 * k, blocks) * TILE

        def pick(n, first, count):
            return backs[k][pl.ds(pl.multiple_of(first + n * cut, 16), count), :]

        def emit(b, value):
            at = slice(b * BLOCK, (b + 1) * BLOCK)
            before = part_ref if k == 0 else out_ref
            out_ref[at, :] = (value + before[at, :].astype(f32)).astype(bf16)

        unsort_rows(bounds, rows_far[k], [2 + 2 * k, 3 + 2 * k], blocks, pick, moved, emit)


def unpack(bounds, theirs, rows_far, lasts, parts, part, backs):
    points, width = part.shape
    blocks = points // BLOCK
    far = len(theirs)
    extra = far * len(lasts)
    return pl.pallas_call(
        functools.partial(unpack_kernel, far, blocks, lasts),
        in_specs=specs("s" + "s" * far + "v" * (2 * far + extra + 1)),
        out_specs=specs("v" * (1 + far)),
        out_shape=[jax.ShapeDtypeStruct(part.shape, bf16)] + [pltpu.VMEM(b.shape, bf16) for b in backs],
        input_output_aliases={2 * far + extra + 2 + k: 1 + k for k in range(far)},
        scratch_shapes=[pltpu.VMEM((blocks * window_rows(2, 128) + WIN, width), bf16)],
        compiler_params=params(20),
        cost_estimate=cost("unpack"),
        name="unpack",
    )(bounds, *theirs, *rows_far, *[keep(x) for x in parts], keep(part), *[keep(b) for b in backs])[0]


def join(cap, kxs, oct_axis, lox_ref, lo_hbm, sem, go):
    other = lax.axis_index(oct_axis) ^ 1
    for n, k in enumerate(kxs):
        at = pl.ds(pl.multiple_of((other ^ (2 * k)) * cap, cap), cap)
        go(pltpu.make_async_copy(lox_ref.at[pl.ds(n * cap, cap), :], lo_hbm.at[at, :], sem.at[n]))


def column_block(axes, n):
    a, b = (lax.axis_index(axis) % 2 for axis in axes)
    return (a ^ (n % 2)) * 2 + (b ^ (n // 2))


def collect_kernel(axes, shape_axis, oct_axis, shapes, span, extra, blocks, cap, message, usual, steps, *refs):
    mine, refs = refs[0], refs[1:]
    theirs, olds, refs = refs[:extra], refs[extra : 2 * extra], refs[2 * extra :]
    gw_ref, info_ref, codes_ref, lo_in, lof_in, outs, lo_hbm, lof_hbm, full, sem = *refs[:5], refs[5:9], *refs[9:]
    source = lax.axis_index(oct_axis)

    def store(go):
        for k in range(extra):
            rows = Rows(theirs[k], [tiles_of(theirs[k], r, blocks, 0) for r in range(2)], source ^ (2 * k + 2), cap, k)
            for u in range(message[1]):
                rows.store(message[0] + u, lo_hbm, lof_hbm, olds[k], u * UNIT, sem, go)

    store(go_start)
    width = gw_ref.shape[0] - 16
    cols = gw_ref.shape[1]
    code_width = codes_ref.shape[1]
    base = lax.axis_index(shape_axis) * span
    full[:width, :] = gw_ref[:width, :]
    ps = jnp.zeros((shapes, cols), f32)
    for s in range(span):
        ps = ps + jnp.where(iota((shapes, 1), 0) == base + s, gw_ref[width + s : width + s + 1, :], 0.0)
    full[width : width + shapes, :] = ps
    lane = iota((1, cols - code_width), 1)
    info = jnp.zeros((shapes, cols), f32)
    for s in range(span):
        number = info_ref[s : s + 1, :1]
        high = jnp.floor(number / 1024.0)
        mid = jnp.floor((number - 1024.0 * high) / 32.0)
        low = number - 1024.0 * high - 32.0 * mid
        digits = jnp.where(lane < 64, low, jnp.where(lane < 128, mid, high))
        code = jnp.where(lax.axis_index(oct_axis) == 0, codes_ref[s : s + 1, :].astype(f32), 0.0)
        info = info + jnp.where(iota((shapes, 1), 0) == base + s, jnp.concatenate([code, digits], axis=1), 0.0)
    full[width + shapes : width + 2 * shapes, :] = info
    flag = jnp.int32(0)
    for k in range(extra):
        ours = units(tiles_of(mine, 2 + 2 * k, blocks) + tiles_of(mine, 3 + 2 * k, blocks))
        other = units(tiles_of(theirs[k], 0, blocks, 0) + tiles_of(theirs[k], 1, blocks, 0))
        most = jnp.maximum(jnp.maximum(ours, LEAD) + other, jnp.maximum(other, LEAD) + ours)
        flag = flag | ((jnp.maximum(ours, other) > usual) | (most > steps)).astype(i32)
    full[width + 2 * shapes :, :] = jnp.zeros((16, cols), f32) + flag.astype(f32)
    for n in range(4):
        at = pl.ds(pl.multiple_of(column_block(axes, n) * 128, 128), 128)
        outs[n][...] = full[:, at].astype(bf16)
    store(go_wait)


def halves(x):
    high = x.astype(bf16)
    return high, (x - high.astype(f32)).astype(bf16)


def finish_kernel(axes, shape_axis, oct_axis, hid, span, cap, kxs, categories, momentum, *refs):
    lox_ref, lo_in, parts, refs = *refs[:2], refs[2:6], refs[6:]
    direction_ref, gain_ref, norm_ref, w_ref, mean_ref, var_ref, refs = *refs[:6], refs[6:]
    dg_ref, gg_ref, bg_ref, cg_ref, mean_out, var_out, left_ref, lo_hbm, full, sem = refs
    join(cap, kxs, oct_axis, lox_ref, lo_hbm, sem, go_start)
    for n in range(4):
        at = pl.ds(pl.multiple_of(column_block(axes, n) * 128, 128), 128)
        full[:, at] = parts[n][...].astype(f32)
    ins, cols = direction_ref.shape
    cats, code_width = mean_ref.shape
    shapes = (full.shape[0] - 16 - (ins - code_width)) // 2
    width = ins - code_width
    ps = full[width : width + shapes, :]
    info = full[width + shapes : width + 2 * shapes, :]
    codes = info[:, :code_width]
    at = code_width
    number = info[:, at : at + 1] + 32.0 * info[:, at + 64 : at + 65] + 1024.0 * info[:, at + 128 : at + 129]
    for c in range(cats):
        chosen = jnp.zeros((shapes, 1), f32)
        for s in range(shapes):
            chosen = jnp.where((iota((shapes, 1), 0) == s) & (categories[s] == c), 1.0, chosen)
        weight = chosen * number
        count = jnp.sum(weight, axis=0, keepdims=True)
        mean = jnp.sum(weight * codes, axis=0, keepdims=True) / count
        var = jnp.sum(weight * codes * codes, axis=0, keepdims=True) / count - mean * mean
        rate = momentum[c]
        mean_out[c : c + 1, :] = (1.0 - rate) * mean_ref[c : c + 1, :] + rate * mean
        var_out[c : c + 1, :] = (1.0 - rate) * var_ref[c : c + 1, :] + rate * var

    gw = full[:width, :]
    codes_all = jnp.concatenate(
        [jnp.zeros((shapes, hid), f32), codes, jnp.zeros((shapes, ins - hid - code_width), f32)], axis=1
    )
    high, low = halves(ps)
    wg = lax.dot_general(jnp.concatenate([codes_all, codes_all], axis=0).astype(bf16), jnp.concatenate([high, low], axis=0),
                         (((0,), (0,)), ((), ())), preferred_element_type=f32)
    head = jnp.where(iota((width, 1), 0) < hid, gw, wg[:width])
    tail = jnp.where(iota((8, 1), 0) + (width - 8) >= hid, gw[width - 8 :], wg[ins - 8 :])
    wg = jnp.concatenate([head, wg[width : ins - 8], tail], axis=0)
    direction = direction_ref[...]
    norms = norm_ref[...]
    dots = jnp.sum(wg * direction, axis=0, keepdims=True)
    gg_ref[...] = dots / norms
    dg_ref[...] = (gain_ref[...] / norms) * (wg - direction * (dots / (norms * norms)))
    bg_ref[...] = jnp.sum(ps, axis=0, keepdims=True)
    base = lax.axis_index(shape_axis) * span
    own = jnp.zeros((8, cols), f32)
    for s in range(span):
        row = jnp.sum(jnp.where(iota((shapes, 1), 0) == base + s, ps, 0.0), axis=0, keepdims=True)
        own = own + jnp.where(iota((8, 1), 0) == s, row, 0.0)
    both = lax.dot_general(jnp.concatenate(halves(own), axis=0), w_ref[...], (((1,), (1,)), ((), ())), preferred_element_type=f32)
    cg_ref[...] = (both[:8] + both[8:])[:span, hid : hid + code_width]
    left_ref[0] = jnp.max(full[width + 2 * shapes : width + 2 * shapes + 8, :128])
    join(cap, kxs, oct_axis, lox_ref, lo_hbm, sem, go_wait)


def finish(axes, span, cap, kxs, categories, momentum, lox, lo, parts, direction, gain, norms, weight, prev_mean, prev_var):
    ins, outs = direction.shape
    return pl.pallas_call(
        functools.partial(finish_kernel, axes, "shape", "oct", HID, span, cap, kxs),
        in_specs=specs("ssva" + "v" * 10),
        out_specs=specs("v" * 6 + "sa"),
        out_shape=[
            jax.ShapeDtypeStruct((ins, outs), f32),
            jax.ShapeDtypeStruct((1, outs), f32),
            jax.ShapeDtypeStruct((1, outs), f32),
            jax.ShapeDtypeStruct((span, prev_mean.shape[1]), f32),
            jax.ShapeDtypeStruct(prev_mean.shape, f32),
            jax.ShapeDtypeStruct(prev_mean.shape, f32),
            jax.ShapeDtypeStruct((1,), f32),
            pltpu.HBM(lo.shape, bf16),
        ],
        input_output_aliases={3: 7},
        scratch_shapes=[pltpu.VMEM((parts[0].shape[0], outs), f32), pltpu.SemaphoreType.DMA((len(kxs),))],
        compiler_params=params(12),
        cost_estimate=cost("finish"),
        name="finish",
    )(categories, momentum, keep(lox), stay(lo), *[keep(p) for p in parts], keep(direction), keep(gain), keep(norms), keep(weight), prev_mean, prev_var)


def swap(v, axis, k):
    n = lax.axis_size(axis)
    return lax.ppermute(v, axis, [(i, i ^ k) for i in range(n)])


def swap_both(v, k):
    n, m = lax.axis_size("shape"), lax.axis_size("oct")
    return lax.ppermute(v, ("shape", "oct"), [(i, i ^ k) for i in range(n * m)])


def bits(axis, first):
    n = lax.axis_size(axis)
    return [(axis, 1 << j) for j in range(first, n.bit_length() - 1)]


def after(x, *others):
    return lax.optimization_barrier((x, *others))[0]


def quarters_to(parts):
    m = lax.axis_size("oct")
    return [swap(parts[0], "oct", 1), swap(parts[1], "shape", 1), swap_both(parts[2], m + 1)]


def total_quarter(parts, before):
    got = quarters_to(parts[1:])
    v = parts[0].astype(f32) + got[0].astype(f32) + got[1].astype(f32) + after(got[2], *before[0]).astype(f32)
    v = v.astype(bf16)
    yield v
    for n, (axis, k) in enumerate(bits("shape", 1) + bits("oct", 1)):
        v = (v.astype(f32) + after(swap(v, axis, k), *before[n + 1]).astype(f32)).astype(bf16)
        yield v


AXES = ("oct", "shape")


def collect(mine, theirs, olds, gw, info, codes, lo, lof, shapes, blocks, cap, message, usual, steps):
    span = codes.shape[0]
    far = len(theirs)
    rows = gw.shape[0] - 16 + 2 * shapes + 16
    out = pl.pallas_call(
        functools.partial(collect_kernel, AXES, "shape", "oct", shapes, span, far, blocks, cap, message, usual, steps),
        in_specs=specs("s" + "s" * far + "v" * far + "vvvaa"),
        out_specs=specs("vvvvaa"),
        out_shape=[pltpu.VMEM((rows, 128), bf16)] * 4 + [pltpu.HBM(lo.shape, bf16), pltpu.HBM(lof.shape, bf16)],
        input_output_aliases={2 * far + 4: 4, 2 * far + 5: 5},
        scratch_shapes=[pltpu.VMEM((rows, gw.shape[1]), f32), pltpu.SemaphoreType.DMA],
        compiler_params=params(8),
        cost_estimate=cost("collect"),
        name="collect",
    )(mine, *theirs, *[keep(o) for o in olds], keep(gw), info, codes, stay(lo), stay(lof))
    return out[:4], out[4], out[5]


def run(usual, steps, point_inputs, shape_ids, octants, categories, codes, direction, gain, bias, cotangent, prev_mean, prev_var, momentum):
    points, width = point_inputs.shape
    oct_count, shape_dev = lax.axis_size("oct"), lax.axis_size("shape")
    cap = 2 * points // oct_count
    span, code_width = codes.shape
    shapes = shape_dev * span
    blocks = points // BLOCK
    far = list(range(1, oct_count // 2))
    messages = plan_messages(usual, steps)
    points_in = [m for m, (first, _) in enumerate(messages) if first < usual]

    (ct_near, ct_far, x_near), heads, queues, rows_far, (row_near, mine, near_names, info) = pack(
        octants, shape_ids, point_inputs, cotangent, messages, oct_count, span, cap)
    ctn, ctf = swap(ct_near, "oct", 1), swap(ct_far, "oct", 1)
    got = {(k, m): swap(heads[2 * (k - 1) + m], "oct", 2 * k) for k in far for m in range(2)}
    lo, lon, gw, buf, wp, wpt, weight, cb, norms, direction_v, gain_v = prepare(
        mine, row_near, x_near, direction, gain, bias, codes, oct_count, cap)
    weights = (wp, wpt, cb)
    lo, lon, lof, gw, buf = local(mine, near_names, cotangent, ctn, weights, lo, lon, gw, buf, len(far), blocks, span, cap)

    queue = {k: queues[k - 1] for k in far}
    named, theirs, back, ahead = {}, {}, {}, {}
    for k in far:
        named[k], theirs[k], back[k] = make_names(after(got[k, 0], gw)[messages[0][1] * UNIT :], k, span, cap)
        ahead[k] = ()
    for m in points_in:
        for k in far:
            (queue[k], lo, lof, gw, back[k]), payloads, ahead[k] = far_step(
                messages, m, points_in, k, mine, theirs[k], named[k], got[k, m], cotangent, ctf, weights,
                (queue[k], lo, lof, gw, back[k]), ahead[k], blocks, span, cap)
            for j, payload in enumerate(payloads):
                got[k, m + 2 + j] = swap(payload, "oct", 2 * k)
        if m == min(1, points_in[-1] - 1):
            part, lo = unlocal(mine, row_near, after(buf, gw), swap(lon, "oct", 1), lo, cap)
            gw = after(gw, part)
    their = [theirs[k] for k in far]
    lasts = list(range(len(points_in), len(messages)))
    order = ((), (0,), (), (1,)) if usual % 2 else ()
    before = [[got[k, lasts[i]] for k in far for i in ii] for ii in order] + [[] for _ in range(20)]
    parts, lo, lof = collect(mine, their, [ahead[k][-1] for k in far], gw, info, codes, lo, lof, shapes, blocks, cap,
                             messages[points_in[-1]], usual, steps)
    lox = swap(lof, "oct", 1)
    for v in total_quarter(parts, before):
        pass
    parts = [v] + quarters_to([v] * 3)
    input_grad = unpack(mine, their, rows_far, [messages[m] for m in lasts], [got[k, m] for k in far for m in lasts], part,
                        [back[k] for k in far])
    direction_grad, gain_grad, bias_grad, code_grad, running_mean, running_var, left, lo = finish(
        AXES, span, cap, tuple(far), categories, momentum, lox, lo, [after(parts[0], input_grad)] + parts[1:], direction_v, gain_v, norms, weight, prev_mean, prev_var)
    outputs = (
        lo,
        input_grad,
        code_grad,
        direction_grad,
        gain_grad[0],
        bias_grad[0],
        running_mean,
        running_var,
    )
    return outputs, left[0]


def body(*args):
    points, oct_count = args[0].shape[0], lax.axis_size("oct")
    most = units(2 * (2 * points // oct_count) // TILE)
    all_steps = max(most, LEAD) + most
    usual, steps = min(USUAL, most), min(STEPS, all_steps)
    outputs, left = run(usual, steps, *args)
    if (usual, steps) == (most, all_steps):
        return outputs

    def more(carry):
        return jnp.float32(0), run(most, all_steps, *args)[0]

    return lax.while_loop(lambda carry: carry[0] > 0, more, (left, outputs))[1]


def solution(mesh):
    both = P(("shape", "oct"), None)
    in_specs = (both, P(("shape", "oct")), both, P(), P("shape", None), P(), P(), P(), both, P(), P(), P())
    out_specs = (both, both, P("shape", None), P(), P(), P(), P(), P())
    return jax.shard_map(body, mesh=mesh, in_specs=in_specs, out_specs=out_specs, check_vma=False)
```

```python
import functools

import jax
import jax.numpy as jnp
from jax import lax
from jax.experimental import pallas as pl
from jax.experimental.pallas import tpu as pltpu
from jax.sharding import PartitionSpec as P

HID = 253
CATS = 5
BLOCK = 256
TILE = 256
ALIGN = 64
UNIT = 2 * TILE
WIN = BLOCK + 16
LEAD = 8
USUAL = 13
STEPS = 21
PART = 4
FAR = 1 << 20

norm_eps = 1e-06
COSTS = dict(pack=30, prepare=30, local=30, unlocal=0.01, names=30, far=30, last=0.01, flush=0.01, unpack=30, merge=0.01, finish=30, collect=0.01)


def cost(name):
    return pl.CostEstimate(flops=max(1, int(COSTS[name] * 10**9)), bytes_accessed=1, transcendentals=0)


f32, bf16, i32 = jnp.float32, jnp.bfloat16, jnp.int32


def params(mib):
    return pltpu.CompilerParams(vmem_limit_bytes=mib * 1024 * 1024)


def keep(x):
    return pltpu.with_memory_space_constraint(x, pltpu.VMEM)


def stay(x):
    return pltpu.with_memory_space_constraint(x, pltpu.HBM)


def specs(text):
    kinds = {"v": pltpu.VMEM, "s": pltpu.SMEM, "a": pl.ANY}
    return [pl.BlockSpec(memory_space=kinds[c]) for c in text]


def iota(shape, dim):
    return lax.broadcasted_iota(i32, shape, dim)


def plan_messages(usual, steps):
    cuts = list(range(0, usual, PART)) + list(range(usual, steps, PART)) + [steps]
    if usual % PART == 1:
        cuts[usual // PART] -= 1
    return [(a, b - a) for a, b in zip(cuts, cuts[1:])]


def ceil_to(n, step):
    return -(-n // step) * step


def plan(labels, groups, span):
    rows = labels.shape[0]
    count = len(groups)
    mask = jnp.concatenate([(labels >= g * span) & (labels < (g + 1) * span) for g in groups], axis=0)
    one = jnp.where(mask, 1.0, 0.0)
    m = one.astype(bf16)
    total = count * rows
    upper = jnp.where(iota((BLOCK, BLOCK), 0) <= iota((BLOCK, BLOCK), 1), 1.0, 0.0).astype(bf16)
    cum = jnp.dot(m, upper, preferred_element_type=f32)
    a, b = iota((total, total), 0), iota((total, total), 1)
    lower = jnp.where((a // rows == b // rows) & (b < a), 1.0, 0.0).astype(bf16)
    tot = jnp.sum(one, axis=1, keepdims=True)
    base = jnp.dot(lower, jnp.broadcast_to(tot, (total, 128)).astype(bf16), preferred_element_type=f32)[:, :1]
    lo, hi = base.astype(i32), (base + tot).astype(i32)
    pos = jnp.where(mask, lo + cum.astype(i32) - 1, -FAR)
    tot_row = lax.dot_general(jnp.ones((8, BLOCK), bf16), m, (((1,), (1,)), ((), ())), preferred_element_type=f32)
    base_row = lax.dot_general(tot_row.astype(bf16), lower, (((1,), (1,)), ((), ())), preferred_element_type=f32)
    return pos, lo, hi, base_row.astype(i32), (base_row + tot_row).astype(i32)


def sorted_rows(pos, lo, hi, rows, first, count):
    row, at = None, 0
    for n in range(first, first + count):
        s = slice(n * rows, (n + 1) * rows)
        start = lo[s] // 16 * 16
        r = pos[s] + (at - start)
        row = r if row is None else jnp.maximum(row, r)
        at = at + (hi[s] + 15) // 16 * 16 - start
    return row


def ahead_by(v, step):
    rows, lanes = v.shape
    if step >= lanes:
        return pltpu.roll(v, rows - step // lanes, 0)
    moved = pltpu.roll(v, lanes - step, 1)
    return jnp.where(iota((rows, lanes), 1) < lanes - step, moved, pltpu.roll(moved, rows - 1, 0))


def back_by(v, step):
    rows, lanes = v.shape
    if step >= lanes:
        return pltpu.roll(v, step // lanes, 0)
    moved = pltpu.roll(v, step, 1)
    return jnp.where(iota((rows, lanes), 1) >= step, moved, pltpu.roll(moved, 1, 0))


def squeeze(pos, labels, group, span):
    rows, lanes = pos.shape
    at = iota((rows, lanes), 0) * lanes + iota((rows, lanes), 1)
    v = jnp.where(pos >= 0, (at - pos) * 16 + (labels - group * span + 1), 0)
    for bit in range((rows * lanes).bit_length() - 1):
        go = jnp.where(((v >> (4 + bit)) & 1) == 1, v, 0)
        v = v - go + ahead_by(go, 1 << bit)
    return v & 15


def stream_names(pos, labels, group, span, cap):
    rows = labels.shape[0]
    first, second = (squeeze(pos[n * rows : (n + 1) * rows], labels, group + n, span) for n in range(2))
    one = jnp.where(pos[:rows] >= 0, 1.0, 0.0)
    count = jnp.sum(jnp.sum(one, axis=1, keepdims=True), axis=0, keepdims=True).astype(i32)
    skip = (count + (ALIGN - 1)) // ALIGN * ALIGN
    step = ALIGN
    while step <= cap:
        second = jnp.where((skip & step) > 0, back_by(second, step), second)
        step *= 2
    return first + second


def filled(bounds, group, blocks, row=1):
    return (bounds[row, (group + 1) * blocks - 1] + (ALIGN - 1)) // ALIGN * ALIGN


def tiles_of(bounds, group, blocks, row=1):
    return (filled(bounds, group, blocks, row) + filled(bounds, group + 1, blocks, row) + (TILE - 1)) // TILE


def spans(bounds, groups, blocks, b):
    at, result = 0, []
    for g in groups:
        lo, hi = bounds[0, g * blocks + b], bounds[1, g * blocks + b]
        first = pl.multiple_of(lo // 16 * 16, 16)
        result.append((first, pl.multiple_of(at, 16) if result else 0, lo - first))
        at = at + ((hi + 15) // 16 * 16 - first)
    return result


def window_rows(count, step):
    return ceil_to(BLOCK + 30 * count, step)


def sort_rows(bounds, row_ref, x_ref, groups, blocks, moved, put):
    rows = window_rows(len(groups), 64)
    for b in range(blocks):
        hot = jnp.where(iota((rows, BLOCK), 0) == row_ref[b : b + 1, :], 1.0, 0.0).astype(bf16)
        out = jnp.dot(hot, x_ref[b * BLOCK : (b + 1) * BLOCK, :], preferred_element_type=f32).astype(bf16)
        moved[b * rows : (b + 1) * rows, :] = out
    moved[blocks * rows :, :] = jnp.zeros((moved.shape[0] - blocks * rows, moved.shape[1]), bf16)
    for n in range(len(groups)):
        for b in range(blocks):
            first, at, over = spans(bounds, groups, blocks, b)[n]
            dst, start = put(n, first)
            at = at + b * rows
            old = dst[pl.ds(start, 16), :]
            new = moved[pl.ds(pl.multiple_of(at, 16), 16), :]
            dst[pl.ds(start, 16), :] = jnp.where(iota((16, 1), 0) < over, old, new)
            rest = pl.ds(pl.multiple_of(start + 16, 16), BLOCK)
            dst[rest, :] = moved[pl.ds(pl.multiple_of(at + 16, 16), BLOCK), :]


def unsort_rows(bounds, row_ref, groups, blocks, pick, moved, emit):
    rows = window_rows(len(groups), 128)
    for b in range(blocks):
        moved[b * rows + WIN : (b + 1) * rows, :] = jnp.zeros((rows - WIN, moved.shape[1]), bf16)
        for n, (first, at, _) in enumerate(spans(bounds, groups, blocks, b)):
            moved[pl.ds(pl.multiple_of(at + b * rows, 16), WIN), :] = pick(n, first, WIN)
    for b in range(blocks):
        hot = jnp.where(iota((rows, BLOCK), 0) == row_ref[b : b + 1, :], 1.0, 0.0).astype(bf16)
        emit(b, jnp.dot(jnp.transpose(hot), moved[b * rows : (b + 1) * rows, :], preferred_element_type=f32))


def layer_tile(x, named, ct, wp_ref, wpt_ref, cb_ref, gw_ref, span):
    rows = x.shape[0]
    col = jnp.transpose(jnp.broadcast_to(named.astype(f32), (8, rows)))[:, :1]
    pre = jnp.dot(x, wp_ref[...], preferred_element_type=f32)
    add = cb_ref[0:1, :]
    for s in range(1, span):
        add = jnp.where(col == s + 1.0, cb_ref[s : s + 1, :], add)
    pre = pre + add
    valid = col > 0.0
    e = jnp.exp(-jnp.abs(pre))
    soft = jnp.maximum(pre, 0.0) + jnp.where(e < 2.0**-12, e, jnp.log(1.0 + e))
    sig = jnp.exp(pre - soft)
    lo = jnp.where(valid, soft, 0.0).astype(bf16)
    gp = jnp.where(valid, ct.astype(f32) * sig, 0.0).astype(bf16)
    gx = jnp.dot(gp, wpt_ref[...], preferred_element_type=f32).astype(bf16)
    sel = jnp.where(jnp.broadcast_to(named, (16, rows)) == iota((16, rows), 0) + 1, 1.0, 0.0).astype(bf16)
    left = jnp.concatenate([jnp.transpose(x), sel], axis=0)
    gw_ref[...] += jnp.dot(left, gp, preferred_element_type=f32)
    return lo, gx


def pack_kernel(oct_count, sizes, shape_axis, oct_axis, span, cap, octants_hbm, ids_hbm, x_hbm, ct_hbm, *refs):
    far = oct_count // 2 - 1
    octants_ref, ids_ref, in_sem, ct_sem = refs[-4:]
    refs = refs[:-4]
    ct_near, ct_far, x_ref, refs = *refs[:3], refs[3:]
    other = lax.axis_index(oct_axis) ^ 1
    blocks_out = []
    for k in range(oct_count // 2):
        there = ct_hbm.at[pl.ds(pl.multiple_of((other ^ (2 * k)) * cap, cap), cap), :]
        here = ct_far.at[pl.ds((k - 1) * cap, cap), :] if k else ct_near
        blocks_out.append(pltpu.make_async_copy(there, here, ct_sem.at[k]))
    fetches = [
        pltpu.make_async_copy(a, b, in_sem.at[i])
        for i, (a, b) in enumerate(zip((octants_hbm, ids_hbm, x_hbm), (octants_ref, ids_ref, x_ref)))
    ]
    for f in fetches + blocks_out:
        f.start()
    heads, refs = refs[: 2 * far], refs[2 * far :]
    queues, rows_far, refs = refs[:far], refs[far : 2 * far], refs[2 * far :]
    row_near, bounds_ref, labels_ref, pos_ref, moved, bounds_v, bounds, sem = refs
    blocks = row_near.shape[0]
    me = lax.axis_index(oct_axis)
    first_shape = lax.axis_index(shape_axis) * span

    def wide(ref):
        return jnp.concatenate([ref[pl.ds(h, blocks, 2), :] for h in range(2)], axis=1)

    for f in fetches[:2]:
        f.wait()
    ids = wide(ids_ref) - first_shape
    labels = (wide(octants_ref) ^ me) * span + ids
    pos, lo, hi, first_row, last_row = plan(labels, range(oct_count), span)
    n = oct_count * blocks
    bounds_v[...] = jnp.zeros(bounds_v.shape, i32)
    bounds_v[0:1, :n] = first_row[:1]
    bounds_v[1:2, :n] = last_row[:1]
    bounds_ref[...] = bounds_v[...]
    copy = pltpu.make_async_copy(bounds_v, bounds, sem)
    copy.start()
    row_near[...] = sorted_rows(pos, lo, hi, blocks, 0, 2)
    for k in range(far):
        rows_far[k][...] = sorted_rows(pos, lo, hi, blocks, 2 + 2 * k, 2)
    labels_ref[...] = labels
    pos_ref[...] = pos[: 2 * blocks]
    for k in range(far):
        queues[k][...] = jnp.zeros(queues[k].shape, bf16)
    copy.wait()
    fetches[2].wait()
    for k in range(far):
        groups = [2 + 2 * k, 3 + 2 * k]
        cut = filled(bounds, groups[0], blocks)
        sort_rows(bounds, rows_far[k], x_ref, groups, blocks, moved,
                  lambda n, first: (queues[k], pl.multiple_of(first + n * cut, 16)))
        heads[2 * k][: sizes[0], :] = queues[k][: sizes[0], :]
        heads[2 * k][sizes[0] :, :] = labels.astype(f32).astype(bf16)
        heads[2 * k + 1][...] = queues[k][sizes[0] : sizes[0] + sizes[1], :]
    for f in blocks_out:
        f.wait()


def pack(octants, ids, points, cotangent, messages, oct_count, span, cap):
    count, width = points.shape
    blocks = count // BLOCK
    far = oct_count // 2 - 1
    shape = jax.ShapeDtypeStruct
    sizes = [n * TILE for _, n in messages[:2]]
    heads = [pltpu.VMEM((sizes[0] + blocks, width), bf16), pltpu.VMEM((sizes[1], width), bf16)] * far
    cols = cotangent.shape[1]
    outs = [pltpu.VMEM((cap, cols), bf16), pltpu.VMEM((far * cap, cols), bf16), pltpu.VMEM(points.shape, bf16)] + heads + [pltpu.VMEM((4 * cap, width), bf16)] * far
    outs += [shape((blocks, BLOCK), i32)] * (far + 1)
    outs += [shape((8, 128), i32), shape((blocks, BLOCK), i32), shape((2 * blocks, BLOCK), i32)]
    out = pl.pallas_call(
        functools.partial(pack_kernel, oct_count, sizes, "shape", "oct", span, cap),
        in_specs=specs("aaaa"),
        out_specs=specs("v" * len(outs)),
        out_shape=outs,
        scratch_shapes=[
            pltpu.VMEM((blocks * window_rows(2, 64) + WIN, width), bf16),
            pltpu.VMEM((8, 128), i32),
            pltpu.SMEM((8, 128), i32),
            pltpu.SemaphoreType.DMA,
            pltpu.VMEM((count // 128, 128), i32),
            pltpu.VMEM((count // 128, 128), i32),
            pltpu.SemaphoreType.DMA((3,)),
            pltpu.SemaphoreType.DMA((oct_count // 2,)),
        ],
        compiler_params=params(16),
        cost_estimate=cost("pack"),
        name="pack",
    )(stay(octants.reshape(-1, 128)), stay(ids.reshape(-1, 128)), stay(points), stay(cotangent))
    x, out = out[:3], out[3:]
    heads, queues, rows_far, out = out[: 2 * far], out[2 * far : 3 * far], out[3 * far : 4 * far], out[4 * far :]
    return x, heads, queues, rows_far, out


def set_weights(hid, direction_ref, gain_ref, bias_ref, codes_ref, wp_ref, wpt_ref, w_ref, cb_ref, norm_ref):
    direction = direction_ref[...]
    norms = jnp.sqrt(jnp.sum(direction * direction, axis=0, keepdims=True) + norm_eps)
    weight = (direction * (gain_ref[...] / norms)).astype(bf16)
    norm_ref[...] = norms
    w_ref[...] = weight
    width = wp_ref.shape[0]
    wf = weight.astype(f32)
    last = jnp.where(iota((8, 1), 0) + (width - 8) < hid, wf[width - 8 : width, :], wf[-8:, :])
    wp = jnp.concatenate([wf[: width - 8, :], last], axis=0)
    wp_ref[...] = wp.astype(bf16)
    wpt_ref[...] = wp.T.astype(bf16)
    span, code_width = codes_ref.shape
    w_code = wf[hid : hid + code_width, :].astype(bf16)
    codes = jnp.concatenate([codes_ref[...].astype(f32), jnp.zeros((8 - span, code_width), f32)], axis=0).astype(bf16)
    cb_ref[...] = jnp.dot(codes, w_code, preferred_element_type=f32) + bias_ref[...]


def prepare_kernel(oct_count, oct_axis, span, cap, bounds, row_ref, labels_ref, pos_ref, x_ref, codes_v, direction_hbm, gain_hbm, bias_hbm,
                   gw_ref, buf, wp_ref, wpt_ref, w_ref, cb_ref, norm_ref, direction_v, gain_v,
                   names_ref, info_ref, moved, bias_v, in_sem):
    blocks = row_ref.shape[0]
    cut = [filled(bounds, r, blocks) for r in range(2)]
    fetches = [
        pltpu.make_async_copy(a, b, in_sem.at[i])
        for i, (a, b) in enumerate(((direction_hbm, direction_v), (gain_hbm, gain_v), (bias_hbm, bias_v)))
    ]
    for f in fetches:
        f.start()

    gw_ref[...] = jnp.zeros(gw_ref.shape, f32)
    buf[...] = jnp.zeros(buf.shape, bf16)
    sort_rows(bounds, row_ref, x_ref, [0, 1], blocks, moved,
              lambda n, first: (buf, pl.multiple_of(first + n * cut[0], 16)))
    labels = labels_ref[...]
    names_ref[...] = stream_names(pos_ref[...], labels, 0, span, cap)
    ids = labels % span
    info_ref[...] = jnp.zeros(info_ref.shape, f32)
    for s in range(span):
        number = jnp.sum(jnp.sum(jnp.where(ids == s, 1.0, 0.0), axis=1, keepdims=True), axis=0, keepdims=True)
        info_ref[s : s + 1, :] = jnp.broadcast_to(number, (1, 128))
    for f in fetches:
        f.wait()
    set_weights(HID, direction_v, gain_v, bias_v, codes_v, wp_ref, wpt_ref, w_ref, cb_ref, norm_ref)


def prepare(bounds, row, labels, pos, points, direction, gain, bias, codes, oct_count, cap):
    width = points.shape[1]
    ins, outs = direction.shape
    blocks = row.shape[0]
    return pl.pallas_call(
        functools.partial(prepare_kernel, oct_count, "oct", codes.shape[0], cap),
        in_specs=specs("svvvvvaaa"),
        out_specs=specs("vvvvvvvvvvv"),
        out_shape=[
            pltpu.VMEM((width + 16, outs), f32),
            pltpu.VMEM((2 * cap + BLOCK + WIN, width), bf16),
            pltpu.VMEM((width, outs), bf16),
            pltpu.VMEM((outs, width), bf16),
            pltpu.VMEM((ins, outs), bf16),
            pltpu.VMEM((8, outs), f32),
            pltpu.VMEM((1, outs), f32),
            pltpu.VMEM((ins, outs), f32),
            pltpu.VMEM((1, outs), f32),
            pltpu.VMEM(row.shape, i32),
            pltpu.VMEM((8, 128), f32),
        ],
        scratch_shapes=[
            pltpu.VMEM((blocks * window_rows(2, 64) + WIN, width), bf16),
            pltpu.VMEM((1, outs), f32),
            pltpu.SemaphoreType.DMA((3,)),
        ],
        compiler_params=params(14),
        cost_estimate=cost("prepare"),
        name="prepare",
    )(bounds, row, labels, pos, keep(points), codes, stay(direction), stay(gain[None, :]), stay(bias[None, :]))


class Rows:
    def __init__(self, cut, source, cap, place):
        self.cut, self.own_at, self.other_at = cut, source * cap, place * cap
        self.total = cut[0] + cut[1]
        self.tiles = (self.total + (TILE - 1)) // TILE

    def move(self, tile, own, other, mine, mine_at, sem, out, go):
        first = tile * TILE
        cut, total = self.cut[0], self.total

        def one(at, rows, second):
            here = mine.at[pl.ds(mine_at + at, rows), :]
            row = first + at
            there = other if second else own
            start = self.other_at + row - cut if second else self.own_at + row
            there = there.at[pl.ds(pl.multiple_of(start, ALIGN), rows), :]
            go(pltpu.make_async_copy(here, there, sem) if out else pltpu.make_async_copy(there, here, sem))

        whole = first + TILE <= cut
        last = (first >= cut) & (first + TILE <= total)
        pl.when(whole)(lambda: one(0, TILE, False))
        pl.when(last)(lambda: one(0, TILE, True))

        @pl.when((first < total) & jnp.logical_not(whole | last))
        def _():
            for at in range(0, TILE, ALIGN):
                pl.when(first + at < cut)(lambda: one(at, ALIGN, False))
                pl.when((first + at >= cut) & (first + at < total))(lambda: one(at, ALIGN, True))

    def fetch(self, tile, ct, ctx, mine, at, sem, go):
        self.move(tile, ct, ctx, mine, at, sem, False, go)

    def store(self, tile, lo, lox, mine, at, sem, go):
        self.move(tile, lo, lox, mine, at, sem, True, go)


def rows_of(bounds, group, blocks, source, cap, place, row=1):
    return Rows([filled(bounds, group + r, blocks, row) for r in range(2)], source, cap, place)


def names_at(names_ref, tile, number):
    return jnp.concatenate([names_ref[pl.ds(tile + i, 1), :] for i in range(number)], axis=1)


def go_start(copy):
    copy.start()


def go_wait(copy):
    copy.wait()


def local_kernel(oct_axis, far, blocks, span, cap, bounds, *refs):
    names_ref, ct_hbm, ctx_ref, wp_ref, wpt_ref, cb_ref, gw_in, buf_in, refs = *refs[:8], refs[8:]
    lo_hbm, lon_hbm, lof_hbm, gw_ref, buf, refs = *refs[:5], refs[5:]
    ct_v, lo_v, zero, ct_sem, lo_sem, zero_sem = refs
    source = lax.axis_index(oct_axis)
    near = rows_of(bounds, 0, blocks, source, cap, 0)
    count = (near.tiles + (PART - 1)) // PART

    def clear(go):
        def empty(array, at, t, cut):
            pl.when(t * TILE >= cut)(lambda: go(pltpu.make_async_copy(zero, array.at[pl.ds(pl.multiple_of(at + t * TILE, TILE), TILE), :], zero_sem)))

            @pl.when((t * TILE < cut) & ((t + 1) * TILE > cut))
            def _():
                for q in range(0, TILE, ALIGN):
                    @pl.when(t * TILE + q >= cut)
                    def _():
                        rows = pl.ds(pl.multiple_of(at + t * TILE + q, ALIGN), ALIGN)
                        go(pltpu.make_async_copy(zero.at[pl.ds(0, ALIGN), :], array.at[rows, :], zero_sem))

        for t in range(cap // TILE):
            empty(lo_hbm, source * cap, t, near.cut[0])
            empty(lon_hbm, 0, t, near.cut[1])
        for k in range(1, far + 1):
            for t in range(cap // TILE):
                at = (source ^ (2 * k)) * cap + t * TILE
                go(pltpu.make_async_copy(zero, lo_hbm.at[pl.ds(pl.multiple_of(at, TILE), TILE), :], zero_sem))
        for t in range(lof_hbm.shape[0] // TILE):
            go(pltpu.make_async_copy(zero, lof_hbm.at[pl.ds(t * TILE, TILE), :], zero_sem))

    def fetch(i, slot, go):
        for j in range(PART):
            near.fetch(i * PART + j, ct_hbm, ctx_ref, ct_v.at[slot], j * TILE, ct_sem.at[slot], go)

    def store(i, slot, go):
        for j in range(PART):
            near.store(i * PART + j, lo_hbm, lon_hbm, lo_v.at[slot], j * TILE, lo_sem.at[slot], go)

    @pl.when(count > 0)
    def _():
        fetch(0, 0, go_start)

    zero[...] = jnp.zeros(zero.shape, bf16)
    clear(go_start)

    def step(i, carry):
        slot = i % 2

        @pl.when(i + 1 < count)
        def _():
            fetch(i + 1, 1 - slot, go_start)

        fetch(i, slot, go_wait)

        @pl.when(i >= 2)
        def _():
            store(i - 2, slot, go_wait)

        def work(size):
            at = pl.ds(pl.multiple_of(i * PART * TILE, TILE), size * TILE)
            ct = ct_v[slot, : size * TILE, :]
            lo, gx = layer_tile(buf[at, :], names_at(names_ref, i * PART, size), ct, wp_ref, wpt_ref, cb_ref, gw_ref, span)
            lo_v[slot, : size * TILE, :] = lo
            buf[at, :] = gx

        more = near.tiles - i * PART > 2
        pl.when(more)(lambda: work(PART))
        pl.when(jnp.logical_not(more))(lambda: work(2))
        store(i, slot, go_start)
        return carry

    lax.fori_loop(0, count, step, 0)
    for back in (2, 1):
        @pl.when(count >= back)
        def _():
            store(count - back, (count - back) % 2, go_wait)

    clear(go_wait)


def local(bounds, names, cotangent, ctx, weights, gw, buf, far, blocks, span, cap):
    outs = cotangent.shape[1]
    return pl.pallas_call(
        functools.partial(local_kernel, "oct", far, blocks, span, cap),
        in_specs=specs("svavvvvvv"),
        out_specs=specs("aaavv"),
        out_shape=[pltpu.HBM(cotangent.shape, bf16), pltpu.HBM((cap, outs), bf16), pltpu.HBM((far * cap, outs), bf16),
                   pltpu.VMEM(gw.shape, f32), pltpu.VMEM(buf.shape, bf16)],
        input_output_aliases={7: 3, 8: 4},
        scratch_shapes=[
            pltpu.VMEM((2, PART * TILE, outs), bf16),
            pltpu.VMEM((2, PART * TILE, outs), bf16),
            pltpu.VMEM((TILE, outs), bf16),
            pltpu.SemaphoreType.DMA((2,)),
            pltpu.SemaphoreType.DMA((2,)),
            pltpu.SemaphoreType.DMA,
        ],
        compiler_params=params(24),
        cost_estimate=cost("local"),
        name="local",
    )(bounds, names, stay(cotangent), keep(ctx), *[keep(w) for w in weights], keep(gw), keep(buf))


def unlocal_kernel(oct_axis, cap, bounds, row_ref, gbuf, lon_ref, lo_in, part_ref, lo_hbm, moved, sem):
    blocks = row_ref.shape[0]
    join(cap, [0], oct_axis, lon_ref, lo_hbm, sem, go_start)

    def emit(b, rows):
        part_ref[b * BLOCK : (b + 1) * BLOCK, :] = rows.astype(bf16)

    cut = filled(bounds, 0, blocks)
    unsort_rows(bounds, row_ref, [0, 1], blocks,
                lambda n, first, rows: gbuf[pl.ds(pl.multiple_of(first + n * cut, 16), rows), :], moved, emit)
    join(cap, [0], oct_axis, lon_ref, lo_hbm, sem, go_wait)


def unlocal(bounds, row, gbuf, lon, lo, cap):
    blocks, width = row.shape[0], gbuf.shape[1]
    return pl.pallas_call(
        functools.partial(unlocal_kernel, "oct", cap),
        in_specs=specs("svvva"),
        out_specs=specs("va"),
        out_shape=[pltpu.VMEM((blocks * BLOCK, width), bf16), pltpu.HBM(lo.shape, bf16)],
        input_output_aliases={4: 1},
        scratch_shapes=[pltpu.VMEM((blocks * window_rows(2, 128) + WIN, width), bf16), pltpu.SemaphoreType.DMA((1,))],
        compiler_params=params(16),
        cost_estimate=cost("unlocal"),
        name="unlocal",
    )(bounds, row, keep(gbuf), keep(lon), stay(lo))


def names_kernel(kx, span, cap, labels_ref, names_ref, count_ref, back_ref):
    labels = labels_ref[...].astype(f32).astype(i32)
    blocks = labels.shape[0]
    groups = [2 * kx, 2 * kx + 1]
    pos, _, _, _, last = plan(labels, groups, span)
    names_ref[...] = stream_names(pos, labels, groups[0], span, cap)
    count_ref[...] = jnp.zeros(count_ref.shape, i32)
    count_ref[0:1, : 2 * blocks] = last[:1]
    back_ref[...] = jnp.zeros(back_ref.shape, bf16)


def make_names(labels, kx, span, cap):
    return pl.pallas_call(
        functools.partial(names_kernel, kx, span, cap),
        in_specs=specs("v"),
        out_specs=specs("vvv"),
        out_shape=[
            jax.ShapeDtypeStruct((labels.shape[0], BLOCK), i32),
            jax.ShapeDtypeStruct((8, 128), i32),
            pltpu.VMEM((2 * cap + UNIT, labels.shape[1]), bf16),
        ],
        compiler_params=params(8),
        cost_estimate=cost("names"),
        name="names",
    )(labels)


def lead_of(tiles):
    return jnp.maximum(tiles, LEAD)


def take_back(place, number, theirs, blocks, x_ref, at, back):
    for i in range(number):
        n = place + i - lead_of(tiles_of(theirs, 0, blocks, 0))

        @pl.when((n >= 0) & (n < (back.shape[0] - UNIT) // TILE))
        def _():
            back[pl.ds(pl.multiple_of(n * TILE, TILE), TILE), :] = x_ref[at + i * TILE : at + (i + 1) * TILE, :]


def far_kernel(message, before, after_it, emits, kx, oct_axis, blocks, span, cap, mine, theirs, *refs):
    names_ref, x_ref, ct_hbm, ctx_ref, wp_ref, wpt_ref, cb_ref, queue_in, lo_in, lof_in, gw_in, back_in, refs = *refs[:12], refs[12:]
    if before:
        ct_v, lo_old, refs = *refs[:2], refs[2:]
    queue, lo_hbm, lof_hbm, gw_ref, back, refs = *refs[:5], refs[5:]
    payloads, refs = refs[: len(emits)], refs[len(emits) :]
    if after_it:
        ct_new, refs = refs[0], refs[1:]
    lo_v, refs = refs[0], refs[1:]
    if not before:
        ct_v, refs = refs[0], refs[1:]
    ct_sem, new_sem, lo_sem = refs
    first, number = message
    source = lax.axis_index(oct_axis) ^ (2 * kx)
    rows = rows_of(theirs, 0, blocks, source, cap, kx - 1, 0)
    lead = lead_of(tiles_of(mine, 2 * kx, blocks))

    def fetch(u, go):
        if not before:
            rows.fetch(first + u, ct_hbm, ctx_ref, ct_v, u * TILE, ct_sem.at[u], go)

    def ahead(go):
        if before:
            for u in range(before[1]):
                rows.store(before[0] + u, lo_hbm, lof_hbm, lo_old, u * TILE, lo_sem, go)
        if after_it:
            for u in range(after_it[1]):
                rows.fetch(after_it[0] + u, ct_hbm, ctx_ref, ct_new, u * TILE, new_sem, go)

    for u in range(number):
        fetch(u, go_start)
    ahead(go_start)
    take_back(first, number, theirs, blocks, x_ref, 0, back)
    for u in range(number):
        fetch(u, go_wait)

    def work(size):
        at = slice(0, size * TILE)
        lo, gx = layer_tile(x_ref[at, :], names_at(names_ref, first, size), ct_v[at, :], wp_ref, wpt_ref, cb_ref, gw_ref, span)
        lo_v[at, :] = lo
        queue[pl.ds(pl.multiple_of((lead + first) * TILE, TILE), size * TILE), :] = gx

    if number > 2:
        pl.when(first + 2 < rows.tiles)(lambda: work(number))
        pl.when((first < rows.tiles) & (first + 2 >= rows.tiles))(lambda: work(2))
    else:
        pl.when(first < rows.tiles)(lambda: work(number))

    for payload, (place, count) in zip(payloads, emits):
        payload[...] = queue[place * TILE : (place + count) * TILE, :]
    ahead(go_wait)


def far_step(messages, m, points_in, kx, mine, theirs, names, x, cotangent, ctx, weights, state, ahead, blocks, span, cap):
    wp, wpt, cb = weights
    queue, lo, lof, gw, back = state
    width, outs = wp.shape
    last = points_in[-1] == m
    message, before, after_it = messages[m], (messages[m - 1] if m > 0 else None), (None if last else messages[m + 1])
    emits = messages[m + 2 :] if last else [messages[m + 2]]
    own = (message[1] * TILE, outs)
    shapes = [pltpu.VMEM(queue.shape, bf16), pltpu.HBM(lo.shape, bf16), pltpu.HBM(lof.shape, bf16), pltpu.VMEM(gw.shape, f32),
              pltpu.VMEM(back.shape, bf16)] + [pltpu.VMEM((count * TILE, width), bf16) for _, count in emits]
    if after_it:
        shapes.append(pltpu.VMEM((after_it[1] * TILE, outs), bf16))
    shapes.append(pltpu.VMEM(own, bf16))
    args = [mine, theirs, names, keep(x), stay(cotangent), keep(ctx), keep(wp), keep(wpt), keep(cb), keep(queue), stay(lo),
            stay(lof), keep(gw), keep(back)] + [keep(a) for a in ahead]
    out = pl.pallas_call(
        functools.partial(far_kernel, message, before, after_it, emits, kx, "oct", blocks, span, cap),
        in_specs=specs("ssvvavvvvvaavv" + "v" * len(ahead)),
        out_specs=specs("vaavv" + "v" * (len(shapes) - 5)),
        out_shape=shapes,
        input_output_aliases={9 + i: i for i in range(5)},
        scratch_shapes=([] if before else [pltpu.VMEM(own, bf16)])
        + [pltpu.SemaphoreType.DMA((message[1],)), pltpu.SemaphoreType.DMA, pltpu.SemaphoreType.DMA],
        compiler_params=params(20),
        cost_estimate=cost("last" if last else "far"),
        name="far",
    )(*args)
    return tuple(out[:5]), out[5 : 5 + len(emits)], tuple(out[5 + len(emits) :])


def unpack_kernel(far, blocks, lasts, bounds, *refs):
    theirs, rows_far, refs = refs[:far], refs[far : 2 * far], refs[2 * far :]
    parts, refs = refs[: far * len(lasts)], refs[far * len(lasts) :]
    part_ref, refs = refs[0], refs[1 + far :]
    out_ref, backs, moved = refs[0], refs[1 : 1 + far], refs[-1]
    for k in range(far):
        for j, (first, number) in enumerate(lasts):
            take_back(first, number, theirs[k], blocks, parts[k * len(lasts) + j], 0, backs[k])
        cut = filled(bounds, 2 + 2 * k, blocks)

        def pick(n, first, count):
            return backs[k][pl.ds(pl.multiple_of(first + n * cut, 16), count), :]

        def emit(b, value):
            at = slice(b * BLOCK, (b + 1) * BLOCK)
            before = part_ref if k == 0 else out_ref
            out_ref[at, :] = (value + before[at, :].astype(f32)).astype(bf16)

        unsort_rows(bounds, rows_far[k], [2 + 2 * k, 3 + 2 * k], blocks, pick, moved, emit)


def unpack(bounds, theirs, rows_far, lasts, parts, part, backs):
    points, width = part.shape
    blocks = points // BLOCK
    far = len(theirs)
    extra = far * len(lasts)
    return pl.pallas_call(
        functools.partial(unpack_kernel, far, blocks, lasts),
        in_specs=specs("s" + "s" * far + "v" * (2 * far + extra + 1)),
        out_specs=specs("v" * (1 + far)),
        out_shape=[jax.ShapeDtypeStruct(part.shape, bf16)] + [pltpu.VMEM(b.shape, bf16) for b in backs],
        input_output_aliases={2 * far + extra + 2 + k: 1 + k for k in range(far)},
        scratch_shapes=[pltpu.VMEM((blocks * window_rows(2, 128) + WIN, width), bf16)],
        compiler_params=params(20),
        cost_estimate=cost("unpack"),
        name="unpack",
    )(bounds, *theirs, *rows_far, *[keep(x) for x in parts], keep(part), *[keep(b) for b in backs])[0]


def join(cap, kxs, oct_axis, lox_ref, lo_hbm, sem, go):
    other = lax.axis_index(oct_axis) ^ 1
    for n, k in enumerate(kxs):
        at = pl.ds(pl.multiple_of((other ^ (2 * k)) * cap, cap), cap)
        go(pltpu.make_async_copy(lox_ref.at[pl.ds(n * cap, cap), :], lo_hbm.at[at, :], sem.at[n]))


def merge_kernel(cap, kxs, oct_axis, lox_ref, lo_in, lo_hbm, sem):
    for go in (go_start, go_wait):
        join(cap, kxs, oct_axis, lox_ref, lo_hbm, sem, go)


def merge(lox, lo, cap, kxs):
    return pl.pallas_call(
        functools.partial(merge_kernel, cap, tuple(kxs), "oct"),
        in_specs=specs("va"),
        out_specs=specs("a")[0],
        out_shape=pltpu.HBM(lo.shape, lo.dtype),
        input_output_aliases={1: 0},
        scratch_shapes=[pltpu.SemaphoreType.DMA((len(kxs),))],
        compiler_params=params(4),
        cost_estimate=cost("merge"),
        name="merge",
    )(keep(lox), stay(lo))


def column_block(axes, n):
    a, b = (lax.axis_index(axis) % 2 for axis in axes)
    return (a ^ (n % 2)) * 2 + (b ^ (n // 2))


def collect_kernel(axes, shape_axis, oct_axis, shapes, span, extra, blocks, cap, message, usual, steps, *refs):
    mine, refs = refs[0], refs[1:]
    theirs, olds, refs = refs[:extra], refs[extra : 2 * extra], refs[2 * extra :]
    gw_ref, info_ref, codes_ref, lo_in, lof_in, outs, lo_hbm, lof_hbm, full, sem = *refs[:5], refs[5:9], *refs[9:]
    source = lax.axis_index(oct_axis)

    def store(go):
        for k in range(extra):
            rows = rows_of(theirs[k], 0, blocks, source ^ (2 * k + 2), cap, k, 0)
            for u in range(message[1]):
                rows.store(message[0] + u, lo_hbm, lof_hbm, olds[k], u * TILE, sem, go)

    store(go_start)
    width = gw_ref.shape[0] - 16
    cols = gw_ref.shape[1]
    code_width = codes_ref.shape[1]
    base = lax.axis_index(shape_axis) * span
    full[:width, :] = gw_ref[:width, :]
    ps = jnp.zeros((shapes, cols), f32)
    for s in range(span):
        ps = ps + jnp.where(iota((shapes, 1), 0) == base + s, gw_ref[width + s : width + s + 1, :], 0.0)
    full[width : width + shapes, :] = ps
    flag = jnp.int32(0)
    for k in range(extra):
        ours = tiles_of(mine, 2 + 2 * k, blocks)
        other = tiles_of(theirs[k], 0, blocks, 0)
        most = jnp.maximum(jnp.maximum(ours, LEAD) + other, jnp.maximum(other, LEAD) + ours)
        flag = flag | ((jnp.maximum(ours, other) > usual) | (most > steps)).astype(i32)
    flag = flag.astype(f32)
    lane = iota((1, cols - code_width), 1)
    info = jnp.zeros((shapes, cols), f32)
    for s in range(span):
        number = info_ref[s : s + 1, :1]
        high = jnp.floor(number / 1024.0)
        mid = jnp.floor((number - 1024.0 * high) / 32.0)
        low = number - 1024.0 * high - 32.0 * mid
        digits = jnp.where(lane < 64, low, jnp.where(lane < 128, mid, jnp.where(lane < 192, high, flag)))
        code = jnp.where(lax.axis_index(oct_axis) == 0, codes_ref[s : s + 1, :].astype(f32), 0.0)
        info = info + jnp.where(iota((shapes, 1), 0) == base + s, jnp.concatenate([code, digits], axis=1), 0.0)
    full[width + shapes : width + 2 * shapes, :] = info
    for n in range(4):
        at = pl.ds(pl.multiple_of(column_block(axes, n) * 128, 128), 128)
        outs[n][...] = full[:, at].astype(bf16)
    store(go_wait)


def halves(x):
    high = x.astype(bf16)
    return high, (x - high.astype(f32)).astype(bf16)


def finish_kernel(axes, shape_axis, hid, span, categories, momentum, *refs):
    parts, refs = refs[:4], refs[4:]
    direction_ref, gain_ref, norm_ref, w_ref, mean_ref, var_ref, refs = *refs[:6], refs[6:]
    dg_ref, gg_ref, bg_ref, cg_ref, mean_out, var_out, left_ref, full = refs
    for n in range(4):
        at = pl.ds(pl.multiple_of(column_block(axes, n) * 128, 128), 128)
        full[:, at] = parts[n][...].astype(f32)
    ins, cols = direction_ref.shape
    cats, code_width = mean_ref.shape
    shapes = (full.shape[0] - (ins - code_width)) // 2
    width = ins - code_width
    ps = full[width : width + shapes, :]
    info = full[width + shapes : width + 2 * shapes, :]
    codes = info[:, :code_width]
    at = code_width
    number = info[:, at : at + 1] + 32.0 * info[:, at + 64 : at + 65] + 1024.0 * info[:, at + 128 : at + 129]
    for c in range(cats):
        chosen = jnp.zeros((shapes, 1), f32)
        for s in range(shapes):
            chosen = jnp.where((iota((shapes, 1), 0) == s) & (categories[s] == c), 1.0, chosen)
        weight = chosen * number
        count = jnp.sum(weight, axis=0, keepdims=True)
        mean = jnp.sum(weight * codes, axis=0, keepdims=True) / count
        var = jnp.sum(weight * codes * codes, axis=0, keepdims=True) / count - mean * mean
        rate = momentum[c]
        mean_out[c : c + 1, :] = (1.0 - rate) * mean_ref[c : c + 1, :] + rate * mean
        var_out[c : c + 1, :] = (1.0 - rate) * var_ref[c : c + 1, :] + rate * var

    gw = full[:width, :]
    codes_all = jnp.concatenate(
        [jnp.zeros((shapes, hid), f32), codes, jnp.zeros((shapes, ins - hid - code_width), f32)], axis=1
    )
    high, low = halves(ps)
    wg = lax.dot_general(jnp.concatenate([codes_all, codes_all], axis=0).astype(bf16), jnp.concatenate([high, low], axis=0),
                         (((0,), (0,)), ((), ())), preferred_element_type=f32)
    head = jnp.where(iota((width, 1), 0) < hid, gw, wg[:width])
    tail = jnp.where(iota((8, 1), 0) + (width - 8) >= hid, gw[width - 8 :], wg[ins - 8 :])
    wg = jnp.concatenate([head, wg[width : ins - 8], tail], axis=0)
    direction = direction_ref[...]
    norms = norm_ref[...]
    dots = jnp.sum(wg * direction, axis=0, keepdims=True)
    gg_ref[...] = dots / norms
    dg_ref[...] = (gain_ref[...] / norms) * (wg - direction * (dots / (norms * norms)))
    bg_ref[...] = jnp.sum(ps, axis=0, keepdims=True)
    base = lax.axis_index(shape_axis) * span
    own = jnp.zeros((8, cols), f32)
    for s in range(span):
        row = jnp.sum(jnp.where(iota((shapes, 1), 0) == base + s, ps, 0.0), axis=0, keepdims=True)
        own = own + jnp.where(iota((8, 1), 0) == s, row, 0.0)
    both = lax.dot_general(jnp.concatenate(halves(own), axis=0), w_ref[...], (((1,), (1,)), ((), ())), preferred_element_type=f32)
    cg_ref[...] = (both[:8] + both[8:])[:span, hid : hid + code_width]
    left_ref[0] = jnp.max(info[:, at + 192 :])


def finish(axes, span, categories, momentum, parts, direction, gain, norms, weight, prev_mean, prev_var):
    ins, outs = direction.shape
    return pl.pallas_call(
        functools.partial(finish_kernel, axes, "shape", HID, span),
        in_specs=specs("ss" + "v" * 10),
        out_specs=specs("v" * 6 + "s"),
        out_shape=[
            jax.ShapeDtypeStruct((ins, outs), f32),
            jax.ShapeDtypeStruct((1, outs), f32),
            jax.ShapeDtypeStruct((1, outs), f32),
            jax.ShapeDtypeStruct((span, prev_mean.shape[1]), f32),
            jax.ShapeDtypeStruct(prev_mean.shape, f32),
            jax.ShapeDtypeStruct(prev_mean.shape, f32),
            jax.ShapeDtypeStruct((1,), f32),
        ],
        scratch_shapes=[pltpu.VMEM((parts[0].shape[0], outs), f32)],
        compiler_params=params(12),
        cost_estimate=cost("finish"),
        name="finish",
    )(categories, momentum, *[keep(p) for p in parts], keep(direction), keep(gain), keep(norms), keep(weight), prev_mean, prev_var)


def swap(v, axis, k):
    n = lax.axis_size(axis)
    return lax.ppermute(v, axis, [(i, i ^ k) for i in range(n)])


def swap_both(v, k):
    n, m = lax.axis_size("shape"), lax.axis_size("oct")
    return lax.ppermute(v, ("shape", "oct"), [(i, i ^ k) for i in range(n * m)])


def bits(axis, first):
    n = lax.axis_size(axis)
    return [(axis, 1 << j) for j in range(first, n.bit_length() - 1)]


def after(x, *others):
    return lax.optimization_barrier((x, *others))[0]


def quarters_to(parts):
    m = lax.axis_size("oct")
    return [swap(parts[0], "oct", 1), swap(parts[1], "shape", 1), swap_both(parts[2], m + 1)]


def total_quarter(parts, before):
    got = quarters_to(parts[1:])
    v = parts[0].astype(f32) + got[0].astype(f32) + got[1].astype(f32) + after(got[2], *before[0]).astype(f32)
    v = v.astype(bf16)
    yield v
    for n, (axis, k) in enumerate(bits("shape", 1) + bits("oct", 1)):
        v = (v.astype(f32) + after(swap(v, axis, k), *before[n + 1]).astype(f32)).astype(bf16)
        yield v


AXES = ("oct", "shape")


def collect(mine, theirs, olds, gw, info, codes, lo, lof, shapes, blocks, cap, message, usual, steps):
    span = codes.shape[0]
    far = len(theirs)
    rows = gw.shape[0] - 16 + 2 * shapes
    out = pl.pallas_call(
        functools.partial(collect_kernel, AXES, "shape", "oct", shapes, span, far, blocks, cap, message, usual, steps),
        in_specs=specs("s" + "s" * far + "v" * far + "vvvaa"),
        out_specs=specs("vvvvaa"),
        out_shape=[pltpu.VMEM((rows, 128), bf16)] * 4 + [pltpu.HBM(lo.shape, bf16), pltpu.HBM(lof.shape, bf16)],
        input_output_aliases={2 * far + 4: 4, 2 * far + 5: 5},
        scratch_shapes=[pltpu.VMEM((rows, gw.shape[1]), f32), pltpu.SemaphoreType.DMA],
        compiler_params=params(8),
        cost_estimate=cost("collect"),
        name="collect",
    )(mine, *theirs, *[keep(o) for o in olds], keep(gw), info, codes, stay(lo), stay(lof))
    return out[:4], out[4], out[5]


def run(usual, steps, point_inputs, shape_ids, octants, categories, codes, direction, gain, bias, cotangent, prev_mean, prev_var, momentum):
    points, width = point_inputs.shape
    oct_count, shape_dev = lax.axis_size("oct"), lax.axis_size("shape")
    cap = 2 * points // oct_count
    span, code_width = codes.shape
    shapes = shape_dev * span
    blocks = points // BLOCK
    far = list(range(1, oct_count // 2))
    messages = plan_messages(usual, steps)
    points_in = [m for m, (first, _) in enumerate(messages) if first < usual]

    (ct_near, ct_far, x_near), heads, queues, rows_far, (row_near, mine, labels, pos) = pack(
        octants, shape_ids, point_inputs, cotangent, messages, oct_count, span, cap)
    ctn, ctf = swap(ct_near, "oct", 1), swap(ct_far, "oct", 1)
    got = {(k, m): swap(heads[2 * (k - 1) + m], "oct", 2 * k) for k in far for m in range(2)}
    gw, buf, wp, wpt, weight, cb, norms, direction_v, gain_v, near_names, info = prepare(
        mine, row_near, labels, pos, x_near, direction, gain, bias, codes, oct_count, cap)
    weights = (wp, wpt, cb)
    lo, lon, lof, gw, buf = local(mine, near_names, cotangent, ctn, weights, gw, buf, len(far), blocks, span, cap)

    queue = {k: queues[k - 1] for k in far}
    named, theirs, back, ahead = {}, {}, {}, {}
    for k in far:
        named[k], theirs[k], back[k] = make_names(after(got[k, 0], gw)[messages[0][1] * TILE :], k, span, cap)
        ahead[k] = ()
    for m in points_in:
        for k in far:
            (queue[k], lo, lof, gw, back[k]), payloads, ahead[k] = far_step(
                messages, m, points_in, k, mine, theirs[k], named[k], got[k, m], cotangent, ctf, weights,
                (queue[k], lo, lof, gw, back[k]), ahead[k], blocks, span, cap)
            for j, payload in enumerate(payloads):
                got[k, m + 2 + j] = swap(payload, "oct", 2 * k)
        if m == min(1, points_in[-1] - 1):
            part, lo = unlocal(mine, row_near, after(buf, gw), swap(lon, "oct", 1), lo, cap)
            gw = after(gw, part)
    their = [theirs[k] for k in far]
    lasts = list(range(len(points_in), len(messages)))
    order = ((), (0,), (), (1,)) if len(lasts) == 2 else ()
    before = [[got[k, lasts[i]] for k in far for i in ii] for ii in order] + [[] for _ in range(20)]
    parts, lo, lof = collect(mine, their, [ahead[k][-1] for k in far], gw, info, codes, lo, lof, shapes, blocks, cap,
                             messages[points_in[-1]], usual, steps)
    lox = swap(lof, "oct", 1)
    input_grad = unpack(mine, their, rows_far, [messages[m] for m in lasts], [got[k, m] for k in far for m in lasts], part,
                        [back[k] for k in far])
    for v in total_quarter(parts, before):
        pass
    parts = [v] + quarters_to([v] * 3)
    lo = merge(lox, lo, cap, far)
    direction_grad, gain_grad, bias_grad, code_grad, running_mean, running_var, left = finish(
        AXES, span, categories, momentum, [after(parts[0], lo, input_grad)] + parts[1:], direction_v, gain_v, norms, weight, prev_mean, prev_var)
    outputs = (
        lo,
        input_grad,
        code_grad,
        direction_grad,
        gain_grad[0],
        bias_grad[0],
        running_mean,
        running_var,
    )
    return outputs, left[0]


def body(*args):
    points, oct_count = args[0].shape[0], lax.axis_size("oct")
    most = 2 * (2 * points // oct_count) // TILE
    all_steps = max(most, LEAD) + most
    usual, steps = min(USUAL, most), min(STEPS, all_steps)
    outputs, left = run(usual, steps, *args)
    if (usual, steps) == (most, all_steps):
        return outputs

    def more(carry):
        return jnp.float32(0), run(most, all_steps, *args)[0]

    return lax.while_loop(lambda carry: carry[0] > 0, more, (left, outputs))[1]


def solution(mesh):
    both = P(("shape", "oct"), None)
    in_specs = (both, P(("shape", "oct")), both, P(), P("shape", None), P(), P(), P(), both, P(), P(), P())
    out_specs = (both, both, P("shape", None), P(), P(), P(), P(), P())
    return jax.shard_map(body, mesh=mesh, in_specs=in_specs, out_specs=out_specs, check_vma=False)
```

```python
import functools

import jax
import jax.numpy as jnp
from jax import lax
from jax.experimental import pallas as pl
from jax.experimental.pallas import tpu as pltpu
from jax.sharding import PartitionSpec as P

HID = 253
CATS = 5
BLOCK = 256
TILE = 256
ALIGN = 64
UNIT = 2 * TILE
WIN = BLOCK + 16
LEAD = 8
USUAL = 13
STEPS = 21
PART = 4
FAR = 1 << 20

norm_eps = 1e-06
COSTS = dict(pack=30, prepare=30, local=30, unlocal=0.01, names=30, far=30, last=0.01, flush=0.01, unpack=30, merge=0.01, finish=30, collect=0.01)


def cost(name):
    return pl.CostEstimate(flops=max(1, int(COSTS[name] * 10**9)), bytes_accessed=1, transcendentals=0)


f32, bf16, i32 = jnp.float32, jnp.bfloat16, jnp.int32


def params(mib):
    return pltpu.CompilerParams(vmem_limit_bytes=mib * 1024 * 1024)


def keep(x):
    return pltpu.with_memory_space_constraint(x, pltpu.VMEM)


def stay(x):
    return pltpu.with_memory_space_constraint(x, pltpu.HBM)


def specs(text):
    kinds = {"v": pltpu.VMEM, "s": pltpu.SMEM, "a": pl.ANY}
    return [pl.BlockSpec(memory_space=kinds[c]) for c in text]


def iota(shape, dim):
    return lax.broadcasted_iota(i32, shape, dim)


def plan_messages(usual, steps):
    cuts = list(range(0, usual, PART)) + list(range(usual, steps, PART)) + [steps]
    if usual % PART == 1:
        cuts[usual // PART] -= 1
    return [(a, b - a) for a, b in zip(cuts, cuts[1:])]


def ceil_to(n, step):
    return -(-n // step) * step


def plan(labels, groups, span):
    rows = labels.shape[0]
    count = len(groups)
    mask = jnp.concatenate([(labels >= g * span) & (labels < (g + 1) * span) for g in groups], axis=0)
    one = jnp.where(mask, 1.0, 0.0)
    m = one.astype(bf16)
    total = count * rows
    upper = jnp.where(iota((BLOCK, BLOCK), 0) <= iota((BLOCK, BLOCK), 1), 1.0, 0.0).astype(bf16)
    cum = jnp.dot(m, upper, preferred_element_type=f32)
    a, b = iota((total, total), 0), iota((total, total), 1)
    lower = jnp.where((a // rows == b // rows) & (b < a), 1.0, 0.0).astype(bf16)
    tot = jnp.sum(one, axis=1, keepdims=True)
    base = jnp.dot(lower, jnp.broadcast_to(tot, (total, 128)).astype(bf16), preferred_element_type=f32)[:, :1]
    lo, hi = base.astype(i32), (base + tot).astype(i32)
    pos = jnp.where(mask, lo + cum.astype(i32) - 1, -FAR)
    tot_row = lax.dot_general(jnp.ones((8, BLOCK), bf16), m, (((1,), (1,)), ((), ())), preferred_element_type=f32)
    base_row = lax.dot_general(tot_row.astype(bf16), lower, (((1,), (1,)), ((), ())), preferred_element_type=f32)
    return pos, lo, hi, base_row.astype(i32), (base_row + tot_row).astype(i32)


def sorted_rows(pos, lo, hi, rows, first, count):
    row, at = None, 0
    for n in range(first, first + count):
        s = slice(n * rows, (n + 1) * rows)
        start = lo[s] // 16 * 16
        r = pos[s] + (at - start)
        row = r if row is None else jnp.maximum(row, r)
        at = at + (hi[s] + 15) // 16 * 16 - start
    return row


def ahead_by(v, step):
    rows, lanes = v.shape
    if step >= lanes:
        return pltpu.roll(v, rows - step // lanes, 0)
    moved = pltpu.roll(v, lanes - step, 1)
    return jnp.where(iota((rows, lanes), 1) < lanes - step, moved, pltpu.roll(moved, rows - 1, 0))


def back_by(v, step):
    rows, lanes = v.shape
    if step >= lanes:
        return pltpu.roll(v, step // lanes, 0)
    moved = pltpu.roll(v, step, 1)
    return jnp.where(iota((rows, lanes), 1) >= step, moved, pltpu.roll(moved, 1, 0))


def squeeze(pos, labels, group, span):
    rows, lanes = pos.shape
    at = iota((rows, lanes), 0) * lanes + iota((rows, lanes), 1)
    v = jnp.where(pos >= 0, (at - pos) * 16 + (labels - group * span + 1), 0)
    for bit in range((rows * lanes).bit_length() - 1):
        go = jnp.where(((v >> (4 + bit)) & 1) == 1, v, 0)
        v = v - go + ahead_by(go, 1 << bit)
    return v & 15


def stream_names(pos, labels, group, span, cap):
    rows = labels.shape[0]
    first, second = (squeeze(pos[n * rows : (n + 1) * rows], labels, group + n, span) for n in range(2))
    one = jnp.where(pos[:rows] >= 0, 1.0, 0.0)
    count = jnp.sum(jnp.sum(one, axis=1, keepdims=True), axis=0, keepdims=True).astype(i32)
    skip = (count + (ALIGN - 1)) // ALIGN * ALIGN
    step = ALIGN
    while step <= cap:
        second = jnp.where((skip & step) > 0, back_by(second, step), second)
        step *= 2
    return first + second


def filled(bounds, group, blocks, row=1):
    return (bounds[row, (group + 1) * blocks - 1] + (ALIGN - 1)) // ALIGN * ALIGN


def tiles_of(bounds, group, blocks, row=1):
    return (filled(bounds, group, blocks, row) + filled(bounds, group + 1, blocks, row) + (TILE - 1)) // TILE


def spans(bounds, groups, blocks, b):
    at, result = 0, []
    for g in groups:
        lo, hi = bounds[0, g * blocks + b], bounds[1, g * blocks + b]
        first = pl.multiple_of(lo // 16 * 16, 16)
        result.append((first, pl.multiple_of(at, 16) if result else 0, lo - first))
        at = at + ((hi + 15) // 16 * 16 - first)
    return result


def window_rows(count, step):
    return ceil_to(BLOCK + 30 * count, step)


def sort_rows(bounds, row_ref, x_ref, groups, blocks, moved, put):
    rows = window_rows(len(groups), 64)
    for b in range(blocks):
        hot = jnp.where(iota((rows, BLOCK), 0) == row_ref[b : b + 1, :], 1.0, 0.0).astype(bf16)
        out = jnp.dot(hot, x_ref[b * BLOCK : (b + 1) * BLOCK, :], preferred_element_type=f32).astype(bf16)
        moved[b * rows : (b + 1) * rows, :] = out
    moved[blocks * rows :, :] = jnp.zeros((moved.shape[0] - blocks * rows, moved.shape[1]), bf16)
    for n in range(len(groups)):
        for b in range(blocks):
            first, at, over = spans(bounds, groups, blocks, b)[n]
            dst, start = put(n, first)
            at = at + b * rows
            old = dst[pl.ds(start, 16), :]
            new = moved[pl.ds(pl.multiple_of(at, 16), 16), :]
            dst[pl.ds(start, 16), :] = jnp.where(iota((16, 1), 0) < over, old, new)
            rest = pl.ds(pl.multiple_of(start + 16, 16), BLOCK)
            dst[rest, :] = moved[pl.ds(pl.multiple_of(at + 16, 16), BLOCK), :]


def unsort_rows(bounds, row_ref, groups, blocks, pick, moved, emit):
    rows = window_rows(len(groups), 128)
    for b in range(blocks):
        moved[b * rows + WIN : (b + 1) * rows, :] = jnp.zeros((rows - WIN, moved.shape[1]), bf16)
        for n, (first, at, _) in enumerate(spans(bounds, groups, blocks, b)):
            moved[pl.ds(pl.multiple_of(at + b * rows, 16), WIN), :] = pick(n, first, WIN)
    for b in range(blocks):
        hot = jnp.where(iota((rows, BLOCK), 0) == row_ref[b : b + 1, :], 1.0, 0.0).astype(bf16)
        emit(b, jnp.dot(jnp.transpose(hot), moved[b * rows : (b + 1) * rows, :], preferred_element_type=f32))


def layer_tile(x, named, ct, wp_ref, wpt_ref, cb_ref, gw_ref, span):
    rows = x.shape[0]
    col = jnp.transpose(jnp.broadcast_to(named.astype(f32), (8, rows)))[:, :1]
    pre = jnp.dot(x, wp_ref[...], preferred_element_type=f32)
    add = cb_ref[0:1, :]
    for s in range(1, span):
        add = jnp.where(col == s + 1.0, cb_ref[s : s + 1, :], add)
    pre = pre + add
    valid = col > 0.0
    e = jnp.exp(-jnp.abs(pre))
    soft = jnp.maximum(pre, 0.0) + jnp.where(e < 2.0**-12, e, jnp.log(1.0 + e))
    sig = jnp.exp(pre - soft)
    lo = jnp.where(valid, soft, 0.0).astype(bf16)
    gp = jnp.where(valid, ct.astype(f32) * sig, 0.0).astype(bf16)
    gx = jnp.dot(gp, wpt_ref[...], preferred_element_type=f32).astype(bf16)
    sel = jnp.where(jnp.broadcast_to(named, (16, rows)) == iota((16, rows), 0) + 1, 1.0, 0.0).astype(bf16)
    left = jnp.concatenate([jnp.transpose(x), sel], axis=0)
    gw_ref[...] += jnp.dot(left, gp, preferred_element_type=f32)
    return lo, gx


def pack_kernel(oct_count, sizes, shape_axis, oct_axis, span, cap, octants_hbm, ids_hbm, x_hbm, ct_hbm, *refs):
    far = oct_count // 2 - 1
    octants_ref, ids_ref, in_sem, ct_sem = refs[-4:]
    refs = refs[:-4]
    ct_near, ct_far, x_ref, refs = *refs[:3], refs[3:]
    other = lax.axis_index(oct_axis) ^ 1
    blocks_out = []
    for k in range(oct_count // 2):
        there = ct_hbm.at[pl.ds(pl.multiple_of((other ^ (2 * k)) * cap, cap), cap), :]
        here = ct_far.at[pl.ds((k - 1) * cap, cap), :] if k else ct_near
        blocks_out.append(pltpu.make_async_copy(there, here, ct_sem.at[k]))
    fetches = [
        pltpu.make_async_copy(a, b, in_sem.at[i])
        for i, (a, b) in enumerate(zip((octants_hbm, ids_hbm, x_hbm), (octants_ref, ids_ref, x_ref)))
    ]
    for f in fetches + blocks_out:
        f.start()
    heads, refs = refs[: 2 * far], refs[2 * far :]
    queues, rows_far, refs = refs[:far], refs[far : 2 * far], refs[2 * far :]
    row_near, bounds_ref, labels_ref, pos_ref, moved, bounds_v, bounds, sem = refs
    blocks = row_near.shape[0]
    me = lax.axis_index(oct_axis)
    first_shape = lax.axis_index(shape_axis) * span

    def wide(ref):
        return jnp.concatenate([ref[pl.ds(h, blocks, 2), :] for h in range(2)], axis=1)

    for f in fetches[:2]:
        f.wait()
    ids = wide(ids_ref) - first_shape
    labels = (wide(octants_ref) ^ me) * span + ids
    pos, lo, hi, first_row, last_row = plan(labels, range(oct_count), span)
    n = oct_count * blocks
    bounds_v[...] = jnp.zeros(bounds_v.shape, i32)
    bounds_v[0:1, :n] = first_row[:1]
    bounds_v[1:2, :n] = last_row[:1]
    bounds_ref[...] = bounds_v[...]
    copy = pltpu.make_async_copy(bounds_v, bounds, sem)
    copy.start()
    row_near[...] = sorted_rows(pos, lo, hi, blocks, 0, 2)
    for k in range(far):
        rows_far[k][...] = sorted_rows(pos, lo, hi, blocks, 2 + 2 * k, 2)
    labels_ref[...] = labels
    pos_ref[...] = pos[: 2 * blocks]
    for k in range(far):
        queues[k][...] = jnp.zeros(queues[k].shape, bf16)
    copy.wait()
    fetches[2].wait()
    for k in range(far):
        groups = [2 + 2 * k, 3 + 2 * k]
        cut = filled(bounds, groups[0], blocks)
        sort_rows(bounds, rows_far[k], x_ref, groups, blocks, moved,
                  lambda n, first: (queues[k], pl.multiple_of(first + n * cut, 16)))
        heads[2 * k][: sizes[0], :] = queues[k][: sizes[0], :]
        heads[2 * k][sizes[0] :, :] = labels.astype(f32).astype(bf16)
        heads[2 * k + 1][...] = queues[k][sizes[0] : sizes[0] + sizes[1], :]
    for f in blocks_out:
        f.wait()


def pack(octants, ids, points, cotangent, messages, oct_count, span, cap):
    count, width = points.shape
    blocks = count // BLOCK
    far = oct_count // 2 - 1
    shape = jax.ShapeDtypeStruct
    sizes = [n * TILE for _, n in messages[:2]]
    heads = [pltpu.VMEM((sizes[0] + blocks, width), bf16), pltpu.VMEM((sizes[1], width), bf16)] * far
    cols = cotangent.shape[1]
    outs = [pltpu.VMEM((cap, cols), bf16), pltpu.VMEM((far * cap, cols), bf16), pltpu.VMEM(points.shape, bf16)] + heads + [pltpu.VMEM((4 * cap, width), bf16)] * far
    outs += [shape((blocks, BLOCK), i32)] * (far + 1)
    outs += [shape((8, 128), i32), shape((blocks, BLOCK), i32), shape((2 * blocks, BLOCK), i32)]
    out = pl.pallas_call(
        functools.partial(pack_kernel, oct_count, sizes, "shape", "oct", span, cap),
        in_specs=specs("aaaa"),
        out_specs=specs("v" * len(outs)),
        out_shape=outs,
        scratch_shapes=[
            pltpu.VMEM((blocks * window_rows(2, 64) + WIN, width), bf16),
            pltpu.VMEM((8, 128), i32),
            pltpu.SMEM((8, 128), i32),
            pltpu.SemaphoreType.DMA,
            pltpu.VMEM((count // 128, 128), i32),
            pltpu.VMEM((count // 128, 128), i32),
            pltpu.SemaphoreType.DMA((3,)),
            pltpu.SemaphoreType.DMA((oct_count // 2,)),
        ],
        compiler_params=params(16),
        cost_estimate=cost("pack"),
        name="pack",
    )(stay(octants.reshape(-1, 128)), stay(ids.reshape(-1, 128)), stay(points), stay(cotangent))
    x, out = out[:3], out[3:]
    heads, queues, rows_far, out = out[: 2 * far], out[2 * far : 3 * far], out[3 * far : 4 * far], out[4 * far :]
    return x, heads, queues, rows_far, out


def set_weights(hid, direction_ref, gain_ref, bias_ref, codes_ref, wp_ref, wpt_ref, w_ref, cb_ref, norm_ref):
    direction = direction_ref[...]
    norms = jnp.sqrt(jnp.sum(direction * direction, axis=0, keepdims=True) + norm_eps)
    weight = (direction * (gain_ref[...] / norms)).astype(bf16)
    norm_ref[...] = norms
    w_ref[...] = weight
    width = wp_ref.shape[0]
    wf = weight.astype(f32)
    last = jnp.where(iota((8, 1), 0) + (width - 8) < hid, wf[width - 8 : width, :], wf[-8:, :])
    wp = jnp.concatenate([wf[: width - 8, :], last], axis=0)
    wp_ref[...] = wp.astype(bf16)
    wpt_ref[...] = wp.T.astype(bf16)
    span, code_width = codes_ref.shape
    w_code = wf[hid : hid + code_width, :].astype(bf16)
    codes = jnp.concatenate([codes_ref[...].astype(f32), jnp.zeros((8 - span, code_width), f32)], axis=0).astype(bf16)
    cb_ref[...] = jnp.dot(codes, w_code, preferred_element_type=f32) + bias_ref[...]


def prepare_kernel(oct_count, oct_axis, span, cap, bounds, row_ref, labels_ref, pos_ref, x_ref, codes_v, direction_hbm, gain_hbm, bias_hbm,
                   gw_ref, buf, wp_ref, wpt_ref, w_ref, cb_ref, norm_ref, direction_v, gain_v,
                   names_ref, info_ref, moved, bias_v, in_sem):
    blocks = row_ref.shape[0]
    cut = [filled(bounds, r, blocks) for r in range(2)]
    fetches = [
        pltpu.make_async_copy(a, b, in_sem.at[i])
        for i, (a, b) in enumerate(((direction_hbm, direction_v), (gain_hbm, gain_v), (bias_hbm, bias_v)))
    ]
    for f in fetches:
        f.start()

    gw_ref[...] = jnp.zeros(gw_ref.shape, f32)
    buf[...] = jnp.zeros(buf.shape, bf16)
    sort_rows(bounds, row_ref, x_ref, [0, 1], blocks, moved,
              lambda n, first: (buf, pl.multiple_of(first + n * cut[0], 16)))
    labels = labels_ref[...]
    names_ref[...] = stream_names(pos_ref[...], labels, 0, span, cap)
    ids = labels % span
    info_ref[...] = jnp.zeros(info_ref.shape, f32)
    for s in range(span):
        number = jnp.sum(jnp.sum(jnp.where(ids == s, 1.0, 0.0), axis=1, keepdims=True), axis=0, keepdims=True)
        info_ref[s : s + 1, :] = jnp.broadcast_to(number, (1, 128))
    for f in fetches:
        f.wait()
    set_weights(HID, direction_v, gain_v, bias_v, codes_v, wp_ref, wpt_ref, w_ref, cb_ref, norm_ref)


def prepare(bounds, row, labels, pos, points, direction, gain, bias, codes, oct_count, cap):
    width = points.shape[1]
    ins, outs = direction.shape
    blocks = row.shape[0]
    return pl.pallas_call(
        functools.partial(prepare_kernel, oct_count, "oct", codes.shape[0], cap),
        in_specs=specs("svvvvvaaa"),
        out_specs=specs("vvvvvvvvvvv"),
        out_shape=[
            pltpu.VMEM((width + 16, outs), f32),
            pltpu.VMEM((2 * cap + BLOCK + WIN, width), bf16),
            pltpu.VMEM((width, outs), bf16),
            pltpu.VMEM((outs, width), bf16),
            pltpu.VMEM((ins, outs), bf16),
            pltpu.VMEM((8, outs), f32),
            pltpu.VMEM((1, outs), f32),
            pltpu.VMEM((ins, outs), f32),
            pltpu.VMEM((1, outs), f32),
            pltpu.VMEM(row.shape, i32),
            pltpu.VMEM((8, 128), f32),
        ],
        scratch_shapes=[
            pltpu.VMEM((blocks * window_rows(2, 64) + WIN, width), bf16),
            pltpu.VMEM((1, outs), f32),
            pltpu.SemaphoreType.DMA((3,)),
        ],
        compiler_params=params(14),
        cost_estimate=cost("prepare"),
        name="prepare",
    )(bounds, row, labels, pos, keep(points), codes, stay(direction), stay(gain[None, :]), stay(bias[None, :]))


class Rows:
    def __init__(self, cut, source, cap, place):
        self.cut, self.own_at, self.other_at = cut, source * cap, place * cap
        self.total = cut[0] + cut[1]
        self.tiles = (self.total + (TILE - 1)) // TILE

    def move(self, tile, own, other, mine, mine_at, sem, out, go):
        first = tile * TILE
        cut, total = self.cut[0], self.total

        def one(at, rows, second):
            here = mine.at[pl.ds(mine_at + at, rows), :]
            row = first + at
            there = other if second else own
            start = self.other_at + row - cut if second else self.own_at + row
            there = there.at[pl.ds(pl.multiple_of(start, ALIGN), rows), :]
            go(pltpu.make_async_copy(here, there, sem) if out else pltpu.make_async_copy(there, here, sem))

        whole = first + TILE <= cut
        last = (first >= cut) & (first + TILE <= total)
        pl.when(whole)(lambda: one(0, TILE, False))
        pl.when(last)(lambda: one(0, TILE, True))

        @pl.when((first < total) & jnp.logical_not(whole | last))
        def _():
            for at in range(0, TILE, ALIGN):
                pl.when(first + at < cut)(lambda: one(at, ALIGN, False))
                pl.when((first + at >= cut) & (first + at < total))(lambda: one(at, ALIGN, True))

    def fetch(self, tile, ct, ctx, mine, at, sem, go):
        self.move(tile, ct, ctx, mine, at, sem, False, go)

    def store(self, tile, lo, lox, mine, at, sem, go):
        self.move(tile, lo, lox, mine, at, sem, True, go)


def rows_of(bounds, group, blocks, source, cap, place, row=1):
    return Rows([filled(bounds, group + r, blocks, row) for r in range(2)], source, cap, place)


def names_at(names_ref, tile, number):
    return jnp.concatenate([names_ref[pl.ds(tile + i, 1), :] for i in range(number)], axis=1)


def go_start(copy):
    copy.start()


def go_wait(copy):
    copy.wait()


def local_kernel(oct_axis, far, blocks, span, cap, bounds, *refs):
    names_ref, ct_hbm, ctx_ref, wp_ref, wpt_ref, cb_ref, gw_in, buf_in, refs = *refs[:8], refs[8:]
    lo_hbm, lon_hbm, lof_hbm, gw_ref, buf, refs = *refs[:5], refs[5:]
    ct_v, lo_v, zero, ct_sem, lo_sem, zero_sem = refs
    source = lax.axis_index(oct_axis)
    near = rows_of(bounds, 0, blocks, source, cap, 0)
    count = (near.tiles + (PART - 1)) // PART

    def clear(go):
        def empty(array, at, t, cut):
            pl.when(t * TILE >= cut)(lambda: go(pltpu.make_async_copy(zero, array.at[pl.ds(pl.multiple_of(at + t * TILE, TILE), TILE), :], zero_sem)))

            @pl.when((t * TILE < cut) & ((t + 1) * TILE > cut))
            def _():
                for q in range(0, TILE, ALIGN):
                    @pl.when(t * TILE + q >= cut)
                    def _():
                        rows = pl.ds(pl.multiple_of(at + t * TILE + q, ALIGN), ALIGN)
                        go(pltpu.make_async_copy(zero.at[pl.ds(0, ALIGN), :], array.at[rows, :], zero_sem))

        for t in range(cap // TILE):
            empty(lo_hbm, source * cap, t, near.cut[0])
            empty(lon_hbm, 0, t, near.cut[1])
        for k in range(1, far + 1):
            for t in range(cap // TILE):
                at = (source ^ (2 * k)) * cap + t * TILE
                go(pltpu.make_async_copy(zero, lo_hbm.at[pl.ds(pl.multiple_of(at, TILE), TILE), :], zero_sem))
        for t in range(lof_hbm.shape[0] // TILE):
            go(pltpu.make_async_copy(zero, lof_hbm.at[pl.ds(t * TILE, TILE), :], zero_sem))

    def fetch(i, slot, go):
        for j in range(PART):
            near.fetch(i * PART + j, ct_hbm, ctx_ref, ct_v.at[slot], j * TILE, ct_sem.at[slot], go)

    def store(i, slot, go):
        for j in range(PART):
            near.store(i * PART + j, lo_hbm, lon_hbm, lo_v.at[slot], j * TILE, lo_sem.at[slot], go)

    @pl.when(count > 0)
    def _():
        fetch(0, 0, go_start)

    zero[...] = jnp.zeros(zero.shape, bf16)
    clear(go_start)

    def step(i, carry):
        slot = i % 2

        @pl.when(i + 1 < count)
        def _():
            fetch(i + 1, 1 - slot, go_start)

        fetch(i, slot, go_wait)

        @pl.when(i >= 2)
        def _():
            store(i - 2, slot, go_wait)

        def work(size):
            at = pl.ds(pl.multiple_of(i * PART * TILE, TILE), size * TILE)
            ct = ct_v[slot, : size * TILE, :]
            lo, gx = layer_tile(buf[at, :], names_at(names_ref, i * PART, size), ct, wp_ref, wpt_ref, cb_ref, gw_ref, span)
            lo_v[slot, : size * TILE, :] = lo
            buf[at, :] = gx

        more = near.tiles - i * PART > 2
        pl.when(more)(lambda: work(PART))
        pl.when(jnp.logical_not(more))(lambda: work(2))
        store(i, slot, go_start)
        return carry

    lax.fori_loop(0, count, step, 0)
    for back in (2, 1):
        @pl.when(count >= back)
        def _():
            store(count - back, (count - back) % 2, go_wait)

    clear(go_wait)


def local(bounds, names, cotangent, ctx, weights, gw, buf, far, blocks, span, cap):
    outs = cotangent.shape[1]
    return pl.pallas_call(
        functools.partial(local_kernel, "oct", far, blocks, span, cap),
        in_specs=specs("svavvvvvv"),
        out_specs=specs("aaavv"),
        out_shape=[pltpu.HBM(cotangent.shape, bf16), pltpu.HBM((cap, outs), bf16), pltpu.HBM((far * cap, outs), bf16),
                   pltpu.VMEM(gw.shape, f32), pltpu.VMEM(buf.shape, bf16)],
        input_output_aliases={7: 3, 8: 4},
        scratch_shapes=[
            pltpu.VMEM((2, PART * TILE, outs), bf16),
            pltpu.VMEM((2, PART * TILE, outs), bf16),
            pltpu.VMEM((TILE, outs), bf16),
            pltpu.SemaphoreType.DMA((2,)),
            pltpu.SemaphoreType.DMA((2,)),
            pltpu.SemaphoreType.DMA,
        ],
        compiler_params=params(24),
        cost_estimate=cost("local"),
        name="local",
    )(bounds, names, stay(cotangent), keep(ctx), *[keep(w) for w in weights], keep(gw), keep(buf))


def unlocal_kernel(oct_axis, cap, bounds, row_ref, gbuf, lon_ref, lo_in, part_ref, lo_hbm, moved, sem):
    blocks = row_ref.shape[0]
    join(cap, [0], oct_axis, lon_ref, lo_hbm, sem, go_start)

    def emit(b, rows):
        part_ref[b * BLOCK : (b + 1) * BLOCK, :] = rows.astype(bf16)

    cut = filled(bounds, 0, blocks)
    unsort_rows(bounds, row_ref, [0, 1], blocks,
                lambda n, first, rows: gbuf[pl.ds(pl.multiple_of(first + n * cut, 16), rows), :], moved, emit)
    join(cap, [0], oct_axis, lon_ref, lo_hbm, sem, go_wait)


def unlocal(bounds, row, gbuf, lon, lo, cap):
    blocks, width = row.shape[0], gbuf.shape[1]
    return pl.pallas_call(
        functools.partial(unlocal_kernel, "oct", cap),
        in_specs=specs("svvva"),
        out_specs=specs("va"),
        out_shape=[pltpu.VMEM((blocks * BLOCK, width), bf16), pltpu.HBM(lo.shape, bf16)],
        input_output_aliases={4: 1},
        scratch_shapes=[pltpu.VMEM((blocks * window_rows(2, 128) + WIN, width), bf16), pltpu.SemaphoreType.DMA((1,))],
        compiler_params=params(16),
        cost_estimate=cost("unlocal"),
        name="unlocal",
    )(bounds, row, keep(gbuf), keep(lon), stay(lo))


def names_kernel(kx, span, cap, labels_ref, names_ref, count_ref, back_ref):
    labels = labels_ref[...].astype(f32).astype(i32)
    blocks = labels.shape[0]
    groups = [2 * kx, 2 * kx + 1]
    pos, _, _, _, last = plan(labels, groups, span)
    names_ref[...] = stream_names(pos, labels, groups[0], span, cap)
    count_ref[...] = jnp.zeros(count_ref.shape, i32)
    count_ref[0:1, : 2 * blocks] = last[:1]
    back_ref[...] = jnp.zeros(back_ref.shape, bf16)


def make_names(labels, kx, span, cap):
    return pl.pallas_call(
        functools.partial(names_kernel, kx, span, cap),
        in_specs=specs("v"),
        out_specs=specs("vvv"),
        out_shape=[
            jax.ShapeDtypeStruct((labels.shape[0], BLOCK), i32),
            jax.ShapeDtypeStruct((8, 128), i32),
            pltpu.VMEM((2 * cap + UNIT, labels.shape[1]), bf16),
        ],
        compiler_params=params(8),
        cost_estimate=cost("names"),
        name="names",
    )(labels)


def lead_of(tiles):
    return jnp.maximum(tiles, LEAD)


def take_back(place, number, theirs, blocks, x_ref, at, back):
    for i in range(number):
        n = place + i - lead_of(tiles_of(theirs, 0, blocks, 0))

        @pl.when((n >= 0) & (n < (back.shape[0] - UNIT) // TILE))
        def _():
            back[pl.ds(pl.multiple_of(n * TILE, TILE), TILE), :] = x_ref[at + i * TILE : at + (i + 1) * TILE, :]


def far_kernel(message, before, after_it, emits, kx, oct_axis, blocks, span, cap, mine, theirs, *refs):
    names_ref, x_ref, ct_hbm, ctx_ref, wp_ref, wpt_ref, cb_ref, queue_in, lo_in, lof_in, gw_in, back_in, refs = *refs[:12], refs[12:]
    if before:
        ct_v, lo_old, refs = *refs[:2], refs[2:]
    queue, lo_hbm, lof_hbm, gw_ref, back, refs = *refs[:5], refs[5:]
    payloads, refs = refs[: len(emits)], refs[len(emits) :]
    if after_it:
        ct_new, refs = refs[0], refs[1:]
    lo_v, refs = refs[0], refs[1:]
    if not before:
        ct_v, refs = refs[0], refs[1:]
    ct_sem, new_sem, lo_sem = refs
    first, number = message
    source = lax.axis_index(oct_axis) ^ (2 * kx)
    rows = rows_of(theirs, 0, blocks, source, cap, kx - 1, 0)
    lead = lead_of(tiles_of(mine, 2 * kx, blocks))

    def fetch(u, go):
        if not before:
            rows.fetch(first + u, ct_hbm, ctx_ref, ct_v, u * TILE, ct_sem.at[u], go)

    def ahead(go):
        if before:
            for u in range(before[1]):
                rows.store(before[0] + u, lo_hbm, lof_hbm, lo_old, u * TILE, lo_sem, go)
        if after_it:
            for u in range(after_it[1]):
                rows.fetch(after_it[0] + u, ct_hbm, ctx_ref, ct_new, u * TILE, new_sem, go)

    for u in range(number):
        fetch(u, go_start)
    ahead(go_start)
    take_back(first, number, theirs, blocks, x_ref, 0, back)
    for u in range(number):
        fetch(u, go_wait)

    def work(size):
        at = slice(0, size * TILE)
        lo, gx = layer_tile(x_ref[at, :], names_at(names_ref, first, size), ct_v[at, :], wp_ref, wpt_ref, cb_ref, gw_ref, span)
        lo_v[at, :] = lo
        queue[pl.ds(pl.multiple_of((lead + first) * TILE, TILE), size * TILE), :] = gx

    if number > 2:
        pl.when(first + 2 < rows.tiles)(lambda: work(number))
        pl.when((first < rows.tiles) & (first + 2 >= rows.tiles))(lambda: work(2))
    else:
        pl.when(first < rows.tiles)(lambda: work(number))

    for payload, (place, count) in zip(payloads, emits):
        payload[...] = queue[place * TILE : (place + count) * TILE, :]
    ahead(go_wait)


def far_step(messages, m, points_in, kx, mine, theirs, names, x, cotangent, ctx, weights, state, ahead, blocks, span, cap):
    wp, wpt, cb = weights
    queue, lo, lof, gw, back = state
    width, outs = wp.shape
    last = points_in[-1] == m
    message, before, after_it = messages[m], (messages[m - 1] if m > 0 else None), (None if last else messages[m + 1])
    emits = messages[m + 2 :] if last else [messages[m + 2]]
    own = (message[1] * TILE, outs)
    shapes = [pltpu.VMEM(queue.shape, bf16), pltpu.HBM(lo.shape, bf16), pltpu.HBM(lof.shape, bf16), pltpu.VMEM(gw.shape, f32),
              pltpu.VMEM(back.shape, bf16)] + [pltpu.VMEM((count * TILE, width), bf16) for _, count in emits]
    if after_it:
        shapes.append(pltpu.VMEM((after_it[1] * TILE, outs), bf16))
    shapes.append(pltpu.VMEM(own, bf16))
    args = [mine, theirs, names, keep(x), stay(cotangent), keep(ctx), keep(wp), keep(wpt), keep(cb), keep(queue), stay(lo),
            stay(lof), keep(gw), keep(back)] + [keep(a) for a in ahead]
    out = pl.pallas_call(
        functools.partial(far_kernel, message, before, after_it, emits, kx, "oct", blocks, span, cap),
        in_specs=specs("ssvvavvvvvaavv" + "v" * len(ahead)),
        out_specs=specs("vaavv" + "v" * (len(shapes) - 5)),
        out_shape=shapes,
        input_output_aliases={9 + i: i for i in range(5)},
        scratch_shapes=([] if before else [pltpu.VMEM(own, bf16)])
        + [pltpu.SemaphoreType.DMA((message[1],)), pltpu.SemaphoreType.DMA, pltpu.SemaphoreType.DMA],
        compiler_params=params(20),
        cost_estimate=cost("last" if last else "far"),
        name="far",
    )(*args)
    return tuple(out[:5]), out[5 : 5 + len(emits)], tuple(out[5 + len(emits) :])


def unpack_kernel(far, blocks, lasts, bounds, *refs):
    theirs, rows_far, refs = refs[:far], refs[far : 2 * far], refs[2 * far :]
    parts, refs = refs[: far * len(lasts)], refs[far * len(lasts) :]
    part_ref, refs = refs[0], refs[1 + far :]
    out_hbm, backs, (moved, out_ref, sem) = refs[0], refs[1 : 1 + far], refs[-3:]
    group = max(1, blocks // 4)

    def send(n):
        rows = pl.ds(n * group * BLOCK, group * BLOCK)
        return pltpu.make_async_copy(out_ref.at[rows, :], out_hbm.at[rows, :], sem.at[n])

    for k in range(far):
        for j, (first, number) in enumerate(lasts):
            take_back(first, number, theirs[k], blocks, parts[k * len(lasts) + j], 0, backs[k])
        cut = filled(bounds, 2 + 2 * k, blocks)

        def pick(n, first, count):
            return backs[k][pl.ds(pl.multiple_of(first + n * cut, 16), count), :]

        def emit(b, value):
            at = slice(b * BLOCK, (b + 1) * BLOCK)
            before = part_ref if k == 0 else out_ref
            out_ref[at, :] = (value + before[at, :].astype(f32)).astype(bf16)
            if k == far - 1 and (b + 1) % group == 0:
                send(b // group).start()

        unsort_rows(bounds, rows_far[k], [2 + 2 * k, 3 + 2 * k], blocks, pick, moved, emit)
    for n in range(blocks // group):
        send(n).wait()


def unpack(bounds, theirs, rows_far, lasts, parts, part, backs):
    points, width = part.shape
    blocks = points // BLOCK
    far = len(theirs)
    extra = far * len(lasts)
    return pl.pallas_call(
        functools.partial(unpack_kernel, far, blocks, lasts),
        in_specs=specs("s" + "s" * far + "v" * (2 * far + extra + 1)),
        out_specs=specs("a" + "v" * far),
        out_shape=[pltpu.HBM(part.shape, bf16)] + [pltpu.VMEM(b.shape, bf16) for b in backs],
        input_output_aliases={2 * far + extra + 2 + k: 1 + k for k in range(far)},
        scratch_shapes=[
            pltpu.VMEM((blocks * window_rows(2, 128) + WIN, width), bf16),
            pltpu.VMEM(part.shape, bf16),
            pltpu.SemaphoreType.DMA((4,)),
        ],
        compiler_params=params(20),
        cost_estimate=cost("unpack"),
        name="unpack",
    )(bounds, *theirs, *rows_far, *[keep(x) for x in parts], keep(part), *[keep(b) for b in backs])[0]


def join(cap, kxs, oct_axis, lox_ref, lo_hbm, sem, go):
    other = lax.axis_index(oct_axis) ^ 1
    for n, k in enumerate(kxs):
        at = pl.ds(pl.multiple_of((other ^ (2 * k)) * cap, cap), cap)
        go(pltpu.make_async_copy(lox_ref.at[pl.ds(n * cap, cap), :], lo_hbm.at[at, :], sem.at[n]))


def merge_kernel(cap, kxs, oct_axis, lox_ref, lo_in, lo_hbm, sem):
    for go in (go_start, go_wait):
        join(cap, kxs, oct_axis, lox_ref, lo_hbm, sem, go)


def merge(lox, lo, cap, kxs):
    return pl.pallas_call(
        functools.partial(merge_kernel, cap, tuple(kxs), "oct"),
        in_specs=specs("va"),
        out_specs=specs("a")[0],
        out_shape=pltpu.HBM(lo.shape, lo.dtype),
        input_output_aliases={1: 0},
        scratch_shapes=[pltpu.SemaphoreType.DMA((len(kxs),))],
        compiler_params=params(4),
        cost_estimate=cost("merge"),
        name="merge",
    )(keep(lox), stay(lo))


def column_block(axes, n):
    a, b = (lax.axis_index(axis) % 2 for axis in axes)
    return (a ^ (n % 2)) * 2 + (b ^ (n // 2))


def collect_kernel(axes, shape_axis, oct_axis, shapes, span, extra, blocks, cap, message, usual, steps, *refs):
    mine, refs = refs[0], refs[1:]
    theirs, olds, refs = refs[:extra], refs[extra : 2 * extra], refs[2 * extra :]
    gw_ref, info_ref, codes_ref, lo_in, lof_in, outs, lo_hbm, lof_hbm, full, sem = *refs[:5], refs[5:9], *refs[9:]
    source = lax.axis_index(oct_axis)

    def store(go):
        for k in range(extra):
            rows = rows_of(theirs[k], 0, blocks, source ^ (2 * k + 2), cap, k, 0)
            for u in range(message[1]):
                rows.store(message[0] + u, lo_hbm, lof_hbm, olds[k], u * TILE, sem, go)

    store(go_start)
    width = gw_ref.shape[0] - 16
    cols = gw_ref.shape[1]
    code_width = codes_ref.shape[1]
    base = lax.axis_index(shape_axis) * span
    full[:width, :] = gw_ref[:width, :]
    ps = jnp.zeros((shapes, cols), f32)
    for s in range(span):
        ps = ps + jnp.where(iota((shapes, 1), 0) == base + s, gw_ref[width + s : width + s + 1, :], 0.0)
    full[width : width + shapes, :] = ps
    flag = jnp.int32(0)
    for k in range(extra):
        ours = tiles_of(mine, 2 + 2 * k, blocks)
        other = tiles_of(theirs[k], 0, blocks, 0)
        most = jnp.maximum(jnp.maximum(ours, LEAD) + other, jnp.maximum(other, LEAD) + ours)
        flag = flag | ((jnp.maximum(ours, other) > usual) | (most > steps)).astype(i32)
    flag = flag.astype(f32)
    lane = iota((1, cols - code_width), 1)
    info = jnp.zeros((shapes, cols), f32)
    for s in range(span):
        number = info_ref[s : s + 1, :1]
        high = jnp.floor(number / 1024.0)
        mid = jnp.floor((number - 1024.0 * high) / 32.0)
        low = number - 1024.0 * high - 32.0 * mid
        digits = jnp.where(lane < 64, low, jnp.where(lane < 128, mid, jnp.where(lane < 192, high, flag)))
        code = jnp.where(lax.axis_index(oct_axis) == 0, codes_ref[s : s + 1, :].astype(f32), 0.0)
        info = info + jnp.where(iota((shapes, 1), 0) == base + s, jnp.concatenate([code, digits], axis=1), 0.0)
    full[width + shapes : width + 2 * shapes, :] = info
    for n in range(4):
        at = pl.ds(pl.multiple_of(column_block(axes, n) * 128, 128), 128)
        outs[n][...] = full[:, at].astype(bf16)
    store(go_wait)


def halves(x):
    high = x.astype(bf16)
    return high, (x - high.astype(f32)).astype(bf16)


def finish_kernel(axes, shape_axis, hid, span, categories, momentum, *refs):
    parts, refs = refs[:4], refs[4:]
    direction_ref, gain_ref, norm_ref, w_ref, mean_ref, var_ref, refs = *refs[:6], refs[6:]
    dg_ref, gg_ref, bg_ref, cg_ref, mean_out, var_out, left_ref, full = refs
    for n in range(4):
        at = pl.ds(pl.multiple_of(column_block(axes, n) * 128, 128), 128)
        full[:, at] = parts[n][...].astype(f32)
    ins, cols = direction_ref.shape
    cats, code_width = mean_ref.shape
    shapes = (full.shape[0] - (ins - code_width)) // 2
    width = ins - code_width
    ps = full[width : width + shapes, :]
    info = full[width + shapes : width + 2 * shapes, :]
    codes = info[:, :code_width]
    at = code_width
    number = info[:, at : at + 1] + 32.0 * info[:, at + 64 : at + 65] + 1024.0 * info[:, at + 128 : at + 129]
    for c in range(cats):
        chosen = jnp.zeros((shapes, 1), f32)
        for s in range(shapes):
            chosen = jnp.where((iota((shapes, 1), 0) == s) & (categories[s] == c), 1.0, chosen)
        weight = chosen * number
        count = jnp.sum(weight, axis=0, keepdims=True)
        mean = jnp.sum(weight * codes, axis=0, keepdims=True) / count
        var = jnp.sum(weight * codes * codes, axis=0, keepdims=True) / count - mean * mean
        rate = momentum[c]
        mean_out[c : c + 1, :] = (1.0 - rate) * mean_ref[c : c + 1, :] + rate * mean
        var_out[c : c + 1, :] = (1.0 - rate) * var_ref[c : c + 1, :] + rate * var

    gw = full[:width, :]
    codes_all = jnp.concatenate(
        [jnp.zeros((shapes, hid), f32), codes, jnp.zeros((shapes, ins - hid - code_width), f32)], axis=1
    )
    high, low = halves(ps)
    wg = lax.dot_general(jnp.concatenate([codes_all, codes_all], axis=0).astype(bf16), jnp.concatenate([high, low], axis=0),
                         (((0,), (0,)), ((), ())), preferred_element_type=f32)
    head = jnp.where(iota((width, 1), 0) < hid, gw, wg[:width])
    tail = jnp.where(iota((8, 1), 0) + (width - 8) >= hid, gw[width - 8 :], wg[ins - 8 :])
    wg = jnp.concatenate([head, wg[width : ins - 8], tail], axis=0)
    direction = direction_ref[...]
    norms = norm_ref[...]
    dots = jnp.sum(wg * direction, axis=0, keepdims=True)
    gg_ref[...] = dots / norms
    dg_ref[...] = (gain_ref[...] / norms) * (wg - direction * (dots / (norms * norms)))
    bg_ref[...] = jnp.sum(ps, axis=0, keepdims=True)
    base = lax.axis_index(shape_axis) * span
    own = jnp.zeros((8, cols), f32)
    for s in range(span):
        row = jnp.sum(jnp.where(iota((shapes, 1), 0) == base + s, ps, 0.0), axis=0, keepdims=True)
        own = own + jnp.where(iota((8, 1), 0) == s, row, 0.0)
    both = lax.dot_general(jnp.concatenate(halves(own), axis=0), w_ref[...], (((1,), (1,)), ((), ())), preferred_element_type=f32)
    cg_ref[...] = (both[:8] + both[8:])[:span, hid : hid + code_width]
    left_ref[0] = jnp.max(info[:, at + 192 :])


def finish(axes, span, categories, momentum, parts, direction, gain, norms, weight, prev_mean, prev_var):
    ins, outs = direction.shape
    return pl.pallas_call(
        functools.partial(finish_kernel, axes, "shape", HID, span),
        in_specs=specs("ss" + "v" * 10),
        out_specs=specs("v" * 6 + "s"),
        out_shape=[
            jax.ShapeDtypeStruct((ins, outs), f32),
            jax.ShapeDtypeStruct((1, outs), f32),
            jax.ShapeDtypeStruct((1, outs), f32),
            jax.ShapeDtypeStruct((span, prev_mean.shape[1]), f32),
            jax.ShapeDtypeStruct(prev_mean.shape, f32),
            jax.ShapeDtypeStruct(prev_mean.shape, f32),
            jax.ShapeDtypeStruct((1,), f32),
        ],
        scratch_shapes=[pltpu.VMEM((parts[0].shape[0], outs), f32)],
        compiler_params=params(12),
        cost_estimate=cost("finish"),
        name="finish",
    )(categories, momentum, *[keep(p) for p in parts], keep(direction), keep(gain), keep(norms), keep(weight), prev_mean, prev_var)


def swap(v, axis, k):
    n = lax.axis_size(axis)
    return lax.ppermute(v, axis, [(i, i ^ k) for i in range(n)])


def swap_both(v, k):
    n, m = lax.axis_size("shape"), lax.axis_size("oct")
    return lax.ppermute(v, ("shape", "oct"), [(i, i ^ k) for i in range(n * m)])


def bits(axis, first):
    n = lax.axis_size(axis)
    return [(axis, 1 << j) for j in range(first, n.bit_length() - 1)]


def after(x, *others):
    return lax.optimization_barrier((x, *others))[0]


def quarters_to(parts):
    m = lax.axis_size("oct")
    return [swap(parts[0], "oct", 1), swap(parts[1], "shape", 1), swap_both(parts[2], m + 1)]


def total_quarter(parts, before):
    got = quarters_to(parts[1:])
    v = parts[0].astype(f32) + got[0].astype(f32) + got[1].astype(f32) + after(got[2], *before[0]).astype(f32)
    v = v.astype(bf16)
    yield v
    for n, (axis, k) in enumerate(bits("shape", 1) + bits("oct", 1)):
        v = (v.astype(f32) + after(swap(v, axis, k), *before[n + 1]).astype(f32)).astype(bf16)
        yield v


AXES = ("oct", "shape")


def collect(mine, theirs, olds, gw, info, codes, lo, lof, shapes, blocks, cap, message, usual, steps):
    span = codes.shape[0]
    far = len(theirs)
    rows = gw.shape[0] - 16 + 2 * shapes
    out = pl.pallas_call(
        functools.partial(collect_kernel, AXES, "shape", "oct", shapes, span, far, blocks, cap, message, usual, steps),
        in_specs=specs("s" + "s" * far + "v" * far + "vvvaa"),
        out_specs=specs("vvvvaa"),
        out_shape=[pltpu.VMEM((rows, 128), bf16)] * 4 + [pltpu.HBM(lo.shape, bf16), pltpu.HBM(lof.shape, bf16)],
        input_output_aliases={2 * far + 4: 4, 2 * far + 5: 5},
        scratch_shapes=[pltpu.VMEM((rows, gw.shape[1]), f32), pltpu.SemaphoreType.DMA],
        compiler_params=params(8),
        cost_estimate=cost("collect"),
        name="collect",
    )(mine, *theirs, *[keep(o) for o in olds], keep(gw), info, codes, stay(lo), stay(lof))
    return out[:4], out[4], out[5]


def run(usual, steps, point_inputs, shape_ids, octants, categories, codes, direction, gain, bias, cotangent, prev_mean, prev_var, momentum):
    points, width = point_inputs.shape
    oct_count, shape_dev = lax.axis_size("oct"), lax.axis_size("shape")
    cap = 2 * points // oct_count
    span, code_width = codes.shape
    shapes = shape_dev * span
    blocks = points // BLOCK
    far = list(range(1, oct_count // 2))
    messages = plan_messages(usual, steps)
    points_in = [m for m, (first, _) in enumerate(messages) if first < usual]

    (ct_near, ct_far, x_near), heads, queues, rows_far, (row_near, mine, labels, pos) = pack(
        octants, shape_ids, point_inputs, cotangent, messages, oct_count, span, cap)
    ctn, ctf = swap(ct_near, "oct", 1), swap(ct_far, "oct", 1)
    got = {(k, m): swap(heads[2 * (k - 1) + m], "oct", 2 * k) for k in far for m in range(2)}
    gw, buf, wp, wpt, weight, cb, norms, direction_v, gain_v, near_names, info = prepare(
        mine, row_near, labels, pos, x_near, direction, gain, bias, codes, oct_count, cap)
    weights = (wp, wpt, cb)
    lo, lon, lof, gw, buf = local(mine, near_names, cotangent, ctn, weights, gw, buf, len(far), blocks, span, cap)

    queue = {k: queues[k - 1] for k in far}
    named, theirs, back, ahead = {}, {}, {}, {}
    for k in far:
        named[k], theirs[k], back[k] = make_names(after(got[k, 0], gw)[messages[0][1] * TILE :], k, span, cap)
        ahead[k] = ()
    for m in points_in:
        for k in far:
            (queue[k], lo, lof, gw, back[k]), payloads, ahead[k] = far_step(
                messages, m, points_in, k, mine, theirs[k], named[k], got[k, m], cotangent, ctf, weights,
                (queue[k], lo, lof, gw, back[k]), ahead[k], blocks, span, cap)
            for j, payload in enumerate(payloads):
                got[k, m + 2 + j] = swap(payload, "oct", 2 * k)
        if m == min(1, points_in[-1] - 1):
            part, lo = unlocal(mine, row_near, after(buf, gw), swap(lon, "oct", 1), lo, cap)
            gw = after(gw, part)
    their = [theirs[k] for k in far]
    lasts = list(range(len(points_in), len(messages)))
    order = ((), (0,), (), (1,)) if len(lasts) == 2 else ()
    before = [[got[k, lasts[i]] for k in far for i in ii] for ii in order] + [[] for _ in range(20)]
    parts, lo, lof = collect(mine, their, [ahead[k][-1] for k in far], gw, info, codes, lo, lof, shapes, blocks, cap,
                             messages[points_in[-1]], usual, steps)
    lox = swap(lof, "oct", 1)
    input_grad = unpack(mine, their, rows_far, [messages[m] for m in lasts], [got[k, m] for k in far for m in lasts], part,
                        [back[k] for k in far])
    for v in total_quarter(parts, before):
        pass
    parts = [v] + quarters_to([v] * 3)
    lo = merge(lox, lo, cap, far)
    direction_grad, gain_grad, bias_grad, code_grad, running_mean, running_var, left = finish(
        AXES, span, categories, momentum, [after(parts[0], lo, input_grad)] + parts[1:], direction_v, gain_v, norms, weight, prev_mean, prev_var)
    outputs = (
        lo,
        input_grad,
        code_grad,
        direction_grad,
        gain_grad[0],
        bias_grad[0],
        running_mean,
        running_var,
    )
    return outputs, left[0]


def body(*args):
    points, oct_count = args[0].shape[0], lax.axis_size("oct")
    most = 2 * (2 * points // oct_count) // TILE
    all_steps = max(most, LEAD) + most
    usual, steps = min(USUAL, most), min(STEPS, all_steps)
    outputs, left = run(usual, steps, *args)
    if (usual, steps) == (most, all_steps):
        return outputs

    def more(carry):
        return jnp.float32(0), run(most, all_steps, *args)[0]

    return lax.while_loop(lambda carry: carry[0] > 0, more, (left, outputs))[1]


def solution(mesh):
    both = P(("shape", "oct"), None)
    in_specs = (both, P(("shape", "oct")), both, P(), P("shape", None), P(), P(), P(), both, P(), P(), P())
    out_specs = (both, both, P("shape", None), P(), P(), P(), P(), P())
    return jax.shard_map(body, mesh=mesh, in_specs=in_specs, out_specs=out_specs, check_vma=False)
```

```python
import functools

import jax
import jax.numpy as jnp
from jax import lax
from jax.experimental import pallas as pl
from jax.experimental.pallas import tpu as pltpu
from jax.sharding import PartitionSpec as P

HID = 253
CATS = 5
BLOCK = 256
TILE = 256
ALIGN = 64
UNIT = 2 * TILE
WIN = BLOCK + 16
LEAD = 8
USUAL = 13
STEPS = 21
PART = 4
FAR = 1 << 20

norm_eps = 1e-06
COSTS = dict(pack=30, prepare=30, local=30, unlocal=0.01, names=30, far=30, last=0.01, flush=0.01, unpack=30, merge=0.01, finish=30, collect=0.01)


def cost(name):
    return pl.CostEstimate(flops=max(1, int(COSTS[name] * 10**9)), bytes_accessed=1, transcendentals=0)


f32, bf16, i32 = jnp.float32, jnp.bfloat16, jnp.int32


def params(mib):
    return pltpu.CompilerParams(vmem_limit_bytes=mib * 1024 * 1024)


def keep(x):
    return pltpu.with_memory_space_constraint(x, pltpu.VMEM)


def stay(x):
    return pltpu.with_memory_space_constraint(x, pltpu.HBM)


def specs(text):
    kinds = {"v": pltpu.VMEM, "s": pltpu.SMEM, "a": pl.ANY}
    return [pl.BlockSpec(memory_space=kinds[c]) for c in text]


def iota(shape, dim):
    return lax.broadcasted_iota(i32, shape, dim)


def plan_messages(usual, steps):
    cuts = list(range(0, usual, PART)) + list(range(usual, steps, PART)) + [steps]
    if usual % PART == 1:
        cuts[usual // PART] -= 1
    return [(a, b - a) for a, b in zip(cuts, cuts[1:])]


def ceil_to(n, step):
    return -(-n // step) * step


def plan(labels, groups, span):
    rows = labels.shape[0]
    count = len(groups)
    mask = jnp.concatenate([(labels >= g * span) & (labels < (g + 1) * span) for g in groups], axis=0)
    one = jnp.where(mask, 1.0, 0.0)
    m = one.astype(bf16)
    total = count * rows
    upper = jnp.where(iota((BLOCK, BLOCK), 0) <= iota((BLOCK, BLOCK), 1), 1.0, 0.0).astype(bf16)
    cum = jnp.dot(m, upper, preferred_element_type=f32)
    a, b = iota((total, total), 0), iota((total, total), 1)
    lower = jnp.where((a // rows == b // rows) & (b < a), 1.0, 0.0).astype(bf16)
    tot = jnp.sum(one, axis=1, keepdims=True)
    base = jnp.dot(lower, jnp.broadcast_to(tot, (total, 128)).astype(bf16), preferred_element_type=f32)[:, :1]
    lo, hi = base.astype(i32), (base + tot).astype(i32)
    pos = jnp.where(mask, lo + cum.astype(i32) - 1, -FAR)
    tot_row = lax.dot_general(jnp.ones((8, BLOCK), bf16), m, (((1,), (1,)), ((), ())), preferred_element_type=f32)
    base_row = lax.dot_general(tot_row.astype(bf16), lower, (((1,), (1,)), ((), ())), preferred_element_type=f32)
    return pos, lo, hi, base_row.astype(i32), (base_row + tot_row).astype(i32)


def sorted_rows(pos, lo, hi, rows, first, count):
    row, at = None, 0
    for n in range(first, first + count):
        s = slice(n * rows, (n + 1) * rows)
        start = lo[s] // 16 * 16
        r = pos[s] + (at - start)
        row = r if row is None else jnp.maximum(row, r)
        at = at + (hi[s] + 15) // 16 * 16 - start
    return row


def ahead_by(v, step):
    rows, lanes = v.shape
    if step >= lanes:
        return pltpu.roll(v, rows - step // lanes, 0)
    moved = pltpu.roll(v, lanes - step, 1)
    return jnp.where(iota((rows, lanes), 1) < lanes - step, moved, pltpu.roll(moved, rows - 1, 0))


def back_by(v, step):
    rows, lanes = v.shape
    if step >= lanes:
        return pltpu.roll(v, step // lanes, 0)
    moved = pltpu.roll(v, step, 1)
    return jnp.where(iota((rows, lanes), 1) >= step, moved, pltpu.roll(moved, 1, 0))


def squeeze(pos, labels, group, span):
    rows, lanes = pos.shape
    at = iota((rows, lanes), 0) * lanes + iota((rows, lanes), 1)
    v = jnp.where(pos >= 0, (at - pos) * 16 + (labels - group * span + 1), 0)
    for bit in range((rows * lanes).bit_length() - 1):
        go = jnp.where(((v >> (4 + bit)) & 1) == 1, v, 0)
        v = v - go + ahead_by(go, 1 << bit)
    return v & 15


def stream_names(pos, labels, group, span, cap):
    rows = labels.shape[0]
    first, second = (squeeze(pos[n * rows : (n + 1) * rows], labels, group + n, span) for n in range(2))
    one = jnp.where(pos[:rows] >= 0, 1.0, 0.0)
    count = jnp.sum(jnp.sum(one, axis=1, keepdims=True), axis=0, keepdims=True).astype(i32)
    skip = (count + (ALIGN - 1)) // ALIGN * ALIGN
    step = ALIGN
    while step <= cap:
        second = jnp.where((skip & step) > 0, back_by(second, step), second)
        step *= 2
    return first + second


def filled(bounds, group, blocks, row=1):
    return (bounds[row, (group + 1) * blocks - 1] + (ALIGN - 1)) // ALIGN * ALIGN


def tiles_of(bounds, group, blocks, row=1):
    return (filled(bounds, group, blocks, row) + filled(bounds, group + 1, blocks, row) + (TILE - 1)) // TILE


def spans(bounds, groups, blocks, b):
    at, result = 0, []
    for g in groups:
        lo, hi = bounds[0, g * blocks + b], bounds[1, g * blocks + b]
        first = pl.multiple_of(lo // 16 * 16, 16)
        result.append((first, pl.multiple_of(at, 16) if result else 0, lo - first))
        at = at + ((hi + 15) // 16 * 16 - first)
    return result


def window_rows(count, step):
    return ceil_to(BLOCK + 30 * count, step)


def sort_rows(bounds, row_ref, x_ref, groups, blocks, moved, put):
    rows = window_rows(len(groups), 64)
    for b in range(blocks):
        hot = jnp.where(iota((rows, BLOCK), 0) == row_ref[b : b + 1, :], 1.0, 0.0).astype(bf16)
        out = jnp.dot(hot, x_ref[b * BLOCK : (b + 1) * BLOCK, :], preferred_element_type=f32).astype(bf16)
        moved[b * rows : (b + 1) * rows, :] = out
    moved[blocks * rows :, :] = jnp.zeros((moved.shape[0] - blocks * rows, moved.shape[1]), bf16)
    for n in range(len(groups)):
        for b in range(blocks):
            first, at, over = spans(bounds, groups, blocks, b)[n]
            dst, start = put(n, first)
            at = at + b * rows
            old = dst[pl.ds(start, 16), :]
            new = moved[pl.ds(pl.multiple_of(at, 16), 16), :]
            dst[pl.ds(start, 16), :] = jnp.where(iota((16, 1), 0) < over, old, new)
            rest = pl.ds(pl.multiple_of(start + 16, 16), BLOCK)
            dst[rest, :] = moved[pl.ds(pl.multiple_of(at + 16, 16), BLOCK), :]
        end = bounds[1, (groups[n] + 1) * blocks - 1]
        dst, start = put(n, (end + 15) // 16 * 16)
        size = ALIGN if n + 1 < len(groups) else PART * TILE
        dst[pl.ds(start, size), :] = jnp.zeros((size, dst.shape[1]), bf16)


def unsort_rows(bounds, row_ref, groups, blocks, pick, moved, emit):
    rows = window_rows(len(groups), 128)
    for b in range(blocks):
        moved[b * rows + WIN : (b + 1) * rows, :] = jnp.zeros((rows - WIN, moved.shape[1]), bf16)
        for n, (first, at, _) in enumerate(spans(bounds, groups, blocks, b)):
            moved[pl.ds(pl.multiple_of(at + b * rows, 16), WIN), :] = pick(n, first, WIN)
    for b in range(blocks):
        hot = jnp.where(iota((rows, BLOCK), 0) == row_ref[b : b + 1, :], 1.0, 0.0).astype(bf16)
        emit(b, jnp.dot(jnp.transpose(hot), moved[b * rows : (b + 1) * rows, :], preferred_element_type=f32))


def layer_tile(x, named, ct, wp_ref, wpt_ref, cb_ref, gw_ref, span):
    rows = x.shape[0]
    col = jnp.transpose(jnp.broadcast_to(named.astype(f32), (8, rows)))[:, :1]
    pre = jnp.dot(x, wp_ref[...], preferred_element_type=f32)
    add = cb_ref[0:1, :]
    for s in range(1, span):
        add = jnp.where(col == s + 1.0, cb_ref[s : s + 1, :], add)
    pre = pre + add
    valid = col > 0.0
    e = jnp.exp(-jnp.abs(pre))
    soft = jnp.maximum(pre, 0.0) + jnp.where(e < 2.0**-12, e, jnp.log(1.0 + e))
    sig = jnp.exp(pre - soft)
    lo = jnp.where(valid, soft, 0.0).astype(bf16)
    gp = jnp.where(valid, ct.astype(f32) * sig, 0.0).astype(bf16)
    gx = jnp.dot(gp, wpt_ref[...], preferred_element_type=f32).astype(bf16)
    sel = jnp.where(jnp.broadcast_to(named, (16, rows)) == iota((16, rows), 0) + 1, 1.0, 0.0).astype(bf16)
    left = jnp.concatenate([jnp.transpose(x), sel], axis=0)
    gw_ref[...] += jnp.dot(left, gp, preferred_element_type=f32)
    return lo, gx


def pack_kernel(oct_count, sizes, shape_axis, oct_axis, span, cap, octants_hbm, ids_hbm, x_hbm, ct_hbm, *refs):
    far = oct_count // 2 - 1
    octants_ref, ids_ref, in_sem, ct_sem = refs[-4:]
    refs = refs[:-4]
    ct_near, ct_far, x_ref, refs = *refs[:3], refs[3:]
    other = lax.axis_index(oct_axis) ^ 1
    blocks_out = []
    for k in range(oct_count // 2):
        there = ct_hbm.at[pl.ds(pl.multiple_of((other ^ (2 * k)) * cap, cap), cap), :]
        here = ct_far.at[pl.ds((k - 1) * cap, cap), :] if k else ct_near
        blocks_out.append(pltpu.make_async_copy(there, here, ct_sem.at[k]))
    fetches = [
        pltpu.make_async_copy(a, b, in_sem.at[i])
        for i, (a, b) in enumerate(zip((octants_hbm, ids_hbm, x_hbm), (octants_ref, ids_ref, x_ref)))
    ]
    for f in fetches + blocks_out:
        f.start()
    heads, refs = refs[: 2 * far], refs[2 * far :]
    queues, rows_far, refs = refs[:far], refs[far : 2 * far], refs[2 * far :]
    row_near, bounds_ref, labels_ref, pos_ref, moved, bounds_v, bounds, sem = refs
    blocks = row_near.shape[0]
    me = lax.axis_index(oct_axis)
    first_shape = lax.axis_index(shape_axis) * span

    def wide(ref):
        return jnp.concatenate([ref[pl.ds(h, blocks, 2), :] for h in range(2)], axis=1)

    for f in fetches[:2]:
        f.wait()
    ids = wide(ids_ref) - first_shape
    labels = (wide(octants_ref) ^ me) * span + ids
    pos, lo, hi, first_row, last_row = plan(labels, range(oct_count), span)
    n = oct_count * blocks
    bounds_v[...] = jnp.zeros(bounds_v.shape, i32)
    bounds_v[0:1, :n] = first_row[:1]
    bounds_v[1:2, :n] = last_row[:1]
    bounds_ref[...] = bounds_v[...]
    copy = pltpu.make_async_copy(bounds_v, bounds, sem)
    copy.start()
    row_near[...] = sorted_rows(pos, lo, hi, blocks, 0, 2)
    for k in range(far):
        rows_far[k][...] = sorted_rows(pos, lo, hi, blocks, 2 + 2 * k, 2)
    labels_ref[...] = labels
    pos_ref[...] = pos[: 2 * blocks]
    for k in range(far):
        queues[k][...] = jnp.zeros(queues[k].shape, bf16)
    copy.wait()
    fetches[2].wait()
    for k in range(far):
        groups = [2 + 2 * k, 3 + 2 * k]
        cut = filled(bounds, groups[0], blocks)
        sort_rows(bounds, rows_far[k], x_ref, groups, blocks, moved,
                  lambda n, first: (queues[k], pl.multiple_of(first + n * cut, 16)))
        heads[2 * k][: sizes[0], :] = queues[k][: sizes[0], :]
        heads[2 * k][sizes[0] :, :] = labels.astype(f32).astype(bf16)
        heads[2 * k + 1][...] = queues[k][sizes[0] : sizes[0] + sizes[1], :]
    for f in blocks_out:
        f.wait()


def pack(octants, ids, points, cotangent, messages, oct_count, span, cap):
    count, width = points.shape
    blocks = count // BLOCK
    far = oct_count // 2 - 1
    shape = jax.ShapeDtypeStruct
    sizes = [n * TILE for _, n in messages[:2]]
    heads = [pltpu.VMEM((sizes[0] + blocks, width), bf16), pltpu.VMEM((sizes[1], width), bf16)] * far
    cols = cotangent.shape[1]
    outs = [pltpu.VMEM((cap, cols), bf16), pltpu.VMEM((far * cap, cols), bf16), pltpu.VMEM(points.shape, bf16)] + heads + [pltpu.VMEM((4 * cap, width), bf16)] * far
    outs += [shape((blocks, BLOCK), i32)] * (far + 1)
    outs += [shape((8, 128), i32), shape((blocks, BLOCK), i32), shape((2 * blocks, BLOCK), i32)]
    out = pl.pallas_call(
        functools.partial(pack_kernel, oct_count, sizes, "shape", "oct", span, cap),
        in_specs=specs("aaaa"),
        out_specs=specs("v" * len(outs)),
        out_shape=outs,
        scratch_shapes=[
            pltpu.VMEM((blocks * window_rows(2, 64) + WIN, width), bf16),
            pltpu.VMEM((8, 128), i32),
            pltpu.SMEM((8, 128), i32),
            pltpu.SemaphoreType.DMA,
            pltpu.VMEM((count // 128, 128), i32),
            pltpu.VMEM((count // 128, 128), i32),
            pltpu.SemaphoreType.DMA((3,)),
            pltpu.SemaphoreType.DMA((oct_count // 2,)),
        ],
        compiler_params=params(16),
        cost_estimate=cost("pack"),
        name="pack",
    )(stay(octants.reshape(-1, 128)), stay(ids.reshape(-1, 128)), stay(points), stay(cotangent))
    x, out = out[:3], out[3:]
    heads, queues, rows_far, out = out[: 2 * far], out[2 * far : 3 * far], out[3 * far : 4 * far], out[4 * far :]
    return x, heads, queues, rows_far, out


def set_weights(hid, direction_ref, gain_ref, bias_ref, codes_ref, wp_ref, wpt_ref, w_ref, cb_ref, norm_ref):
    direction = direction_ref[...]
    norms = jnp.sqrt(jnp.sum(direction * direction, axis=0, keepdims=True) + norm_eps)
    weight = (direction * (gain_ref[...] / norms)).astype(bf16)
    norm_ref[...] = norms
    w_ref[...] = weight
    width = wp_ref.shape[0]
    wf = weight.astype(f32)
    last = jnp.where(iota((8, 1), 0) + (width - 8) < hid, wf[width - 8 : width, :], wf[-8:, :])
    wp = jnp.concatenate([wf[: width - 8, :], last], axis=0)
    wp_ref[...] = wp.astype(bf16)
    wpt_ref[...] = wp.T.astype(bf16)
    span, code_width = codes_ref.shape
    w_code = wf[hid : hid + code_width, :].astype(bf16)
    codes = jnp.concatenate([codes_ref[...].astype(f32), jnp.zeros((8 - span, code_width), f32)], axis=0).astype(bf16)
    cb_ref[...] = jnp.dot(codes, w_code, preferred_element_type=f32) + bias_ref[...]


def prepare_kernel(oct_count, oct_axis, span, cap, bounds, row_ref, labels_ref, pos_ref, x_ref, codes_v, direction_hbm, gain_hbm, bias_hbm,
                   gw_ref, buf, wp_ref, wpt_ref, w_ref, cb_ref, norm_ref, direction_v, gain_v,
                   names_ref, info_ref, moved, bias_v, in_sem):
    blocks = row_ref.shape[0]
    cut = [filled(bounds, r, blocks) for r in range(2)]
    fetches = [
        pltpu.make_async_copy(a, b, in_sem.at[i])
        for i, (a, b) in enumerate(((direction_hbm, direction_v), (gain_hbm, gain_v), (bias_hbm, bias_v)))
    ]
    for f in fetches:
        f.start()

    gw_ref[...] = jnp.zeros(gw_ref.shape, f32)
    sort_rows(bounds, row_ref, x_ref, [0, 1], blocks, moved,
              lambda n, first: (buf, pl.multiple_of(first + n * cut[0], 16)))
    labels = labels_ref[...]
    names_ref[...] = stream_names(pos_ref[...], labels, 0, span, cap)
    ids = labels % span
    info_ref[...] = jnp.zeros(info_ref.shape, f32)
    for s in range(span):
        number = jnp.sum(jnp.sum(jnp.where(ids == s, 1.0, 0.0), axis=1, keepdims=True), axis=0, keepdims=True)
        info_ref[s : s + 1, :] = jnp.broadcast_to(number, (1, 128))
    for f in fetches:
        f.wait()
    set_weights(HID, direction_v, gain_v, bias_v, codes_v, wp_ref, wpt_ref, w_ref, cb_ref, norm_ref)


def prepare(bounds, row, labels, pos, points, direction, gain, bias, codes, oct_count, cap):
    width = points.shape[1]
    ins, outs = direction.shape
    blocks = row.shape[0]
    return pl.pallas_call(
        functools.partial(prepare_kernel, oct_count, "oct", codes.shape[0], cap),
        in_specs=specs("svvvvvaaa"),
        out_specs=specs("vvvvvvvvvvv"),
        out_shape=[
            pltpu.VMEM((width + 16, outs), f32),
            pltpu.VMEM((2 * cap + PART * TILE, width), bf16),
            pltpu.VMEM((width, outs), bf16),
            pltpu.VMEM((outs, width), bf16),
            pltpu.VMEM((ins, outs), bf16),
            pltpu.VMEM((8, outs), f32),
            pltpu.VMEM((1, outs), f32),
            pltpu.VMEM((ins, outs), f32),
            pltpu.VMEM((1, outs), f32),
            pltpu.VMEM(row.shape, i32),
            pltpu.VMEM((8, 128), f32),
        ],
        scratch_shapes=[
            pltpu.VMEM((blocks * window_rows(2, 64) + WIN, width), bf16),
            pltpu.VMEM((1, outs), f32),
            pltpu.SemaphoreType.DMA((3,)),
        ],
        compiler_params=params(14),
        cost_estimate=cost("prepare"),
        name="prepare",
    )(bounds, row, labels, pos, keep(points), codes, stay(direction), stay(gain[None, :]), stay(bias[None, :]))


class Rows:
    def __init__(self, cut, source, cap, place):
        self.cut, self.own_at, self.other_at = cut, source * cap, place * cap
        self.total = cut[0] + cut[1]
        self.tiles = (self.total + (TILE - 1)) // TILE

    def move(self, tile, own, other, mine, mine_at, sem, out, go):
        first = tile * TILE
        cut, total = self.cut[0], self.total

        def one(at, rows, second):
            here = mine.at[pl.ds(mine_at + at, rows), :]
            row = first + at
            there = other if second else own
            start = self.other_at + row - cut if second else self.own_at + row
            there = there.at[pl.ds(pl.multiple_of(start, ALIGN), rows), :]
            go(pltpu.make_async_copy(here, there, sem) if out else pltpu.make_async_copy(there, here, sem))

        whole = first + TILE <= cut
        last = (first >= cut) & (first + TILE <= total)
        pl.when(whole)(lambda: one(0, TILE, False))
        pl.when(last)(lambda: one(0, TILE, True))

        @pl.when((first < total) & jnp.logical_not(whole | last))
        def _():
            for at in range(0, TILE, ALIGN):
                pl.when(first + at < cut)(lambda: one(at, ALIGN, False))
                pl.when((first + at >= cut) & (first + at < total))(lambda: one(at, ALIGN, True))

    def fetch(self, tile, ct, ctx, mine, at, sem, go):
        self.move(tile, ct, ctx, mine, at, sem, False, go)

    def store(self, tile, lo, lox, mine, at, sem, go):
        self.move(tile, lo, lox, mine, at, sem, True, go)


def rows_of(bounds, group, blocks, source, cap, place, row=1):
    return Rows([filled(bounds, group + r, blocks, row) for r in range(2)], source, cap, place)


def names_at(names_ref, tile, number):
    return jnp.concatenate([names_ref[pl.ds(tile + i, 1), :] for i in range(number)], axis=1)


def go_start(copy):
    copy.start()


def go_wait(copy):
    copy.wait()


def local_kernel(oct_axis, far, blocks, span, cap, bounds, *refs):
    names_ref, ct_hbm, ctx_ref, wp_ref, wpt_ref, cb_ref, gw_in, buf_in, refs = *refs[:8], refs[8:]
    lo_hbm, lon_hbm, lof_hbm, gw_ref, buf, refs = *refs[:5], refs[5:]
    ct_v, lo_v, zero, ct_sem, lo_sem, zero_sem = refs
    source = lax.axis_index(oct_axis)
    near = rows_of(bounds, 0, blocks, source, cap, 0)
    count = (near.tiles + (PART - 1)) // PART

    def clear(go):
        def empty(array, at, t, cut):
            pl.when(t * TILE >= cut)(lambda: go(pltpu.make_async_copy(zero, array.at[pl.ds(pl.multiple_of(at + t * TILE, TILE), TILE), :], zero_sem)))

            @pl.when((t * TILE < cut) & ((t + 1) * TILE > cut))
            def _():
                for q in range(0, TILE, ALIGN):
                    @pl.when(t * TILE + q >= cut)
                    def _():
                        rows = pl.ds(pl.multiple_of(at + t * TILE + q, ALIGN), ALIGN)
                        go(pltpu.make_async_copy(zero.at[pl.ds(0, ALIGN), :], array.at[rows, :], zero_sem))

        for t in range(cap // TILE):
            empty(lo_hbm, source * cap, t, near.cut[0])
            empty(lon_hbm, 0, t, near.cut[1])
        for k in range(1, far + 1):
            for t in range(cap // TILE):
                at = (source ^ (2 * k)) * cap + t * TILE
                go(pltpu.make_async_copy(zero, lo_hbm.at[pl.ds(pl.multiple_of(at, TILE), TILE), :], zero_sem))
        for t in range(lof_hbm.shape[0] // TILE):
            go(pltpu.make_async_copy(zero, lof_hbm.at[pl.ds(t * TILE, TILE), :], zero_sem))

    def fetch(i, slot, go):
        for j in range(PART):
            near.fetch(i * PART + j, ct_hbm, ctx_ref, ct_v.at[slot], j * TILE, ct_sem.at[slot], go)

    def store(i, slot, go):
        for j in range(PART):
            near.store(i * PART + j, lo_hbm, lon_hbm, lo_v.at[slot], j * TILE, lo_sem.at[slot], go)

    @pl.when(count > 0)
    def _():
        fetch(0, 0, go_start)

    zero[...] = jnp.zeros(zero.shape, bf16)
    clear(go_start)

    def step(i, carry):
        slot = i % 2

        @pl.when(i + 1 < count)
        def _():
            fetch(i + 1, 1 - slot, go_start)

        fetch(i, slot, go_wait)

        @pl.when(i >= 2)
        def _():
            store(i - 2, slot, go_wait)

        def work(size):
            at = pl.ds(pl.multiple_of(i * PART * TILE, TILE), size * TILE)
            ct = ct_v[slot, : size * TILE, :]
            lo, gx = layer_tile(buf[at, :], names_at(names_ref, i * PART, size), ct, wp_ref, wpt_ref, cb_ref, gw_ref, span)
            lo_v[slot, : size * TILE, :] = lo
            buf[at, :] = gx

        more = near.tiles - i * PART > 2
        pl.when(more)(lambda: work(PART))
        pl.when(jnp.logical_not(more))(lambda: work(2))
        store(i, slot, go_start)
        return carry

    lax.fori_loop(0, count, step, 0)
    for back in (2, 1):
        @pl.when(count >= back)
        def _():
            store(count - back, (count - back) % 2, go_wait)

    clear(go_wait)


def local(bounds, names, cotangent, ctx, weights, gw, buf, far, blocks, span, cap):
    outs = cotangent.shape[1]
    return pl.pallas_call(
        functools.partial(local_kernel, "oct", far, blocks, span, cap),
        in_specs=specs("svavvvvvv"),
        out_specs=specs("aaavv"),
        out_shape=[pltpu.HBM(cotangent.shape, bf16), pltpu.HBM((cap, outs), bf16), pltpu.HBM((far * cap, outs), bf16),
                   pltpu.VMEM(gw.shape, f32), pltpu.VMEM(buf.shape, bf16)],
        input_output_aliases={7: 3, 8: 4},
        scratch_shapes=[
            pltpu.VMEM((2, PART * TILE, outs), bf16),
            pltpu.VMEM((2, PART * TILE, outs), bf16),
            pltpu.VMEM((TILE, outs), bf16),
            pltpu.SemaphoreType.DMA((2,)),
            pltpu.SemaphoreType.DMA((2,)),
            pltpu.SemaphoreType.DMA,
        ],
        compiler_params=params(24),
        cost_estimate=cost("local"),
        name="local",
    )(bounds, names, stay(cotangent), keep(ctx), *[keep(w) for w in weights], keep(gw), keep(buf))


def unlocal_kernel(oct_axis, cap, bounds, row_ref, gbuf, lon_ref, lo_in, part_ref, lo_hbm, moved, sem):
    blocks = row_ref.shape[0]
    join(cap, [0], oct_axis, lon_ref, lo_hbm, sem, go_start)

    def emit(b, rows):
        part_ref[b * BLOCK : (b + 1) * BLOCK, :] = rows.astype(bf16)

    cut = filled(bounds, 0, blocks)
    unsort_rows(bounds, row_ref, [0, 1], blocks,
                lambda n, first, rows: gbuf[pl.ds(pl.multiple_of(first + n * cut, 16), rows), :], moved, emit)
    join(cap, [0], oct_axis, lon_ref, lo_hbm, sem, go_wait)


def unlocal(bounds, row, gbuf, lon, lo, cap):
    blocks, width = row.shape[0], gbuf.shape[1]
    return pl.pallas_call(
        functools.partial(unlocal_kernel, "oct", cap),
        in_specs=specs("svvva"),
        out_specs=specs("va"),
        out_shape=[pltpu.VMEM((blocks * BLOCK, width), bf16), pltpu.HBM(lo.shape, bf16)],
        input_output_aliases={4: 1},
        scratch_shapes=[pltpu.VMEM((blocks * window_rows(2, 128) + WIN, width), bf16), pltpu.SemaphoreType.DMA((1,))],
        compiler_params=params(16),
        cost_estimate=cost("unlocal"),
        name="unlocal",
    )(bounds, row, keep(gbuf), keep(lon), stay(lo))


def names_kernel(kx, span, cap, labels_ref, names_ref, count_ref, back_ref):
    labels = labels_ref[...].astype(f32).astype(i32)
    blocks = labels.shape[0]
    groups = [2 * kx, 2 * kx + 1]
    pos, _, _, _, last = plan(labels, groups, span)
    names_ref[...] = stream_names(pos, labels, groups[0], span, cap)
    count_ref[...] = jnp.zeros(count_ref.shape, i32)
    count_ref[0:1, : 2 * blocks] = last[:1]
    back_ref[...] = jnp.zeros(back_ref.shape, bf16)


def make_names(labels, kx, span, cap):
    return pl.pallas_call(
        functools.partial(names_kernel, kx, span, cap),
        in_specs=specs("v"),
        out_specs=specs("vvv"),
        out_shape=[
            jax.ShapeDtypeStruct((labels.shape[0], BLOCK), i32),
            jax.ShapeDtypeStruct((8, 128), i32),
            pltpu.VMEM((2 * cap + UNIT, labels.shape[1]), bf16),
        ],
        compiler_params=params(8),
        cost_estimate=cost("names"),
        name="names",
    )(labels)


def lead_of(tiles):
    return jnp.maximum(tiles, LEAD)


def take_back(place, number, theirs, blocks, x_ref, at, back):
    for i in range(number):
        n = place + i - lead_of(tiles_of(theirs, 0, blocks, 0))

        @pl.when((n >= 0) & (n < (back.shape[0] - UNIT) // TILE))
        def _():
            back[pl.ds(pl.multiple_of(n * TILE, TILE), TILE), :] = x_ref[at + i * TILE : at + (i + 1) * TILE, :]


def far_kernel(message, before, after_it, emits, kx, oct_axis, blocks, span, cap, mine, theirs, *refs):
    names_ref, x_ref, ct_hbm, ctx_ref, wp_ref, wpt_ref, cb_ref, queue_in, lo_in, lof_in, gw_in, back_in, refs = *refs[:12], refs[12:]
    if before:
        ct_v, lo_old, refs = *refs[:2], refs[2:]
    queue, lo_hbm, lof_hbm, gw_ref, back, refs = *refs[:5], refs[5:]
    payloads, refs = refs[: len(emits)], refs[len(emits) :]
    if after_it:
        ct_new, refs = refs[0], refs[1:]
    lo_v, refs = refs[0], refs[1:]
    if not before:
        ct_v, refs = refs[0], refs[1:]
    ct_sem, new_sem, lo_sem = refs
    first, number = message
    source = lax.axis_index(oct_axis) ^ (2 * kx)
    rows = rows_of(theirs, 0, blocks, source, cap, kx - 1, 0)
    lead = lead_of(tiles_of(mine, 2 * kx, blocks))

    def fetch(u, go):
        if not before:
            rows.fetch(first + u, ct_hbm, ctx_ref, ct_v, u * TILE, ct_sem.at[u], go)

    def ahead(go):
        if before:
            for u in range(before[1]):
                rows.store(before[0] + u, lo_hbm, lof_hbm, lo_old, u * TILE, lo_sem, go)
        if after_it:
            for u in range(after_it[1]):
                rows.fetch(after_it[0] + u, ct_hbm, ctx_ref, ct_new, u * TILE, new_sem, go)

    for u in range(number):
        fetch(u, go_start)
    ahead(go_start)
    take_back(first, number, theirs, blocks, x_ref, 0, back)
    for u in range(number):
        fetch(u, go_wait)

    def work(size):
        at = slice(0, size * TILE)
        lo, gx = layer_tile(x_ref[at, :], names_at(names_ref, first, size), ct_v[at, :], wp_ref, wpt_ref, cb_ref, gw_ref, span)
        lo_v[at, :] = lo
        queue[pl.ds(pl.multiple_of((lead + first) * TILE, TILE), size * TILE), :] = gx

    if number > 2:
        pl.when(first + 2 < rows.tiles)(lambda: work(number))
        pl.when((first < rows.tiles) & (first + 2 >= rows.tiles))(lambda: work(2))
    else:
        pl.when(first < rows.tiles)(lambda: work(number))

    for payload, (place, count) in zip(payloads, emits):
        payload[...] = queue[place * TILE : (place + count) * TILE, :]
    ahead(go_wait)


def far_step(messages, m, points_in, kx, mine, theirs, names, x, cotangent, ctx, weights, state, ahead, blocks, span, cap):
    wp, wpt, cb = weights
    queue, lo, lof, gw, back = state
    width, outs = wp.shape
    last = points_in[-1] == m
    message, before, after_it = messages[m], (messages[m - 1] if m > 0 else None), (None if last else messages[m + 1])
    emits = messages[m + 2 :] if last else [messages[m + 2]]
    own = (message[1] * TILE, outs)
    shapes = [pltpu.VMEM(queue.shape, bf16), pltpu.HBM(lo.shape, bf16), pltpu.HBM(lof.shape, bf16), pltpu.VMEM(gw.shape, f32),
              pltpu.VMEM(back.shape, bf16)] + [pltpu.VMEM((count * TILE, width), bf16) for _, count in emits]
    if after_it:
        shapes.append(pltpu.VMEM((after_it[1] * TILE, outs), bf16))
    shapes.append(pltpu.VMEM(own, bf16))
    args = [mine, theirs, names, keep(x), stay(cotangent), keep(ctx), keep(wp), keep(wpt), keep(cb), keep(queue), stay(lo),
            stay(lof), keep(gw), keep(back)] + [keep(a) for a in ahead]
    out = pl.pallas_call(
        functools.partial(far_kernel, message, before, after_it, emits, kx, "oct", blocks, span, cap),
        in_specs=specs("ssvvavvvvvaavv" + "v" * len(ahead)),
        out_specs=specs("vaavv" + "v" * (len(shapes) - 5)),
        out_shape=shapes,
        input_output_aliases={9 + i: i for i in range(5)},
        scratch_shapes=([] if before else [pltpu.VMEM(own, bf16)])
        + [pltpu.SemaphoreType.DMA((message[1],)), pltpu.SemaphoreType.DMA, pltpu.SemaphoreType.DMA],
        compiler_params=params(20),
        cost_estimate=cost("last" if last else "far"),
        name="far",
    )(*args)
    return tuple(out[:5]), out[5 : 5 + len(emits)], tuple(out[5 + len(emits) :])


def unpack_kernel(far, blocks, lasts, bounds, *refs):
    theirs, rows_far, refs = refs[:far], refs[far : 2 * far], refs[2 * far :]
    parts, refs = refs[: far * len(lasts)], refs[far * len(lasts) :]
    part_ref, refs = refs[0], refs[1 + far :]
    out_hbm, backs, (moved, out_ref, sem) = refs[0], refs[1 : 1 + far], refs[-3:]
    group = max(1, blocks // 4)

    def send(n):
        rows = pl.ds(n * group * BLOCK, group * BLOCK)
        return pltpu.make_async_copy(out_ref.at[rows, :], out_hbm.at[rows, :], sem.at[n])

    for k in range(far):
        for j, (first, number) in enumerate(lasts):
            take_back(first, number, theirs[k], blocks, parts[k * len(lasts) + j], 0, backs[k])
        cut = filled(bounds, 2 + 2 * k, blocks)

        def pick(n, first, count):
            return backs[k][pl.ds(pl.multiple_of(first + n * cut, 16), count), :]

        def emit(b, value):
            at = slice(b * BLOCK, (b + 1) * BLOCK)
            before = part_ref if k == 0 else out_ref
            out_ref[at, :] = (value + before[at, :].astype(f32)).astype(bf16)
            if k == far - 1 and (b + 1) % group == 0:
                send(b // group).start()

        unsort_rows(bounds, rows_far[k], [2 + 2 * k, 3 + 2 * k], blocks, pick, moved, emit)
    for n in range(blocks // group):
        send(n).wait()


def unpack(bounds, theirs, rows_far, lasts, parts, part, backs):
    points, width = part.shape
    blocks = points // BLOCK
    far = len(theirs)
    extra = far * len(lasts)
    return pl.pallas_call(
        functools.partial(unpack_kernel, far, blocks, lasts),
        in_specs=specs("s" + "s" * far + "v" * (2 * far + extra + 1)),
        out_specs=specs("a" + "v" * far),
        out_shape=[pltpu.HBM(part.shape, bf16)] + [pltpu.VMEM(b.shape, bf16) for b in backs],
        input_output_aliases={2 * far + extra + 2 + k: 1 + k for k in range(far)},
        scratch_shapes=[
            pltpu.VMEM((blocks * window_rows(2, 128) + WIN, width), bf16),
            pltpu.VMEM(part.shape, bf16),
            pltpu.SemaphoreType.DMA((4,)),
        ],
        compiler_params=params(20),
        cost_estimate=cost("unpack"),
        name="unpack",
    )(bounds, *theirs, *rows_far, *[keep(x) for x in parts], keep(part), *[keep(b) for b in backs])[0]


def join(cap, kxs, oct_axis, lox_ref, lo_hbm, sem, go):
    other = lax.axis_index(oct_axis) ^ 1
    for n, k in enumerate(kxs):
        at = pl.ds(pl.multiple_of((other ^ (2 * k)) * cap, cap), cap)
        go(pltpu.make_async_copy(lox_ref.at[pl.ds(n * cap, cap), :], lo_hbm.at[at, :], sem.at[n]))


def merge_kernel(cap, kxs, oct_axis, lox_ref, lo_in, lo_hbm, sem):
    for go in (go_start, go_wait):
        join(cap, kxs, oct_axis, lox_ref, lo_hbm, sem, go)


def merge(lox, lo, cap, kxs):
    return pl.pallas_call(
        functools.partial(merge_kernel, cap, tuple(kxs), "oct"),
        in_specs=specs("va"),
        out_specs=specs("a")[0],
        out_shape=pltpu.HBM(lo.shape, lo.dtype),
        input_output_aliases={1: 0},
        scratch_shapes=[pltpu.SemaphoreType.DMA((len(kxs),))],
        compiler_params=params(4),
        cost_estimate=cost("merge"),
        name="merge",
    )(keep(lox), stay(lo))


def column_block(axes, n):
    a, b = (lax.axis_index(axis) % 2 for axis in axes)
    return (a ^ (n % 2)) * 2 + (b ^ (n // 2))


def collect_kernel(axes, shape_axis, oct_axis, shapes, span, extra, blocks, cap, message, usual, steps, *refs):
    mine, refs = refs[0], refs[1:]
    theirs, olds, refs = refs[:extra], refs[extra : 2 * extra], refs[2 * extra :]
    gw_ref, info_ref, codes_ref, lo_in, lof_in, outs, lo_hbm, lof_hbm, full, sem = *refs[:5], refs[5:9], *refs[9:]
    source = lax.axis_index(oct_axis)

    def store(go):
        for k in range(extra):
            rows = rows_of(theirs[k], 0, blocks, source ^ (2 * k + 2), cap, k, 0)
            for u in range(message[1]):
                rows.store(message[0] + u, lo_hbm, lof_hbm, olds[k], u * TILE, sem, go)

    store(go_start)
    width = gw_ref.shape[0] - 16
    cols = gw_ref.shape[1]
    code_width = codes_ref.shape[1]
    base = lax.axis_index(shape_axis) * span
    full[:width, :] = gw_ref[:width, :]
    ps = jnp.zeros((shapes, cols), f32)
    for s in range(span):
        ps = ps + jnp.where(iota((shapes, 1), 0) == base + s, gw_ref[width + s : width + s + 1, :], 0.0)
    full[width : width + shapes, :] = ps
    flag = jnp.int32(0)
    for k in range(extra):
        ours = tiles_of(mine, 2 + 2 * k, blocks)
        other = tiles_of(theirs[k], 0, blocks, 0)
        most = jnp.maximum(jnp.maximum(ours, LEAD) + other, jnp.maximum(other, LEAD) + ours)
        flag = flag | ((jnp.maximum(ours, other) > usual) | (most > steps)).astype(i32)
    flag = flag.astype(f32)
    lane = iota((1, cols - code_width), 1)
    info = jnp.zeros((shapes, cols), f32)
    for s in range(span):
        number = info_ref[s : s + 1, :1]
        high = jnp.floor(number / 1024.0)
        mid = jnp.floor((number - 1024.0 * high) / 32.0)
        low = number - 1024.0 * high - 32.0 * mid
        digits = jnp.where(lane < 64, low, jnp.where(lane < 128, mid, jnp.where(lane < 192, high, flag)))
        code = jnp.where(lax.axis_index(oct_axis) == 0, codes_ref[s : s + 1, :].astype(f32), 0.0)
        info = info + jnp.where(iota((shapes, 1), 0) == base + s, jnp.concatenate([code, digits], axis=1), 0.0)
    full[width + shapes : width + 2 * shapes, :] = info
    for n in range(4):
        at = pl.ds(pl.multiple_of(column_block(axes, n) * 128, 128), 128)
        outs[n][...] = full[:, at].astype(bf16)
    store(go_wait)


def halves(x):
    high = x.astype(bf16)
    return high, (x - high.astype(f32)).astype(bf16)


def finish_kernel(axes, shape_axis, hid, span, categories, momentum, *refs):
    parts, refs = refs[:4], refs[4:]
    direction_ref, gain_ref, norm_ref, w_ref, mean_ref, var_ref, refs = *refs[:6], refs[6:]
    dg_ref, gg_ref, bg_ref, cg_ref, mean_out, var_out, left_ref, full = refs
    for n in range(4):
        at = pl.ds(pl.multiple_of(column_block(axes, n) * 128, 128), 128)
        full[:, at] = parts[n][...].astype(f32)
    ins, cols = direction_ref.shape
    cats, code_width = mean_ref.shape
    shapes = (full.shape[0] - (ins - code_width)) // 2
    width = ins - code_width
    ps = full[width : width + shapes, :]
    info = full[width + shapes : width + 2 * shapes, :]
    codes = info[:, :code_width]
    at = code_width
    number = info[:, at : at + 1] + 32.0 * info[:, at + 64 : at + 65] + 1024.0 * info[:, at + 128 : at + 129]
    for c in range(cats):
        chosen = jnp.zeros((shapes, 1), f32)
        for s in range(shapes):
            chosen = jnp.where((iota((shapes, 1), 0) == s) & (categories[s] == c), 1.0, chosen)
        weight = chosen * number
        count = jnp.sum(weight, axis=0, keepdims=True)
        mean = jnp.sum(weight * codes, axis=0, keepdims=True) / count
        var = jnp.sum(weight * codes * codes, axis=0, keepdims=True) / count - mean * mean
        rate = momentum[c]
        mean_out[c : c + 1, :] = (1.0 - rate) * mean_ref[c : c + 1, :] + rate * mean
        var_out[c : c + 1, :] = (1.0 - rate) * var_ref[c : c + 1, :] + rate * var

    gw = full[:width, :]
    codes_all = jnp.concatenate(
        [jnp.zeros((shapes, hid), f32), codes, jnp.zeros((shapes, ins - hid - code_width), f32)], axis=1
    )
    high, low = halves(ps)
    wg = lax.dot_general(jnp.concatenate([codes_all, codes_all], axis=0).astype(bf16), jnp.concatenate([high, low], axis=0),
                         (((0,), (0,)), ((), ())), preferred_element_type=f32)
    head = jnp.where(iota((width, 1), 0) < hid, gw, wg[:width])
    tail = jnp.where(iota((8, 1), 0) + (width - 8) >= hid, gw[width - 8 :], wg[ins - 8 :])
    wg = jnp.concatenate([head, wg[width : ins - 8], tail], axis=0)
    direction = direction_ref[...]
    norms = norm_ref[...]
    dots = jnp.sum(wg * direction, axis=0, keepdims=True)
    gg_ref[...] = dots / norms
    dg_ref[...] = (gain_ref[...] / norms) * (wg - direction * (dots / (norms * norms)))
    bg_ref[...] = jnp.sum(ps, axis=0, keepdims=True)
    base = lax.axis_index(shape_axis) * span
    own = jnp.zeros((8, cols), f32)
    for s in range(span):
        row = jnp.sum(jnp.where(iota((shapes, 1), 0) == base + s, ps, 0.0), axis=0, keepdims=True)
        own = own + jnp.where(iota((8, 1), 0) == s, row, 0.0)
    both = lax.dot_general(jnp.concatenate(halves(own), axis=0), w_ref[...], (((1,), (1,)), ((), ())), preferred_element_type=f32)
    cg_ref[...] = (both[:8] + both[8:])[:span, hid : hid + code_width]
    left_ref[0] = jnp.max(info[:, at + 192 :])


def finish(axes, span, categories, momentum, parts, direction, gain, norms, weight, prev_mean, prev_var):
    ins, outs = direction.shape
    return pl.pallas_call(
        functools.partial(finish_kernel, axes, "shape", HID, span),
        in_specs=specs("ss" + "v" * 10),
        out_specs=specs("v" * 6 + "s"),
        out_shape=[
            jax.ShapeDtypeStruct((ins, outs), f32),
            jax.ShapeDtypeStruct((1, outs), f32),
            jax.ShapeDtypeStruct((1, outs), f32),
            jax.ShapeDtypeStruct((span, prev_mean.shape[1]), f32),
            jax.ShapeDtypeStruct(prev_mean.shape, f32),
            jax.ShapeDtypeStruct(prev_mean.shape, f32),
            jax.ShapeDtypeStruct((1,), f32),
        ],
        scratch_shapes=[pltpu.VMEM((parts[0].shape[0], outs), f32)],
        compiler_params=params(12),
        cost_estimate=cost("finish"),
        name="finish",
    )(categories, momentum, *[keep(p) for p in parts], keep(direction), keep(gain), keep(norms), keep(weight), prev_mean, prev_var)


def swap(v, axis, k):
    n = lax.axis_size(axis)
    return lax.ppermute(v, axis, [(i, i ^ k) for i in range(n)])


def swap_both(v, k):
    n, m = lax.axis_size("shape"), lax.axis_size("oct")
    return lax.ppermute(v, ("shape", "oct"), [(i, i ^ k) for i in range(n * m)])


def bits(axis, first):
    n = lax.axis_size(axis)
    return [(axis, 1 << j) for j in range(first, n.bit_length() - 1)]


def after(x, *others):
    return lax.optimization_barrier((x, *others))[0]


def quarters_to(parts):
    m = lax.axis_size("oct")
    return [swap(parts[0], "oct", 1), swap(parts[1], "shape", 1), swap_both(parts[2], m + 1)]


def total_quarter(parts, before):
    got = quarters_to(parts[1:])
    v = parts[0].astype(f32) + got[0].astype(f32) + got[1].astype(f32) + after(got[2], *before[0]).astype(f32)
    v = v.astype(bf16)
    yield v
    for n, (axis, k) in enumerate(bits("shape", 1) + bits("oct", 1)):
        v = (v.astype(f32) + after(swap(v, axis, k), *before[n + 1]).astype(f32)).astype(bf16)
        yield v


AXES = ("oct", "shape")


def collect(mine, theirs, olds, gw, info, codes, lo, lof, shapes, blocks, cap, message, usual, steps):
    span = codes.shape[0]
    far = len(theirs)
    rows = gw.shape[0] - 16 + 2 * shapes
    out = pl.pallas_call(
        functools.partial(collect_kernel, AXES, "shape", "oct", shapes, span, far, blocks, cap, message, usual, steps),
        in_specs=specs("s" + "s" * far + "v" * far + "vvvaa"),
        out_specs=specs("vvvvaa"),
        out_shape=[pltpu.VMEM((rows, 128), bf16)] * 4 + [pltpu.HBM(lo.shape, bf16), pltpu.HBM(lof.shape, bf16)],
        input_output_aliases={2 * far + 4: 4, 2 * far + 5: 5},
        scratch_shapes=[pltpu.VMEM((rows, gw.shape[1]), f32), pltpu.SemaphoreType.DMA],
        compiler_params=params(8),
        cost_estimate=cost("collect"),
        name="collect",
    )(mine, *theirs, *[keep(o) for o in olds], keep(gw), info, codes, stay(lo), stay(lof))
    return out[:4], out[4], out[5]


def run(usual, steps, point_inputs, shape_ids, octants, categories, codes, direction, gain, bias, cotangent, prev_mean, prev_var, momentum):
    points, width = point_inputs.shape
    oct_count, shape_dev = lax.axis_size("oct"), lax.axis_size("shape")
    cap = 2 * points // oct_count
    span, code_width = codes.shape
    shapes = shape_dev * span
    blocks = points // BLOCK
    far = list(range(1, oct_count // 2))
    messages = plan_messages(usual, steps)
    points_in = [m for m, (first, _) in enumerate(messages) if first < usual]

    (ct_near, ct_far, x_near), heads, queues, rows_far, (row_near, mine, labels, pos) = pack(
        octants, shape_ids, point_inputs, cotangent, messages, oct_count, span, cap)
    ctn, ctf = swap(ct_near, "oct", 1), swap(ct_far, "oct", 1)
    got = {(k, m): swap(heads[2 * (k - 1) + m], "oct", 2 * k) for k in far for m in range(2)}
    gw, buf, wp, wpt, weight, cb, norms, direction_v, gain_v, near_names, info = prepare(
        mine, row_near, labels, pos, x_near, direction, gain, bias, codes, oct_count, cap)
    weights = (wp, wpt, cb)
    lo, lon, lof, gw, buf = local(mine, near_names, cotangent, ctn, weights, gw, buf, len(far), blocks, span, cap)

    queue = {k: queues[k - 1] for k in far}
    named, theirs, back, ahead = {}, {}, {}, {}
    for k in far:
        named[k], theirs[k], back[k] = make_names(after(got[k, 0], gw)[messages[0][1] * TILE :], k, span, cap)
        ahead[k] = ()
    for m in points_in:
        for k in far:
            (queue[k], lo, lof, gw, back[k]), payloads, ahead[k] = far_step(
                messages, m, points_in, k, mine, theirs[k], named[k], got[k, m], cotangent, ctf, weights,
                (queue[k], lo, lof, gw, back[k]), ahead[k], blocks, span, cap)
            for j, payload in enumerate(payloads):
                got[k, m + 2 + j] = swap(payload, "oct", 2 * k)
        if m == min(1, points_in[-1] - 1):
            part, lo = unlocal(mine, row_near, after(buf, gw), swap(lon, "oct", 1), lo, cap)
            gw = after(gw, part)
    their = [theirs[k] for k in far]
    lasts = list(range(len(points_in), len(messages)))
    order = ((), (0,), (), (1,)) if len(lasts) == 2 else ()
    before = [[got[k, lasts[i]] for k in far for i in ii] for ii in order] + [[] for _ in range(20)]
    parts, lo, lof = collect(mine, their, [ahead[k][-1] for k in far], gw, info, codes, lo, lof, shapes, blocks, cap,
                             messages[points_in[-1]], usual, steps)
    lox = swap(lof, "oct", 1)
    input_grad = unpack(mine, their, rows_far, [messages[m] for m in lasts], [got[k, m] for k in far for m in lasts], part,
                        [back[k] for k in far])
    for v in total_quarter(parts, before):
        pass
    parts = [v] + quarters_to([v] * 3)
    lo = merge(lox, lo, cap, far)
    direction_grad, gain_grad, bias_grad, code_grad, running_mean, running_var, left = finish(
        AXES, span, categories, momentum, [after(parts[0], lo, input_grad)] + parts[1:], direction_v, gain_v, norms, weight, prev_mean, prev_var)
    outputs = (
        lo,
        input_grad,
        code_grad,
        direction_grad,
        gain_grad[0],
        bias_grad[0],
        running_mean,
        running_var,
    )
    return outputs, left[0]


def body(*args):
    points, oct_count = args[0].shape[0], lax.axis_size("oct")
    most = 2 * (2 * points // oct_count) // TILE
    all_steps = max(most, LEAD) + most
    usual, steps = min(USUAL, most), min(STEPS, all_steps)
    outputs, left = run(usual, steps, *args)
    if (usual, steps) == (most, all_steps):
        return outputs

    def more(carry):
        return jnp.float32(0), run(most, all_steps, *args)[0]

    return lax.while_loop(lambda carry: carry[0] > 0, more, (left, outputs))[1]


def solution(mesh):
    both = P(("shape", "oct"), None)
    in_specs = (both, P(("shape", "oct")), both, P(), P("shape", None), P(), P(), P(), both, P(), P(), P())
    out_specs = (both, both, P("shape", None), P(), P(), P(), P(), P())
    return jax.shard_map(body, mesh=mesh, in_specs=in_specs, out_specs=out_specs, check_vma=False)
```
